32 devices in a mesh: dp: 8 (over z, x), mp: 4 (over y, core).
Axes of the slice: x: 2, y: 2, z: 4, core: 2. Of those that a mesh axis runs over, the one named last changes fastest.
Arguments:
- enc_in: bfloat16 [8, 1344, 768], P('dp', 'mp'), may hold values from -6 to 6
- dec_in: bfloat16 [8, 448, 768], P('dp', 'mp'), may hold values from -6 to 6
- dec_len: int32 [8], P('dp'), may hold values from 5 to 448, as said below
- norm_gain: bfloat16 [5, 768], replicated, may hold values from 0.5 to 1.5
- norm_shift: bfloat16 [5, 768], replicated, may hold values from -1.8 to 1.8
- qkv: bfloat16 [3, 3, 768, 768], P(None, None, None, 'mp')
- qv_bias: bfloat16 [3, 2, 768], P(None, None, 'mp'), may hold values from -1.8 to 1.8
- proj: bfloat16 [3, 768, 768], P(None, 'mp')
- out_bias: bfloat16 [5, 768], replicated, may hold values from -1.8 to 1.8
- fc1: bfloat16 [2, 768, 3072], P(None, None, 'mp')
- fc1_bias: bfloat16 [2, 3072], P(None, 'mp'), may hold values from -1.8 to 1.8
- fc2: bfloat16 [2, 3072, 768], P(None, 'mp')
- enc_cot: bfloat16 [8, 1344, 768], P('dp', 'mp'), may hold values from -6 to 6
- dec_cot: bfloat16 [8, 448, 768], P('dp', 'mp'), may hold values from -6 to 6
Outputs:
- enc_out: bfloat16 [8, 1344, 768], P('dp', 'mp')
- dec_out: bfloat16 [8, 448, 768], P('dp', 'mp')
- enc_in_grad: float32 [8, 1344, 768], P('dp', 'mp')
- dec_in_grad: float32 [8, 448, 768], P('dp', 'mp')
- norm_gain_grad: float32 [5, 768], replicated
- norm_shift_grad: float32 [5, 768], replicated
- qkv_grad: float32 [3, 3, 768, 768], P(None, None, None, 'mp')
- qv_bias_grad: float32 [3, 2, 768], P(None, None, 'mp')
- proj_grad: float32 [3, 768, 768], P(None, 'mp')
- out_bias_grad: float32 [5, 768], replicated
- fc1_grad: float32 [2, 768, 3072], P(None, None, 'mp')
- fc1_bias_grad: float32 [2, 3072], P(None, 'mp')
- fc2_grad: float32 [2, 3072, 768], P(None, 'mp')
The draws below stay inside these ranges and needn't reach their ends.
Inputs may be any that keep to these rules, and one draw needn't show every extreme that they name: `dec_len`: among the 1 clips of each index of dp, one, which one drawn from the seed, has tokens on every index of mp; on the first index of dp that clip has exactly 448 tokens.
All inputs are finite; a program needn't handle non-finite values.
Results may differ from the reference program's by a relative error of at most 0.017.
Values may be sent and summed in bfloat16 or wider, within the bound.
A program may use at most 192 MiB of HBM per device.

```python
import jax
import jax.numpy as jnp
from jax import lax

D = 768
HEADS = 12
HEAD = 64
FF = 3072
FRAMES = 1344
DEC = 448
CLIPS_DEV = 1
CLIPS = 8
N_MP = 4


def draw_dec_len(key, part):
    key = jax.random.fold_in(key, 11)
    first_key, second_key, third_key = jax.random.split(key, 3)
    groups = CLIPS // CLIPS_DEV
    lengths = jax.random.randint(first_key, (groups, CLIPS_DEV), 5, DEC + 1)
    picks = jax.random.randint(second_key, (groups, 1), 0, CLIPS_DEV)
    reaching = jax.random.randint(third_key, (groups, 1), DEC - DEC // N_MP + 1, DEC + 1)
    group_index = lax.broadcasted_iota(jnp.int32, (groups, 1), 0)
    reaching = jnp.where(group_index == 0, DEC, reaching)
    slots = lax.broadcasted_iota(jnp.int32, lengths.shape, 1)
    return jnp.where(slots == picks, reaching, lengths).reshape(CLIPS).astype(jnp.int32)


def clipped_normal(key, shape, scale, bound):
    values = jax.random.normal(key, shape, jnp.float32)
    return jnp.clip(values, -bound, bound) * scale


def draw_norm_gain(key, part):
    key = jax.random.fold_in(key, 21)
    return (1.0 + clipped_normal(key, (5, D), 0.1, 5.0)).astype(jnp.bfloat16)


def draw_norm_shift(key, part):
    key = jax.random.fold_in(key, 22)
    return clipped_normal(key, (5, D), 0.3, 6.0).astype(jnp.bfloat16)


def draw_qkv(key, part):
    key = jax.random.fold_in(key, 23)
    return clipped_normal(key, (3, 3, D, D), D ** (-0.5), 6.0).astype(jnp.bfloat16)


def draw_qv_bias(key, part):
    key = jax.random.fold_in(key, 24)
    return clipped_normal(key, (3, 2, D), 0.3, 6.0).astype(jnp.bfloat16)


def draw_proj(key, part):
    key = jax.random.fold_in(key, 25)
    return clipped_normal(key, (3, D, D), (D // 8) ** (-0.5), 6.0).astype(jnp.bfloat16)


def draw_out_bias(key, part):
    key = jax.random.fold_in(key, 26)
    return clipped_normal(key, (5, D), 0.3, 6.0).astype(jnp.bfloat16)


def draw_fc1(key, part):
    key = jax.random.fold_in(key, 27)
    return clipped_normal(key, (2, D, FF), D ** (-0.5), 6.0).astype(jnp.bfloat16)


def draw_fc1_bias(key, part):
    key = jax.random.fold_in(key, 28)
    return clipped_normal(key, (2, FF), 0.3, 6.0).astype(jnp.bfloat16)


def draw_fc2(key, part):
    key = jax.random.fold_in(key, 29)
    return clipped_normal(key, (2, FF, D), FF ** (-0.5), 6.0).astype(jnp.bfloat16)


def shard_levels(stream_key, shape, pieces, least, largest):
    def one(position, shards_of):
        draws = jax.random.uniform(jax.random.fold_in(jax.random.fold_in(stream_key, 6), position), (shards_of,), jnp.float32, least / len(pieces), largest / len(pieces))
        return jnp.repeat(jnp.exp(draws), shape[position] // shards_of).reshape((-1,) + (1,) * (len(shape) - position - 1))

    gain = one(*pieces[0])
    for cut in pieces[1:]:
        gain = gain * one(*cut)
    return gain


def scatter_about(stream_key, shape, deviation, reach, shards=(), held_as=jnp.bfloat16):
    array = deviation * jax.random.normal(stream_key, shape, jnp.float32)
    if shards:
        array = array * shard_levels(stream_key, shape, shards, -0.22, 0.18)
    return jnp.clip(array, -reach, reach).astype(held_as)


def setup_inputs(seed: int = 0) -> dict:
    seeds = jax.random.split(jax.random.key(seed), 15)
    return {
        "enc_in": scatter_about(seeds[0], (CLIPS, FRAMES, D), 1.0, 6.0, ((0, 8), (1, 4))),
        "dec_in": scatter_about(seeds[1], (CLIPS, DEC, D), 1.0, 6.0, ((0, 8), (1, 4))),
        "dec_len": draw_dec_len(jax.random.fold_in(seeds[14], 71), 0),
        "norm_gain": draw_norm_gain(jax.random.fold_in(seeds[14], 71), 0),
        "norm_shift": draw_norm_shift(jax.random.fold_in(seeds[14], 71), 0),
        "qkv": draw_qkv(jax.random.fold_in(seeds[14], 71), 0),
        "qv_bias": draw_qv_bias(jax.random.fold_in(seeds[14], 71), 0),
        "proj": draw_proj(jax.random.fold_in(seeds[14], 71), 0),
        "out_bias": draw_out_bias(jax.random.fold_in(seeds[14], 71), 0),
        "fc1": draw_fc1(jax.random.fold_in(seeds[14], 71), 0),
        "fc1_bias": draw_fc1_bias(jax.random.fold_in(seeds[14], 71), 0),
        "fc2": draw_fc2(jax.random.fold_in(seeds[14], 71), 0),
        "enc_cot": scatter_about(seeds[12], (CLIPS, FRAMES, D), 1.0, 6.0, ((0, 8), (1, 4))),
        "dec_cot": scatter_about(seeds[13], (CLIPS, DEC, D), 1.0, 6.0, ((0, 8), (1, 4))),
    }


@jax.custom_vjp
def low(v):
    return lax.optimization_barrier(v.astype(jnp.bfloat16)).astype(jnp.float32)

@jax.custom_vjp
def low_back(v):
    return v

def low_keep(v):
    return (low(v), None)

def low_pass(kept, grad):
    return (grad,)

def back_keep(v):
    return (v, None)

def back_low(kept, grad):
    return (low(grad),)
low.defvjp(low_keep, low_pass)
low_back.defvjp(back_keep, back_low)
highest = lax.Precision.HIGHEST
epsilon = 1e-05
masked_score = -1e+30

def rounded_both(value):
    return low(low_back(value))

def normalize(rows_in, gain_row, shift_row):
    average = lax.optimization_barrier(jnp.mean(rows_in, axis=-1, keepdims=True))
    centred = rows_in - average
    spread = lax.optimization_barrier(jnp.mean(centred * centred, axis=-1, keepdims=True))
    return centred * lax.rsqrt(spread + epsilon) * gain_row + shift_row

def matmul(operand, weight):
    return jnp.dot(operand, weight, precision=highest, preferred_element_type=jnp.float32)

def attend(queries, key_rows, values, causal):
    row_count = queries.shape[0]
    split_query = queries.reshape(row_count, HEADS, HEAD)
    split_keys = key_rows.reshape(key_rows.shape[0], HEADS, HEAD)
    split_values = values.reshape(values.shape[0], HEADS, HEAD)
    scores = jnp.einsum('rhe,she->hrs', split_query, split_keys, precision=highest) * HEAD ** (-0.5)
    if causal:
        row_index = lax.broadcasted_iota(jnp.int32, scores.shape, 1)
        col_index = lax.broadcasted_iota(jnp.int32, scores.shape, 2)
        scores = jnp.where(col_index <= row_index, scores, masked_score)
    scores = low_back(scores)
    weights = low(jax.nn.softmax(scores, axis=-1))
    mixed_out = jnp.einsum('hrs,she->rhe', weights, split_values, precision=highest)
    return rounded_both(mixed_out.reshape(row_count, HEADS * HEAD))

def encoder(frames, params):
    norm_gain, norm_shift, qkv, qv_bias, proj, out_bias, fc1, fc1_bias, fc2 = params
    normed = low(normalize(frames, norm_gain[0], norm_shift[0]))
    queries = rounded_both(matmul(normed, qkv[0, 0]) + qv_bias[0, 0])
    key_rows = rounded_both(matmul(normed, qkv[0, 1]))
    values = rounded_both(matmul(normed, qkv[0, 2]) + qv_bias[0, 1])
    middle = frames + low_back(matmul(attend(queries, key_rows, values, False), proj[0]) + out_bias[0])
    normed = low(normalize(middle, norm_gain[1], norm_shift[1]))
    hidden = low_back(matmul(normed, fc1[0]) + fc1_bias[0])
    activated = low(jax.nn.gelu(hidden, approximate=False))
    return middle + low_back(matmul(activated, fc2[0]) + out_bias[1])

def decoder(tokens, memory, valid_rows, params):
    norm_gain, norm_shift, qkv, qv_bias, proj, out_bias, fc1, fc1_bias, fc2 = params
    normed = low(normalize(tokens, norm_gain[2], norm_shift[2]))
    queries = rounded_both(matmul(normed, qkv[1, 0]) + qv_bias[1, 0])
    key_rows = rounded_both(matmul(normed, qkv[1, 1]))
    values = rounded_both(matmul(normed, qkv[1, 2]) + qv_bias[1, 1])
    after_self = tokens + low_back(matmul(attend(queries, key_rows, values, True), proj[1]) + out_bias[2])
    normed = low(normalize(after_self, norm_gain[3], norm_shift[3]))
    cross_queries = rounded_both(matmul(normed, qkv[2, 0]) + qv_bias[2, 0])
    cross_keys = rounded_both(matmul(memory, qkv[2, 1]))
    cross_values = rounded_both(matmul(memory, qkv[2, 2]) + qv_bias[2, 1])
    second = after_self + low_back(matmul(attend(cross_queries, cross_keys, cross_values, False), proj[2]) + out_bias[3])
    normed = low(normalize(second, norm_gain[4], norm_shift[4]))
    hidden = low_back(matmul(normed, fc1[1]) + fc1_bias[1])
    activated = low(jax.nn.gelu(hidden, approximate=False))
    after_mlp = second + low_back(matmul(activated, fc2[1]) + out_bias[4])
    return after_mlp * valid_rows

def reference(enc_in, dec_in, dec_len, norm_gain, norm_shift, qkv, qv_bias, proj, out_bias, fc1, fc1_bias, fc2, enc_cot, dec_cot):
    params = tuple((weight.astype(jnp.float32) for weight in (norm_gain, norm_shift, qkv, qv_bias, proj, out_bias, fc1, fc1_bias, fc2)))
    totals = tuple((jnp.zeros(weight.shape, jnp.float32) for weight in params))

    def clip_step(carried, clip_data):
        frames, tokens, length, frame_cot, token_cot = clip_data
        valid_rows = (lax.iota(jnp.int32, DEC) < length).astype(jnp.float32)[:, None]

        def forward(weights, frame_rows, token_rows):
            encoded = encoder(frame_rows, weights)
            return (encoded, decoder(token_rows, low(encoded), valid_rows, weights))
        outputs, pullback = jax.vjp(forward, params, frames.astype(jnp.float32), tokens.astype(jnp.float32))
        gradients, frame_grad, token_grad = pullback((frame_cot.astype(jnp.float32), token_cot.astype(jnp.float32)))
        carried = jax.tree.map(jnp.add, carried, gradients)
        return (carried, (outputs[0].astype(jnp.bfloat16), outputs[1].astype(jnp.bfloat16), frame_grad, token_grad))
    totals, (enc_out, dec_out, enc_grad, dec_grad) = lax.scan(clip_step, totals, (enc_in, dec_in, dec_len, enc_cot, dec_cot))
    return (enc_out, dec_out, enc_grad, dec_grad, totals[0], totals[1], totals[2], totals[3], totals[4], totals[5], totals[6], totals[7], totals[8])
```

```python
import jax
import jax.numpy as jnp
from jax import lax
from jax.sharding import PartitionSpec as P

HEAD = 64


epsilon = 1e-05
masked_score = -1e30


def normalize(rows_in, gain_row, shift_row):
    average = jnp.mean(rows_in, axis=-1, keepdims=True)
    centred = rows_in - average
    spread = jnp.mean(centred * centred, axis=-1, keepdims=True)
    return centred * lax.rsqrt(spread + epsilon) * gain_row + shift_row


def norm_back(rows_in, gain_row, shift_row, gradient):
    unused, pullback = jax.vjp(normalize, rows_in, gain_row, shift_row)
    return pullback(gradient)


def activate(hidden):
    return jax.nn.gelu(hidden, approximate=False)


def activate_back(hidden, gradient):
    unused, pullback = jax.vjp(activate, hidden)
    return pullback(gradient)[0]


def product(operand, weight):
    return jnp.einsum("crd,dh->crh", operand, weight, preferred_element_type=jnp.float32)


def product_back(gradient, weight):
    return jnp.einsum("crh,dh->crd", gradient, weight, preferred_element_type=jnp.float32)


def weight_grad(operand, gradient):
    return jnp.einsum("crd,crh->dh", operand, gradient, preferred_element_type=jnp.float32)


def column_sums(gradient):
    return jnp.sum(gradient, axis=(0, 1), dtype=jnp.float32)


def gather_rows(normed):
    return lax.all_gather(normed, "mp", axis=1, tiled=True)


def sum_rows(partial_value):
    return lax.psum_scatter(
        partial_value.astype(jnp.bfloat16), "mp", scatter_dimension=1, tiled=True
    ).astype(jnp.float32)


def gather_grads(gradient):
    return lax.all_gather(gradient, "mp", axis=1, tiled=True)


def sum_grads(partial_value):
    return lax.psum_scatter(
        partial_value.astype(jnp.bfloat16), "mp", scatter_dimension=1, tiled=True
    ).astype(jnp.float32)


def sum_clips(values):
    sent = tuple(value.astype(jnp.bfloat16) for value in values)
    return tuple(value.astype(jnp.float32) for value in lax.psum(sent, "dp"))


def score_block(queries, key_rows, causal):
    row_count = queries.shape[0]
    split_query = queries.reshape(row_count, -1, HEAD)
    split_keys = key_rows.reshape(key_rows.shape[0], -1, HEAD)
    scores = jnp.einsum(
        "rhe,she->hrs", split_query, split_keys, preferred_element_type=jnp.float32
    ) * HEAD ** (-0.5)
    if causal:
        row_index = lax.broadcasted_iota(jnp.int32, scores.shape, 1)
        col_index = lax.broadcasted_iota(jnp.int32, scores.shape, 2)
        scores = jnp.where(col_index <= row_index, scores, masked_score)
    return (scores, split_query, split_keys)


def attend(queries, key_rows, values, causal):

    def one_clip(clip_block):
        query_clip, keys_clip, values_clip = clip_block
        scores, unused_query, unused_keys = score_block(query_clip, keys_clip, causal)
        highest = jnp.max(scores, axis=-1, keepdims=True)
        logsum = highest + jnp.log(jnp.sum(jnp.exp(scores - highest), axis=-1, keepdims=True))
        weights = jnp.exp(scores - logsum).astype(jnp.bfloat16)
        split_values = values_clip.reshape(values_clip.shape[0], -1, HEAD)
        mixed_out = jnp.einsum(
            "hrs,she->rhe", weights, split_values, preferred_element_type=jnp.float32
        )
        return (mixed_out.reshape(query_clip.shape).astype(jnp.bfloat16), logsum)

    return lax.map(one_clip, (queries, key_rows, values))


def attend_back(queries, key_rows, values, logsum, gradient, causal):

    def one_clip(clip_block):
        query_clip, keys_clip, values_clip, logsum_clip, grad_clip = clip_block
        scores, split_query, split_keys = score_block(query_clip, keys_clip, causal)
        weights = jnp.exp(scores - logsum_clip)
        split_values = values_clip.reshape(values_clip.shape[0], -1, HEAD)
        split_grad = grad_clip.reshape(grad_clip.shape[0], -1, HEAD)
        weight_grads = jnp.einsum(
            "rhe,she->hrs", split_grad, split_values, preferred_element_type=jnp.float32
        )
        inner_sum = jnp.sum(weights * weight_grads, axis=-1, keepdims=True)
        score_grads = (weights * (weight_grads - inner_sum)).astype(jnp.bfloat16)
        score_scale = HEAD ** (-0.5)
        query_grad = (
            jnp.einsum("hrs,she->rhe", score_grads, split_keys, preferred_element_type=jnp.float32)
            * score_scale
        )
        keys_grad = (
            jnp.einsum("hrs,rhe->she", score_grads, split_query, preferred_element_type=jnp.float32)
            * score_scale
        )
        values_grad = jnp.einsum(
            "hrs,rhe->she",
            weights.astype(jnp.bfloat16),
            split_grad,
            preferred_element_type=jnp.float32,
        )
        return tuple(
            (
                piece_grad.reshape(piece_grad.shape[0], -1).astype(jnp.bfloat16)
                for piece_grad in (query_grad, keys_grad, values_grad)
            )
        )

    return lax.map(one_clip, (queries, key_rows, values, logsum, gradient))


def encoder_forward(frames, weights):
    norm_gain, norm_shift, qkv, qv_bias, proj, out_bias, fc1, fc1_bias, fc2 = weights
    normed = normalize(frames, norm_gain[0], norm_shift[0]).astype(jnp.bfloat16)
    gathered = gather_rows(normed)
    queries = (product(gathered, qkv[0, 0]) + qv_bias[0, 0]).astype(jnp.bfloat16)
    key_rows = product(gathered, qkv[0, 1]).astype(jnp.bfloat16)
    values = (product(gathered, qkv[0, 2]) + qv_bias[0, 1]).astype(jnp.bfloat16)
    mixed_out, logsum = attend(queries, key_rows, values, False)
    middle = frames + sum_rows(product(mixed_out, proj[0])) + out_bias[0]
    gathered_two = gather_rows(normalize(middle, norm_gain[1], norm_shift[1]).astype(jnp.bfloat16))
    hidden = product(gathered_two, fc1[0]) + fc1_bias[0]
    activated = activate(hidden).astype(jnp.bfloat16)
    encoded = middle + sum_rows(product(activated, fc2[0])) + out_bias[1]
    return (
        encoded,
        (
            gathered,
            queries,
            key_rows,
            values,
            mixed_out,
            logsum,
            middle,
            gathered_two,
            hidden,
            activated,
        ),
    )


def encoder_backward(frames, saved, gradient, weights):
    norm_gain, norm_shift, qkv, qv_bias, proj, out_bias, fc1, fc1_bias, fc2 = weights
    (
        gathered,
        queries,
        key_rows,
        values,
        mixed_out,
        logsum,
        middle,
        gathered_two,
        hidden,
        activated,
    ) = saved
    branch = gather_grads(gradient.astype(jnp.bfloat16))
    fc2_grad = weight_grad(activated, branch)
    bias_mlp = column_sums(branch)
    hidden_grad = activate_back(hidden, product_back(branch, fc2[0])).astype(jnp.bfloat16)
    fc1_grad = weight_grad(gathered_two, hidden_grad)
    fc1_bias_grad = column_sums(hidden_grad)
    middle_norm, gain_one, shift_one = norm_back(
        middle, norm_gain[1], norm_shift[1], sum_grads(product_back(hidden_grad, fc1[0]))
    )
    middle_grad = gradient + middle_norm
    branch = gather_grads(middle_grad.astype(jnp.bfloat16))
    proj_grad = weight_grad(mixed_out, branch)
    bias_attend = column_sums(branch)
    mixed_grad = product_back(branch, proj[0]).astype(jnp.bfloat16)
    query_grad, key_grad, value_grad = attend_back(
        queries, key_rows, values, logsum, mixed_grad, False
    )
    qkv_grad = jnp.stack(
        [
            weight_grad(gathered, query_grad),
            weight_grad(gathered, key_grad),
            weight_grad(gathered, value_grad),
        ]
    )
    qv_grad = jnp.stack([column_sums(query_grad), column_sums(value_grad)])
    gathered_grad = (
        product_back(query_grad, qkv[0, 0])
        + product_back(key_grad, qkv[0, 1])
        + product_back(value_grad, qkv[0, 2])
    )
    frames_norm, gain_zero, shift_zero = norm_back(
        frames, norm_gain[0], norm_shift[0], sum_grads(gathered_grad)
    )
    frames_grad = middle_grad + frames_norm
    gradients = (
        qkv_grad,
        qv_grad,
        proj_grad,
        jnp.stack([bias_attend, bias_mlp]),
        fc1_grad,
        fc1_bias_grad,
        fc2_grad,
    )
    return (
        frames_grad,
        gradients,
        jnp.stack([gain_zero, gain_one]),
        jnp.stack([shift_zero, shift_one]),
    )


def decoder_forward(tokens, memory, valid_rows, weights):
    norm_gain, norm_shift, qkv, qv_bias, proj, out_bias, fc1, fc1_bias, fc2 = weights
    gathered = gather_rows(normalize(tokens, norm_gain[2], norm_shift[2]).astype(jnp.bfloat16))
    queries = (product(gathered, qkv[1, 0]) + qv_bias[1, 0]).astype(jnp.bfloat16)
    key_rows = product(gathered, qkv[1, 1]).astype(jnp.bfloat16)
    values = (product(gathered, qkv[1, 2]) + qv_bias[1, 1]).astype(jnp.bfloat16)
    mixed_out, logsum = attend(queries, key_rows, values, True)
    after_self = tokens + sum_rows(product(mixed_out, proj[1])) + out_bias[2]
    gathered_two = gather_rows(
        normalize(after_self, norm_gain[3], norm_shift[3]).astype(jnp.bfloat16)
    )
    cross_queries = (product(gathered_two, qkv[2, 0]) + qv_bias[2, 0]).astype(jnp.bfloat16)
    cross_keys = product(memory, qkv[2, 1]).astype(jnp.bfloat16)
    cross_values = (product(memory, qkv[2, 2]) + qv_bias[2, 1]).astype(jnp.bfloat16)
    cross_mixed, cross_logsum = attend(cross_queries, cross_keys, cross_values, False)
    second = after_self + sum_rows(product(cross_mixed, proj[2])) + out_bias[3]
    gathered_three = gather_rows(
        normalize(second, norm_gain[4], norm_shift[4]).astype(jnp.bfloat16)
    )
    hidden = product(gathered_three, fc1[1]) + fc1_bias[1]
    activated = activate(hidden).astype(jnp.bfloat16)
    after_mlp = second + sum_rows(product(activated, fc2[1])) + out_bias[4]
    saved = (
        gathered,
        queries,
        key_rows,
        values,
        mixed_out,
        logsum,
        after_self,
        gathered_two,
        cross_queries,
        cross_keys,
        cross_values,
        cross_mixed,
        cross_logsum,
        second,
        gathered_three,
        hidden,
        activated,
    )
    return (after_mlp * valid_rows, saved)


def decoder_backward(tokens, memory, saved, gradient, weights):
    norm_gain, norm_shift, qkv, qv_bias, proj, out_bias, fc1, fc1_bias, fc2 = weights
    (
        gathered,
        queries,
        key_rows,
        values,
        mixed_out,
        logsum,
        after_self,
        gathered_two,
        cross_queries,
        cross_keys,
        cross_values,
        cross_mixed,
        cross_logsum,
        second,
        gathered_three,
        hidden,
        activated,
    ) = saved
    branch = gather_grads(gradient.astype(jnp.bfloat16))
    fc2_grad = weight_grad(activated, branch)
    bias_mlp = column_sums(branch)
    hidden_grad = activate_back(hidden, product_back(branch, fc2[1])).astype(jnp.bfloat16)
    fc1_grad = weight_grad(gathered_three, hidden_grad)
    fc1_bias_grad = column_sums(hidden_grad)
    second_norm, gain_three, shift_three = norm_back(
        second, norm_gain[4], norm_shift[4], sum_grads(product_back(hidden_grad, fc1[1]))
    )
    second_grad = gradient + second_norm
    branch = gather_grads(second_grad.astype(jnp.bfloat16))
    cross_proj_grad = weight_grad(cross_mixed, branch)
    bias_cross = column_sums(branch)
    cross_mixed_grad = product_back(branch, proj[2]).astype(jnp.bfloat16)
    cross_query_grad, cross_key_grad, cross_value_grad = attend_back(
        cross_queries, cross_keys, cross_values, cross_logsum, cross_mixed_grad, False
    )
    cross_qkv_grad = jnp.stack(
        [
            weight_grad(gathered_two, cross_query_grad),
            weight_grad(memory, cross_key_grad),
            weight_grad(memory, cross_value_grad),
        ]
    )
    cross_qv_grad = jnp.stack([column_sums(cross_query_grad), column_sums(cross_value_grad)])
    memory_grad = sum_grads(
        product_back(cross_key_grad, qkv[2, 1]) + product_back(cross_value_grad, qkv[2, 2])
    )
    self_norm, gain_two, shift_two = norm_back(
        after_self,
        norm_gain[3],
        norm_shift[3],
        sum_grads(product_back(cross_query_grad, qkv[2, 0])),
    )
    self_grad = second_grad + self_norm
    branch = gather_grads(self_grad.astype(jnp.bfloat16))
    self_proj_grad = weight_grad(mixed_out, branch)
    bias_self = column_sums(branch)
    mixed_grad = product_back(branch, proj[1]).astype(jnp.bfloat16)
    query_grad, key_grad, value_grad = attend_back(
        queries, key_rows, values, logsum, mixed_grad, True
    )
    self_qkv_grad = jnp.stack(
        [
            weight_grad(gathered, query_grad),
            weight_grad(gathered, key_grad),
            weight_grad(gathered, value_grad),
        ]
    )
    self_qv_grad = jnp.stack([column_sums(query_grad), column_sums(value_grad)])
    gathered_grad = (
        product_back(query_grad, qkv[1, 0])
        + product_back(key_grad, qkv[1, 1])
        + product_back(value_grad, qkv[1, 2])
    )
    tokens_norm, gain_one, shift_one = norm_back(
        tokens, norm_gain[2], norm_shift[2], sum_grads(gathered_grad)
    )
    tokens_grad = self_grad + tokens_norm
    gradients = (
        jnp.stack([self_qkv_grad, cross_qkv_grad]),
        jnp.stack([self_qv_grad, cross_qv_grad]),
        jnp.stack([self_proj_grad, cross_proj_grad]),
        jnp.stack([bias_self, bias_cross, bias_mlp]),
        fc1_grad,
        fc1_bias_grad,
        fc2_grad,
    )
    return (
        tokens_grad,
        memory_grad,
        gradients,
        jnp.stack([gain_one, gain_two, gain_three]),
        jnp.stack([shift_one, shift_two, shift_three]),
    )


def on_device(
    enc_in,
    dec_in,
    dec_len,
    norm_gain,
    norm_shift,
    qkv,
    qv_bias,
    proj,
    out_bias,
    fc1,
    fc1_bias,
    fc2,
    enc_cot,
    dec_cot,
):
    weights = (
        norm_gain.astype(jnp.float32),
        norm_shift.astype(jnp.float32),
        qkv,
        qv_bias,
        proj,
        out_bias,
        fc1,
        fc1_bias,
        fc2,
    )
    frames = enc_in.astype(jnp.float32)
    tokens = dec_in.astype(jnp.float32)
    clip_count, token_count = (dec_in.shape[0], dec_in.shape[1])
    positions = lax.axis_index("mp") * token_count + lax.broadcasted_iota(
        jnp.int32, (clip_count, token_count), 1
    )
    valid_rows = (positions < dec_len[:, None]).astype(jnp.float32)[:, :, None]
    encoded, enc_saved = encoder_forward(frames, weights)
    enc_out = encoded.astype(jnp.bfloat16)
    memory = gather_rows(enc_out)
    decoded, dec_saved = decoder_forward(tokens, memory, valid_rows, weights)
    tokens_grad, memory_grad, dec_grads, dec_gains, dec_shifts = decoder_backward(
        tokens, memory, dec_saved, dec_cot.astype(jnp.float32) * valid_rows, weights
    )
    encoded_grad = enc_cot.astype(jnp.float32) + memory_grad
    frames_grad, enc_grads, enc_gains, enc_shifts = encoder_backward(
        frames, enc_saved, encoded_grad, weights
    )
    dec_wide = sum_clips((dec_grads[0], dec_grads[2], dec_grads[4], dec_grads[6]))
    enc_mlp = sum_clips((enc_grads[4], enc_grads[6]))
    enc_attend = sum_clips((enc_grads[0], enc_grads[2]))
    merged = (
        jnp.concatenate([enc_attend[0][None], dec_wide[0]]),
        jnp.concatenate([enc_grads[1][None], dec_grads[1]]),
        jnp.concatenate([enc_attend[1][None], dec_wide[1]]),
        jnp.concatenate([enc_grads[3], dec_grads[3]]),
        jnp.stack([enc_mlp[0], dec_wide[2]]),
        jnp.stack([enc_grads[5], dec_grads[5]]),
        jnp.stack([enc_mlp[1], dec_wide[3]]),
    )
    narrow = lax.psum((merged[1], merged[3], merged[5]), "dp")
    merged = (merged[0], narrow[0], merged[2], narrow[1], merged[4], narrow[2], merged[6])
    gain_grad, shift_grad = lax.psum(
        (jnp.concatenate([enc_gains, dec_gains]), jnp.concatenate([enc_shifts, dec_shifts])),
        ("dp", "mp"),
    )
    return (
        enc_out,
        decoded.astype(jnp.bfloat16),
        frames_grad,
        tokens_grad,
        gain_grad,
        shift_grad,
        merged[0],
        merged[1],
        merged[2],
        merged[3],
        merged[4],
        merged[5],
        merged[6],
    )


def solution(mesh):
    placed = (
        P("dp", "mp", None),
        P("dp", "mp", None),
        P("dp"),
        P(),
        P(),
        P(None, None, None, "mp"),
        P(None, None, "mp"),
        P(None, "mp", None),
        P(),
        P(None, None, "mp"),
        P(None, "mp"),
        P(None, "mp", None),
        P("dp", "mp", None),
        P("dp", "mp", None),
    )
    return jax.shard_map(
        on_device,
        mesh=mesh,
        in_specs=placed,
        out_specs=(
            P("dp", "mp", None),
            P("dp", "mp", None),
            P("dp", "mp", None),
            P("dp", "mp", None),
            P(),
            P(),
            P(None, None, None, "mp"),
            P(None, None, "mp"),
            P(None, "mp", None),
            P(),
            P(None, None, "mp"),
            P(None, "mp"),
            P(None, "mp", None),
        ),
        check_vma=False,
    )
```

```python
import functools
import math

import jax
import jax.numpy as jnp
from jax import lax
from jax.experimental import pallas as pl
from jax.experimental.pallas import tpu as pltpu
from jax.sharding import PartitionSpec as P

HEAD = 64
epsilon = 1e-05
masked_score = -1e30
f32 = jnp.float32
bf16 = jnp.bfloat16
NN = (((1,), (0,)), ((), ()))
NT = (((1,), (1,)), ((), ()))
TN = (((0,), (0,)), ((), ()))
SCALE = HEAD ** (-0.5)
SCORE_TO_LOG2 = SCALE * math.log2(math.e)
ANY = pl.BlockSpec(memory_space=pl.ANY)
VMEM = pl.BlockSpec(memory_space=pltpu.VMEM)


def dot(a, b, dims=NN):
    return lax.dot_general(a, b, dims, preferred_element_type=f32)


def window(start, size):
    return pl.ds(pl.multiple_of(start, 16), size)


def places():
    me = lax.axis_index("mp")
    core = lax.rem(me, 2)
    mate = me + 1 - 2 * core
    opp = lax.rem(me + 2, 4)
    diag = lax.rem(mate + 2, 4)
    return me, mate, opp, diag


def remote(src, dst, sent, landed, axis, index):
    return pltpu.make_async_remote_copy(
        src_ref=src,
        dst_ref=dst,
        send_sem=sent,
        recv_sem=landed,
        device_id={axis: index},
        device_id_type=pl.DeviceIdType.MESH,
    )


class Gather:
    def __init__(self, buf, sems, rows, step):
        self.buf, self.sems, self.rows, self.step = buf, sems, rows, step
        self.me, self.mate_id, self.opp_id, self.diag_id = places()

    def at(self, block, j):
        return window(block * self.rows + j * self.step, self.step)

    def copy(self, kind, block, j, target):
        part = self.buf.at[self.at(block, j)]
        return remote(part, part, self.sems.at[2 * kind, j], self.sems.at[2 * kind + 1, j], "mp", target)

    def send(self, j):
        self.copy(0, self.me, j, self.opp_id).start()
        self.copy(1, self.me, j, self.mate_id).start()

    def mate(self, j):
        self.copy(1, self.mate_id, j, self.mate_id).wait_recv()

    def opp(self, j):
        self.copy(0, self.opp_id, j, self.opp_id).wait_recv()
        self.copy(2, self.opp_id, j, self.mate_id).start()

    def diag(self, j):
        self.copy(2, self.diag_id, j, self.mate_id).wait_recv()

    def close(self, j):
        self.copy(0, self.me, j, self.opp_id).wait_send()
        self.copy(1, self.me, j, self.mate_id).wait_send()
        self.copy(2, self.opp_id, j, self.mate_id).wait_send()


class Scatter:
    def __init__(self, own, send, land, ysend, yland, sems, rows, step):
        self.own, self.out, self.land, self.ysend, self.yland = own, send, land, ysend, yland
        self.sems, self.rows, self.step = sems, rows, step
        self.me, self.mate_id, self.opp_id, self.diag_id = places()

    def near(self, half, j):
        part = window(half * self.rows + j * self.step, self.step)
        return remote(
            self.out.at[part], self.land.at[part],
            self.sems.at[2 * half, j], self.sems.at[2 * half + 1, j], "mp", self.mate_id,
        )

    def far(self, j):
        part = window(j * self.step, self.step)
        return remote(
            self.ysend.at[part], self.yland.at[part],
            self.sems.at[4, j], self.sems.at[5, j], "mp", self.opp_id,
        )

    def put_diag(self, j, value):
        self.out[window(j * self.step, self.step), :] = value.astype(bf16)
        self.near(0, j).start()

    def put_opp(self, j, value):
        part = window(j * self.step, self.step)
        self.near(0, j).wait_recv()
        self.ysend[part, :] = (value + self.land[part, :].astype(f32)).astype(bf16)
        self.far(j).start()

    def put_mate(self, j, value):
        self.out[window(self.rows + j * self.step, self.step), :] = value.astype(bf16)
        self.near(1, j).start()

    def put_own(self, j, value):
        self.own[window(j * self.step, self.step), :] = value

    def total(self, j):
        self.near(1, j).wait_recv()
        self.far(j).wait_recv()
        part = window(j * self.step, self.step)
        near = self.land[window(self.rows + j * self.step, self.step), :].astype(f32)
        return self.own[part, :] + near + self.yland[part, :].astype(f32)

    def close(self, j):
        self.near(0, j).wait_send()
        self.near(1, j).wait_send()
        self.far(j).wait_send()


def scatter_shapes(rows, width, steps):
    return [
        pltpu.VMEM((rows, width), f32),
        pltpu.VMEM((2 * rows, width), bf16),
        pltpu.VMEM((2 * rows, width), bf16),
        pltpu.VMEM((rows, width), bf16),
        pltpu.VMEM((rows, width), bf16),
        pltpu.SemaphoreType.DMA((6, steps)),
    ]


def meet(partners):
    barrier = pltpu.get_barrier_semaphore()
    for axis, index in partners:
        pl.semaphore_signal(barrier, inc=1, device_id={axis: index}, device_id_type=pl.DeviceIdType.MESH)
    pl.semaphore_wait(barrier, len(partners))


def layer_norm(rows_in, gain_row, shift_row):
    average = jnp.mean(rows_in, axis=-1, keepdims=True)
    centred = rows_in - average
    spread = jnp.mean(centred * centred, axis=-1, keepdims=True)
    return centred * lax.rsqrt(spread + epsilon) * gain_row + shift_row


def head_row(width, h):
    lane = lax.broadcasted_iota(jnp.int32, (1, width), 1)
    return jnp.where((lane >= h * HEAD) & (lane < (h + 1) * HEAD), 1.0, 0.0).astype(f32)


def attend_rows(q_ref, k_ref, v_ref, out_ref, log_ref, start, size, causal):
    width = q_ref.shape[1]
    part = window(start, size)
    queries = q_ref[part, :]
    keys = k_ref[...]
    values = v_ref[...]
    lane = lax.broadcasted_iota(jnp.int32, (size, log_ref.shape[1]), 1)
    mixed = jnp.zeros((size, width), f32)
    logs = jnp.zeros((size, log_ref.shape[1]), f32)
    for h in range(width // HEAD):
        picked = head_row(width, h)
        scores = dot(queries * picked.astype(bf16), keys, NT)
        if causal:
            row_index = lax.broadcasted_iota(jnp.int32, scores.shape, 0) + start
            col_index = lax.broadcasted_iota(jnp.int32, scores.shape, 1)
            scores = jnp.where(col_index <= row_index, scores, masked_score)
        highest = jnp.max(scores, axis=-1, keepdims=True)
        powers = jnp.exp2((scores - highest) * SCORE_TO_LOG2)
        total = jnp.sum(powers, axis=-1, keepdims=True)
        mixed = mixed + dot(powers.astype(bf16), values) * (picked / total)
        logs = jnp.where(lane == h, highest * SCORE_TO_LOG2 + jnp.log2(total), logs)
    out_ref[part, :] = mixed.astype(bf16)
    log_ref[part, :] = logs


def gelu_parts(hidden):
    below = 0.5 + 0.5 * lax.erf(hidden * (0.5 ** 0.5))
    density = jnp.exp2(hidden * hidden * (-0.5 * math.log2(math.e))) * ((2 * math.pi) ** (-0.5))
    return hidden * below, below + hidden * density


def forward_kernel(
    R, T,
    enc_in, dec_in, gain_ref, shift_ref, qv_bias, out_bias, fc1_bias, qkv, proj, fc1, fc2,
    o_enc, o_g1, o_q, o_k, o_v, o_a, o_l, o_mid, o_g2, o_e, o_gd, o_g3, o_ck, o_cv,
    o_m1, o_sq, o_sk, o_sv, o_sa, o_sl, o_as, o_m2, o_cq,
    w_e, w_s, w_c, w_pe, w_ps, w_f1, w_f2,
    g1, q, k, v, a, l, lt, mid, g2, e, gd, g3, ck, cv, m1, sq, sk, sv, sa, sl, slt, after, m2, cq, enc,
    *rest,
):
    rest = list(rest)
    take = lambda n: [rest.pop(0) for _ in range(n)]
    rs1, rs2, rsd = take(6), take(6), take(6)
    ag1, ag2, ag3, agd1, agd2 = take(5)
    load_sem, save_sem = take(2)
    S = T
    steps = R // S
    me, mate, opp, diag = places()
    loads = [
        pltpu.make_async_copy(src, dst, load_sem.at[i])
        for i, (src, dst) in enumerate(
            [(qkv.at[0], w_e), (qkv.at[1], w_s), (qkv.at[2], w_c), (proj.at[0], w_pe), (proj.at[1], w_ps),
             (fc1.at[0], w_f1), (fc2.at[0], w_f2)]
        )
    ]
    for load in loads:
        load.start()
    saves = []

    def save(src, dst):
        copy = pltpu.make_async_copy(src, dst, save_sem.at[len(saves)])
        copy.start()
        saves.append(copy)

    gains = gain_ref[...].astype(f32)
    shifts = shift_ref[...].astype(f32)
    branch_bias = out_bias[...].astype(f32)
    head_bias = qv_bias[...].astype(f32)
    wide_bias = fc1_bias[...].astype(f32)

    meet([("mp", mate), ("mp", opp)])

    gd1 = Gather(m1, agd1, T, S)
    m1[window(me * T, T), :] = layer_norm(dec_in[0].astype(f32), gains[2:3], shifts[2:3]).astype(bf16)
    gd1.send(0)
    ge1 = Gather(g1, ag1, R, S)

    @pl.loop(0, steps)
    def _(j):
        rows = enc_in[0, window(j * S, S), :].astype(f32)
        g1[window(me * R + j * S, S), :] = layer_norm(rows, gains[0:1], shifts[0:1]).astype(bf16)
        ge1.send(j)

    def project_block(block):
        part = window(block * R, R)
        rows = g1[part, :]
        q[part, :] = (dot(rows, w_e[0]) + head_bias[0, 0:1]).astype(bf16)
        k[part, :] = dot(rows, w_e[1]).astype(bf16)
        v[part, :] = (dot(rows, w_e[2]) + head_bias[0, 1:2]).astype(bf16)

    loads[0].wait()

    @pl.loop(0, steps)
    def _(j):
        ge1.mate(j)

    @pl.loop(0, 2)
    def _(i):
        project_block(me + i * (mate - me))

    gd1.mate(0)
    gd1.opp(0)
    gd1.diag(0)
    save(m1, o_m1)
    loads[1].wait()
    sq[...] = (dot(m1[...], w_s[0]) + head_bias[1, 0:1]).astype(bf16)
    sk[...] = dot(m1[...], w_s[1]).astype(bf16)
    sv[...] = (dot(m1[...], w_s[2]) + head_bias[1, 1:2]).astype(bf16)
    save(sq, o_sq)
    save(sk, o_sk)
    save(sv, o_sv)

    @pl.loop(0, 2)
    def _(i):
        attend_rows(sq, sk, sv, sa, sl, i * 2 * T, 2 * T, True)

    save(sa, o_sa)
    slt[...] = jnp.transpose(sl[...])[0:8]
    save(slt, o_sl)
    loads[4].wait()
    sd = Scatter(*rsd, T, S)
    sd.put_diag(0, dot(sa[window(diag * T, T), :], w_ps[...]))
    sd.put_opp(0, dot(sa[window(opp * T, T), :], w_ps[...]))
    sd.put_mate(0, dot(sa[window(mate * T, T), :], w_ps[...]))
    sd.put_own(0, dot(sa[window(me * T, T), :], w_ps[...]))

    @pl.loop(0, steps)
    def _(j):
        ge1.opp(j)

    @pl.loop(0, steps)
    def _(j):
        ge1.diag(j)

    @pl.loop(0, 2)
    def _(i):
        project_block(opp + i * (diag - opp))

    save(g1, o_g1)
    save(q, o_q)
    save(k, o_k)
    save(v, o_v)
    loads[3].wait()
    s1 = Scatter(*rs1, R, S)

    def attend_block(block, put):
        attend_rows(q, k, v, a, l, block * R, R, False)

        @pl.loop(0, steps)
        def _(j):
            put(j, dot(a[window(block * R + j * S, S), :], w_pe[...]))

    attend_block(diag, s1.put_diag)
    attend_block(opp, s1.put_opp)

    after[...] = dec_in[0].astype(f32) + sd.total(0) + branch_bias[2:3]
    gd2 = Gather(m2, agd2, T, S)
    m2[window(me * T, T), :] = layer_norm(after[...], gains[3:4], shifts[3:4]).astype(bf16)
    gd2.send(0)
    save(after, o_as)

    attend_block(mate, s1.put_mate)
    attend_block(me, s1.put_own)
    lt[...] = jnp.transpose(l[...])[0:8]
    save(lt, o_l)
    save(a, o_a)

    ge2 = Gather(g2, ag2, R, S)

    @pl.loop(0, steps)
    def _(j):
        part = window(j * S, S)
        rows = enc_in[0, part, :].astype(f32) + s1.total(j) + branch_bias[0:1]
        mid[part, :] = rows
        g2[window(me * R + j * S, S), :] = layer_norm(rows, gains[1:2], shifts[1:2]).astype(bf16)
        ge2.send(j)

    save(mid, o_mid)
    gd2.mate(0)
    gd2.opp(0)
    gd2.diag(0)
    loads[2].wait()
    cq[...] = (dot(m2[...], w_c[0]) + head_bias[2, 0:1]).astype(bf16)
    save(m2, o_m2)
    save(cq, o_cq)
    loads[5].wait()
    loads[6].wait()
    s2 = Scatter(*rs2, R, S)

    def feed(block, j):
        part = window(block * R + j * S, S)
        hidden = dot(g2[part, :], w_f1[...]) + wide_bias[0:1]
        active, slope = gelu_parts(hidden)
        active = active.astype(bf16)
        e[part, :] = active
        gd[part, :] = slope.astype(bf16)
        return dot(active, w_f2[...])

    @pl.loop(0, steps)
    def _(j):
        s2.put_own(j, feed(me, j))

    @pl.loop(0, steps)
    def _(j):
        ge2.mate(j)
        s2.put_mate(j, feed(mate, j))

    @pl.loop(0, steps)
    def _(j):
        ge2.opp(j)
        ge2.diag(j)
        s2.put_diag(j, feed(diag, j))
        s2.put_opp(j, feed(opp, j))

    save(g2, o_g2)
    save(e, o_e)
    save(gd, o_gd)
    ge3 = Gather(g3, ag3, R, S)

    @pl.loop(0, steps)
    def _(j):
        part = window(j * S, S)
        rows = (mid[part, :] + s2.total(j) + branch_bias[1:2]).astype(bf16)
        enc[part, :] = rows
        g3[window(me * R + j * S, S), :] = rows
        ge3.send(j)

    save(enc, o_enc)

    def cross_block(block):
        part = window(block * R, R)
        rows = g3[part, :]
        ck[part, :] = dot(rows, w_c[1]).astype(bf16)
        cv[part, :] = (dot(rows, w_c[2]) + head_bias[2, 1:2]).astype(bf16)

    @pl.loop(0, steps)
    def _(j):
        ge3.mate(j)

    @pl.loop(0, 2)
    def _(i):
        cross_block(me + i * (mate - me))

    @pl.loop(0, steps)
    def _(j):
        ge3.opp(j)

    @pl.loop(0, steps)
    def _(j):
        ge3.diag(j)

    @pl.loop(0, 2)
    def _(i):
        cross_block(opp + i * (diag - opp))

    save(g3, o_g3)
    save(ck, o_ck)
    save(cv, o_cv)

    @pl.loop(0, steps)
    def _(j):
        for each in (ge1, s1, ge2, s2, ge3):
            each.close(j)

    for each in (gd1, sd, gd2):
        each.close(0)
    for copy in saves:
        copy.wait()


def forward_call(enc_in, dec_in, norm_gain, norm_shift, qv_bias, out_bias, fc1_bias, qkv, proj, fc1, fc2):
    R, D = enc_in.shape[1:]
    T = dec_in.shape[1]
    W = qkv.shape[-1]
    F = fc1.shape[-1]
    steps = R // T
    V = lambda *shape: pltpu.VMEM(shape, bf16)
    V32 = lambda *shape: pltpu.VMEM(shape, f32)
    B = lambda *shape: jax.ShapeDtypeStruct(shape, bf16)
    B32 = lambda *shape: jax.ShapeDtypeStruct(shape, f32)
    N, M = 4 * R, 4 * T
    outs = dict(
        enc=B(R, D), g1=B(N, D), q=B(N, W), k=B(N, W), v=B(N, W), a=B(N, W), l=B32(8, N), mid=B32(R, D),
        g2=B(N, D), e=B(N, F), gd=B(N, F), g3=B(N, D), ck=B(N, W), cv=B(N, W),
        m1=B(M, D), sq=B(M, W), sk=B(M, W), sv=B(M, W), sa=B(M, W), sl=B32(8, M), after=B32(T, D),
        m2=B(M, D), cq=B(M, W),
    )
    scratch = [
        V(3, D, W), V(3, D, W), V(3, D, W), V(W, D), V(W, D), V(D, F), V(F, D),
        V(N, D), V(N, W), V(N, W), V(N, W), V(N, W), V32(N, 128), V32(8, N), V32(R, D), V(N, D), V(N, F), V(N, F),
        V(N, D), V(N, W), V(N, W),
        V(M, D), V(M, W), V(M, W), V(M, W), V(M, W), V32(M, 128), V32(8, M), V32(T, D), V(M, D), V(M, W), V(R, D),
    ]
    scratch += scatter_shapes(R, D, steps) + scatter_shapes(R, D, steps) + scatter_shapes(T, D, 1)
    scratch += [pltpu.SemaphoreType.DMA((6, steps))] * 3 + [pltpu.SemaphoreType.DMA((6, 1))] * 2
    scratch += [pltpu.SemaphoreType.DMA((7,)), pltpu.SemaphoreType.DMA((len(outs),))]
    results = pl.pallas_call(
        functools.partial(forward_kernel, R, T),
        out_shape=list(outs.values()),
        in_specs=[VMEM] * 7 + [ANY] * 4,
        out_specs=[ANY] * len(outs),
        scratch_shapes=scratch,
        compiler_params=pltpu.CompilerParams(
            collective_id=0, has_side_effects=True, vmem_limit_bytes=60 << 20
        ),
        name="encoder_forward",
    )(enc_in, dec_in, norm_gain, norm_shift, qv_bias, out_bias, fc1_bias, qkv, proj, fc1, fc2)
    return dict(zip(outs, results))


def normalize(rows_in, gain_row, shift_row):
    average = jnp.mean(rows_in, axis=-1, keepdims=True)
    centred = rows_in - average
    spread = jnp.mean(centred * centred, axis=-1, keepdims=True)
    return centred * lax.rsqrt(spread + epsilon) * gain_row + shift_row


def norm_back(rows_in, gain_row, shift_row, gradient):
    unused, pullback = jax.vjp(normalize, rows_in, gain_row, shift_row)
    return pullback(gradient)


def activate(hidden):
    return jax.nn.gelu(hidden, approximate=False)


def activate_back(hidden, gradient):
    unused, pullback = jax.vjp(activate, hidden)
    return pullback(gradient)[0]


def product(operand, weight):
    return jnp.einsum("crd,dh->crh", operand, weight, preferred_element_type=jnp.float32)


def product_back(gradient, weight):
    return jnp.einsum("crh,dh->crd", gradient, weight, preferred_element_type=jnp.float32)


def weight_grad(operand, gradient):
    return jnp.einsum("crd,crh->dh", operand, gradient, preferred_element_type=jnp.float32)


def column_sums(gradient):
    return jnp.sum(gradient, axis=(0, 1), dtype=jnp.float32)


def gather_rows(normed):
    return lax.all_gather(normed, "mp", axis=1, tiled=True)


def sum_rows(partial_value):
    return lax.psum_scatter(
        partial_value.astype(jnp.bfloat16), "mp", scatter_dimension=1, tiled=True
    ).astype(jnp.float32)


def gather_grads(gradient):
    return lax.all_gather(gradient, "mp", axis=1, tiled=True)


def sum_grads(partial_value):
    return lax.psum_scatter(
        partial_value.astype(jnp.bfloat16), "mp", scatter_dimension=1, tiled=True
    ).astype(jnp.float32)


def sum_clips(values):
    sent = tuple(value.astype(jnp.bfloat16) for value in values)
    return tuple(value.astype(jnp.float32) for value in lax.psum(sent, "dp"))


def score_block(queries, key_rows, causal):
    row_count = queries.shape[0]
    split_query = queries.reshape(row_count, -1, HEAD)
    split_keys = key_rows.reshape(key_rows.shape[0], -1, HEAD)
    scores = jnp.einsum(
        "rhe,she->hrs", split_query, split_keys, preferred_element_type=jnp.float32
    ) * HEAD ** (-0.5)
    if causal:
        row_index = lax.broadcasted_iota(jnp.int32, scores.shape, 1)
        col_index = lax.broadcasted_iota(jnp.int32, scores.shape, 2)
        scores = jnp.where(col_index <= row_index, scores, masked_score)
    return (scores, split_query, split_keys)


def attend(queries, key_rows, values, causal):

    def one_clip(clip_block):
        query_clip, keys_clip, values_clip = clip_block
        scores, unused_query, unused_keys = score_block(query_clip, keys_clip, causal)
        highest = jnp.max(scores, axis=-1, keepdims=True)
        logsum = highest + jnp.log(jnp.sum(jnp.exp(scores - highest), axis=-1, keepdims=True))
        weights = jnp.exp(scores - logsum).astype(jnp.bfloat16)
        split_values = values_clip.reshape(values_clip.shape[0], -1, HEAD)
        mixed_out = jnp.einsum(
            "hrs,she->rhe", weights, split_values, preferred_element_type=jnp.float32
        )
        return (mixed_out.reshape(query_clip.shape).astype(jnp.bfloat16), logsum)

    return lax.map(one_clip, (queries, key_rows, values))


def attend_back(queries, key_rows, values, logsum, gradient, causal):

    def one_clip(clip_block):
        query_clip, keys_clip, values_clip, logsum_clip, grad_clip = clip_block
        scores, split_query, split_keys = score_block(query_clip, keys_clip, causal)
        weights = jnp.exp(scores - logsum_clip)
        split_values = values_clip.reshape(values_clip.shape[0], -1, HEAD)
        split_grad = grad_clip.reshape(grad_clip.shape[0], -1, HEAD)
        weight_grads = jnp.einsum(
            "rhe,she->hrs", split_grad, split_values, preferred_element_type=jnp.float32
        )
        inner_sum = jnp.sum(weights * weight_grads, axis=-1, keepdims=True)
        score_grads = (weights * (weight_grads - inner_sum)).astype(jnp.bfloat16)
        score_scale = HEAD ** (-0.5)
        query_grad = (
            jnp.einsum("hrs,she->rhe", score_grads, split_keys, preferred_element_type=jnp.float32)
            * score_scale
        )
        keys_grad = (
            jnp.einsum("hrs,rhe->she", score_grads, split_query, preferred_element_type=jnp.float32)
            * score_scale
        )
        values_grad = jnp.einsum(
            "hrs,rhe->she",
            weights.astype(jnp.bfloat16),
            split_grad,
            preferred_element_type=jnp.float32,
        )
        return tuple(
            (
                piece_grad.reshape(piece_grad.shape[0], -1).astype(jnp.bfloat16)
                for piece_grad in (query_grad, keys_grad, values_grad)
            )
        )

    return lax.map(one_clip, (queries, key_rows, values, logsum, gradient))


def encoder_forward(frames, weights):
    norm_gain, norm_shift, qkv, qv_bias, proj, out_bias, fc1, fc1_bias, fc2 = weights
    normed = normalize(frames, norm_gain[0], norm_shift[0]).astype(jnp.bfloat16)
    gathered = gather_rows(normed)
    queries = (product(gathered, qkv[0, 0]) + qv_bias[0, 0]).astype(jnp.bfloat16)
    key_rows = product(gathered, qkv[0, 1]).astype(jnp.bfloat16)
    values = (product(gathered, qkv[0, 2]) + qv_bias[0, 1]).astype(jnp.bfloat16)
    mixed_out, logsum = attend(queries, key_rows, values, False)
    middle = frames + sum_rows(product(mixed_out, proj[0])) + out_bias[0]
    gathered_two = gather_rows(normalize(middle, norm_gain[1], norm_shift[1]).astype(jnp.bfloat16))
    hidden = product(gathered_two, fc1[0]) + fc1_bias[0]
    activated = activate(hidden).astype(jnp.bfloat16)
    encoded = middle + sum_rows(product(activated, fc2[0])) + out_bias[1]
    return (
        encoded,
        (
            gathered,
            queries,
            key_rows,
            values,
            mixed_out,
            logsum,
            middle,
            gathered_two,
            hidden,
            activated,
        ),
    )


def encoder_backward(frames, saved, gradient, weights):
    norm_gain, norm_shift, qkv, qv_bias, proj, out_bias, fc1, fc1_bias, fc2 = weights
    (
        gathered,
        queries,
        key_rows,
        values,
        mixed_out,
        logsum,
        middle,
        gathered_two,
        hidden,
        activated,
    ) = saved
    branch = gather_grads(gradient.astype(jnp.bfloat16))
    fc2_grad = weight_grad(activated, branch)
    bias_mlp = column_sums(branch)
    hidden_grad = (hidden.astype(jnp.float32) * product_back(branch, fc2[0])).astype(jnp.bfloat16)
    fc1_grad = weight_grad(gathered_two, hidden_grad)
    fc1_bias_grad = column_sums(hidden_grad)
    middle_norm, gain_one, shift_one = norm_back(
        middle, norm_gain[1], norm_shift[1], sum_grads(product_back(hidden_grad, fc1[0]))
    )
    middle_grad = gradient + middle_norm
    branch = gather_grads(middle_grad.astype(jnp.bfloat16))
    proj_grad = weight_grad(mixed_out, branch)
    bias_attend = column_sums(branch)
    mixed_grad = product_back(branch, proj[0]).astype(jnp.bfloat16)
    query_grad, key_grad, value_grad = attend_back(
        queries, key_rows, values, logsum, mixed_grad, False
    )
    qkv_grad = jnp.stack(
        [
            weight_grad(gathered, query_grad),
            weight_grad(gathered, key_grad),
            weight_grad(gathered, value_grad),
        ]
    )
    qv_grad = jnp.stack([column_sums(query_grad), column_sums(value_grad)])
    gathered_grad = (
        product_back(query_grad, qkv[0, 0])
        + product_back(key_grad, qkv[0, 1])
        + product_back(value_grad, qkv[0, 2])
    )
    frames_norm, gain_zero, shift_zero = norm_back(
        frames, norm_gain[0], norm_shift[0], sum_grads(gathered_grad)
    )
    frames_grad = middle_grad + frames_norm
    gradients = (
        qkv_grad,
        qv_grad,
        proj_grad,
        jnp.stack([bias_attend, bias_mlp]),
        fc1_grad,
        fc1_bias_grad,
        fc2_grad,
    )
    return (
        frames_grad,
        gradients,
        jnp.stack([gain_zero, gain_one]),
        jnp.stack([shift_zero, shift_one]),
    )


def decoder_forward(tokens, memory, valid_rows, weights, kept, logs):
    norm_gain, norm_shift, qkv, qv_bias, proj, out_bias, fc1, fc1_bias, fc2 = weights
    gathered, queries, key_rows, values, mixed_out = (kept[n][None] for n in ("m1", "sq", "sk", "sv", "sa"))
    logsum = logs(kept["sl"])
    after_self = kept["after"][None]
    gathered_two, cross_queries, cross_keys, cross_values = (kept[n][None] for n in ("m2", "cq", "ck", "cv"))
    cross_mixed, cross_logsum = attend(cross_queries, cross_keys, cross_values, False)
    second = after_self + sum_rows(product(cross_mixed, proj[2])) + out_bias[3]
    gathered_three = gather_rows(
        normalize(second, norm_gain[4], norm_shift[4]).astype(jnp.bfloat16)
    )
    hidden = product(gathered_three, fc1[1]) + fc1_bias[1]
    activated = activate(hidden).astype(jnp.bfloat16)
    after_mlp = second + sum_rows(product(activated, fc2[1])) + out_bias[4]
    saved = (
        gathered,
        queries,
        key_rows,
        values,
        mixed_out,
        logsum,
        after_self,
        gathered_two,
        cross_queries,
        cross_keys,
        cross_values,
        cross_mixed,
        cross_logsum,
        second,
        gathered_three,
        hidden,
        activated,
    )
    return (after_mlp * valid_rows, saved)


def decoder_backward(tokens, memory, saved, gradient, weights):
    norm_gain, norm_shift, qkv, qv_bias, proj, out_bias, fc1, fc1_bias, fc2 = weights
    (
        gathered,
        queries,
        key_rows,
        values,
        mixed_out,
        logsum,
        after_self,
        gathered_two,
        cross_queries,
        cross_keys,
        cross_values,
        cross_mixed,
        cross_logsum,
        second,
        gathered_three,
        hidden,
        activated,
    ) = saved
    branch = gather_grads(gradient.astype(jnp.bfloat16))
    fc2_grad = weight_grad(activated, branch)
    bias_mlp = column_sums(branch)
    hidden_grad = activate_back(hidden, product_back(branch, fc2[1])).astype(jnp.bfloat16)
    fc1_grad = weight_grad(gathered_three, hidden_grad)
    fc1_bias_grad = column_sums(hidden_grad)
    second_norm, gain_three, shift_three = norm_back(
        second, norm_gain[4], norm_shift[4], sum_grads(product_back(hidden_grad, fc1[1]))
    )
    second_grad = gradient + second_norm
    branch = gather_grads(second_grad.astype(jnp.bfloat16))
    cross_proj_grad = weight_grad(cross_mixed, branch)
    bias_cross = column_sums(branch)
    cross_mixed_grad = product_back(branch, proj[2]).astype(jnp.bfloat16)
    cross_query_grad, cross_key_grad, cross_value_grad = attend_back(
        cross_queries, cross_keys, cross_values, cross_logsum, cross_mixed_grad, False
    )
    cross_qkv_grad = jnp.stack(
        [
            weight_grad(gathered_two, cross_query_grad),
            weight_grad(memory, cross_key_grad),
            weight_grad(memory, cross_value_grad),
        ]
    )
    cross_qv_grad = jnp.stack([column_sums(cross_query_grad), column_sums(cross_value_grad)])
    memory_grad = sum_grads(
        product_back(cross_key_grad, qkv[2, 1]) + product_back(cross_value_grad, qkv[2, 2])
    )
    self_norm, gain_two, shift_two = norm_back(
        after_self,
        norm_gain[3],
        norm_shift[3],
        sum_grads(product_back(cross_query_grad, qkv[2, 0])),
    )
    self_grad = second_grad + self_norm
    branch = gather_grads(self_grad.astype(jnp.bfloat16))
    self_proj_grad = weight_grad(mixed_out, branch)
    bias_self = column_sums(branch)
    mixed_grad = product_back(branch, proj[1]).astype(jnp.bfloat16)
    query_grad, key_grad, value_grad = attend_back(
        queries, key_rows, values, logsum, mixed_grad, True
    )
    self_qkv_grad = jnp.stack(
        [
            weight_grad(gathered, query_grad),
            weight_grad(gathered, key_grad),
            weight_grad(gathered, value_grad),
        ]
    )
    self_qv_grad = jnp.stack([column_sums(query_grad), column_sums(value_grad)])
    gathered_grad = (
        product_back(query_grad, qkv[1, 0])
        + product_back(key_grad, qkv[1, 1])
        + product_back(value_grad, qkv[1, 2])
    )
    tokens_norm, gain_one, shift_one = norm_back(
        tokens, norm_gain[2], norm_shift[2], sum_grads(gathered_grad)
    )
    tokens_grad = self_grad + tokens_norm
    gradients = (
        jnp.stack([self_qkv_grad, cross_qkv_grad]),
        jnp.stack([self_qv_grad, cross_qv_grad]),
        jnp.stack([self_proj_grad, cross_proj_grad]),
        jnp.stack([bias_self, bias_cross, bias_mlp]),
        fc1_grad,
        fc1_bias_grad,
        fc2_grad,
    )
    return (
        tokens_grad,
        memory_grad,
        gradients,
        jnp.stack([gain_one, gain_two, gain_three]),
        jnp.stack([shift_one, shift_two, shift_three]),
    )


def on_device(
    enc_in,
    dec_in,
    dec_len,
    norm_gain,
    norm_shift,
    qkv,
    qv_bias,
    proj,
    out_bias,
    fc1,
    fc1_bias,
    fc2,
    enc_cot,
    dec_cot,
):
    weights = (
        norm_gain.astype(jnp.float32),
        norm_shift.astype(jnp.float32),
        qkv,
        qv_bias,
        proj,
        out_bias,
        fc1,
        fc1_bias,
        fc2,
    )
    frames = enc_in.astype(jnp.float32)
    tokens = dec_in.astype(jnp.float32)
    clip_count, token_count = (dec_in.shape[0], dec_in.shape[1])
    positions = lax.axis_index("mp") * token_count + lax.broadcasted_iota(
        jnp.int32, (clip_count, token_count), 1
    )
    valid_rows = (positions < dec_len[:, None]).astype(jnp.float32)[:, :, None]
    kept = forward_call(enc_in, dec_in, norm_gain, norm_shift, qv_bias, out_bias, fc1_bias, qkv, proj, fc1, fc2)
    enc_out = kept["enc"][None]
    memory = kept["g3"][None]
    ln2 = math.log(2.0)
    logs = lambda t: (t[:3] * ln2)[None, :, :, None]
    enc_saved = (kept["g1"][None], kept["q"][None], kept["k"][None], kept["v"][None], kept["a"][None], logs(kept["l"]),
        kept["mid"][None], kept["g2"][None], kept["gd"][None], kept["e"][None])
    decoded, dec_saved = decoder_forward(tokens, memory, valid_rows, weights, kept, logs)
    tokens_grad, memory_grad, dec_grads, dec_gains, dec_shifts = decoder_backward(
        tokens, memory, dec_saved, dec_cot.astype(jnp.float32) * valid_rows, weights
    )
    encoded_grad = enc_cot.astype(jnp.float32) + memory_grad
    frames_grad, enc_grads, enc_gains, enc_shifts = encoder_backward(
        frames, enc_saved, encoded_grad, weights
    )
    dec_wide = sum_clips((dec_grads[0], dec_grads[2], dec_grads[4], dec_grads[6]))
    enc_mlp = sum_clips((enc_grads[4], enc_grads[6]))
    enc_attend = sum_clips((enc_grads[0], enc_grads[2]))
    merged = (
        jnp.concatenate([enc_attend[0][None], dec_wide[0]]),
        jnp.concatenate([enc_grads[1][None], dec_grads[1]]),
        jnp.concatenate([enc_attend[1][None], dec_wide[1]]),
        jnp.concatenate([enc_grads[3], dec_grads[3]]),
        jnp.stack([enc_mlp[0], dec_wide[2]]),
        jnp.stack([enc_grads[5], dec_grads[5]]),
        jnp.stack([enc_mlp[1], dec_wide[3]]),
    )
    narrow = lax.psum((merged[1], merged[3], merged[5]), "dp")
    merged = (merged[0], narrow[0], merged[2], narrow[1], merged[4], narrow[2], merged[6])
    gain_grad, shift_grad = lax.psum(
        (jnp.concatenate([enc_gains, dec_gains]), jnp.concatenate([enc_shifts, dec_shifts])),
        ("dp", "mp"),
    )
    return (
        enc_out,
        decoded.astype(jnp.bfloat16),
        frames_grad,
        tokens_grad,
        gain_grad,
        shift_grad,
        merged[0],
        merged[1],
        merged[2],
        merged[3],
        merged[4],
        merged[5],
        merged[6],
    )


def solution(mesh):
    placed = (
        P("dp", "mp", None),
        P("dp", "mp", None),
        P("dp"),
        P(),
        P(),
        P(None, None, None, "mp"),
        P(None, None, "mp"),
        P(None, "mp", None),
        P(),
        P(None, None, "mp"),
        P(None, "mp"),
        P(None, "mp", None),
        P("dp", "mp", None),
        P("dp", "mp", None),
    )
    return jax.shard_map(
        on_device,
        mesh=mesh,
        in_specs=placed,
        out_specs=(
            P("dp", "mp", None),
            P("dp", "mp", None),
            P("dp", "mp", None),
            P("dp", "mp", None),
            P(),
            P(),
            P(None, None, None, "mp"),
            P(None, None, "mp"),
            P(None, "mp", None),
            P(),
            P(None, None, "mp"),
            P(None, "mp"),
            P(None, "mp", None),
        ),
        check_vma=False,
    )
```

```python
import functools
import math

import jax
import jax.numpy as jnp
from jax import lax
from jax.experimental import pallas as pl
from jax.experimental.pallas import tpu as pltpu
from jax.sharding import PartitionSpec as P

HEAD = 64
epsilon = 1e-05
masked_score = -1e30
f32 = jnp.float32
bf16 = jnp.bfloat16
NN = (((1,), (0,)), ((), ()))
NT = (((1,), (1,)), ((), ()))
TN = (((0,), (0,)), ((), ()))
SCALE = HEAD ** (-0.5)
SCORE_TO_LOG2 = SCALE * math.log2(math.e)
ANY = pl.BlockSpec(memory_space=pl.ANY)
VMEM = pl.BlockSpec(memory_space=pltpu.VMEM)


def dot(a, b, dims=NN):
    return lax.dot_general(a, b, dims, preferred_element_type=f32)


def window(start, size):
    return pl.ds(pl.multiple_of(start, 16), size)


def places():
    me = lax.axis_index("mp")
    core = lax.rem(me, 2)
    mate = me + 1 - 2 * core
    opp = lax.rem(me + 2, 4)
    diag = lax.rem(mate + 2, 4)
    return me, mate, opp, diag


def remote(src, dst, sent, landed, axis, index):
    return pltpu.make_async_remote_copy(
        src_ref=src,
        dst_ref=dst,
        send_sem=sent,
        recv_sem=landed,
        device_id={axis: index},
        device_id_type=pl.DeviceIdType.MESH,
    )


class Gather:
    def __init__(self, buf, sems, rows, step):
        self.buf, self.sems, self.rows, self.step = buf, sems, rows, step
        self.me, self.mate_id, self.opp_id, self.diag_id = places()

    def at(self, block, j):
        return window(block * self.rows + j * self.step, self.step)

    def copy(self, kind, block, j, target):
        part = self.buf.at[self.at(block, j)]
        return remote(part, part, self.sems.at[2 * kind, j], self.sems.at[2 * kind + 1, j], "mp", target)

    def send(self, j):
        self.copy(0, self.me, j, self.opp_id).start()
        self.copy(1, self.me, j, self.mate_id).start()

    def mate(self, j):
        self.copy(1, self.mate_id, j, self.mate_id).wait_recv()

    def opp(self, j):
        self.copy(0, self.opp_id, j, self.opp_id).wait_recv()
        self.copy(2, self.opp_id, j, self.mate_id).start()

    def diag(self, j):
        self.copy(2, self.diag_id, j, self.mate_id).wait_recv()

    def close(self, j):
        self.copy(0, self.me, j, self.opp_id).wait_send()
        self.copy(1, self.me, j, self.mate_id).wait_send()
        self.copy(2, self.opp_id, j, self.mate_id).wait_send()


class Scatter:
    def __init__(self, own, send, land, ysend, yland, sems, rows, step):
        self.own, self.out, self.land, self.ysend, self.yland = own, send, land, ysend, yland
        self.sems, self.rows, self.step = sems, rows, step
        self.me, self.mate_id, self.opp_id, self.diag_id = places()

    def near(self, half, j):
        part = window(half * self.rows + j * self.step, self.step)
        return remote(
            self.out.at[part], self.land.at[part],
            self.sems.at[2 * half, j], self.sems.at[2 * half + 1, j], "mp", self.mate_id,
        )

    def far(self, j):
        part = window(j * self.step, self.step)
        return remote(
            self.ysend.at[part], self.yland.at[part],
            self.sems.at[4, j], self.sems.at[5, j], "mp", self.opp_id,
        )

    def put_diag(self, j, value):
        self.out[window(j * self.step, self.step), :] = value.astype(bf16)
        self.near(0, j).start()

    def put_opp(self, j, value):
        part = window(j * self.step, self.step)
        self.near(0, j).wait_recv()
        self.ysend[part, :] = (value + self.land[part, :].astype(f32)).astype(bf16)
        self.far(j).start()

    def put_mate(self, j, value):
        self.out[window(self.rows + j * self.step, self.step), :] = value.astype(bf16)
        self.near(1, j).start()

    def put_own(self, j, value):
        self.own[window(j * self.step, self.step), :] = value

    def total(self, j):
        self.near(1, j).wait_recv()
        self.far(j).wait_recv()
        part = window(j * self.step, self.step)
        near = self.land[window(self.rows + j * self.step, self.step), :].astype(f32)
        return self.own[part, :] + near + self.yland[part, :].astype(f32)

    def close(self, j):
        self.near(0, j).wait_send()
        self.near(1, j).wait_send()
        self.far(j).wait_send()


def scatter_shapes(rows, width, steps):
    return [
        pltpu.VMEM((rows, width), f32),
        pltpu.VMEM((2 * rows, width), bf16),
        pltpu.VMEM((2 * rows, width), bf16),
        pltpu.VMEM((rows, width), bf16),
        pltpu.VMEM((rows, width), bf16),
        pltpu.SemaphoreType.DMA((6, steps)),
    ]


def meet(partners):
    barrier = pltpu.get_barrier_semaphore()
    for axis, index in partners:
        pl.semaphore_signal(barrier, inc=1, device_id={axis: index}, device_id_type=pl.DeviceIdType.MESH)
    pl.semaphore_wait(barrier, len(partners))


def layer_norm(rows_in, gain_row, shift_row):
    average = jnp.mean(rows_in, axis=-1, keepdims=True)
    centred = rows_in - average
    spread = jnp.mean(centred * centred, axis=-1, keepdims=True)
    return centred * lax.rsqrt(spread + epsilon) * gain_row + shift_row


def head_row(width, h):
    lane = lax.broadcasted_iota(jnp.int32, (1, width), 1)
    return jnp.where((lane >= h * HEAD) & (lane < (h + 1) * HEAD), 1.0, 0.0).astype(f32)


def attend_rows(q_ref, k_ref, v_ref, out_ref, log_ref, start, size, causal):
    width = q_ref.shape[1]
    part = window(start, size)
    queries = q_ref[part, :]
    keys = k_ref[...]
    values = v_ref[...]
    lane = lax.broadcasted_iota(jnp.int32, (size, log_ref.shape[1]), 1)
    mixed = jnp.zeros((size, width), f32)
    logs = jnp.zeros((size, log_ref.shape[1]), f32)
    for h in range(width // HEAD):
        picked = head_row(width, h)
        scores = dot(queries * picked.astype(bf16), keys, NT)
        if causal:
            row_index = lax.broadcasted_iota(jnp.int32, scores.shape, 0) + start
            col_index = lax.broadcasted_iota(jnp.int32, scores.shape, 1)
            scores = jnp.where(col_index <= row_index, scores, masked_score)
        highest = jnp.max(scores, axis=-1, keepdims=True)
        powers = jnp.exp2((scores - highest) * SCORE_TO_LOG2)
        total = jnp.sum(powers, axis=-1, keepdims=True)
        mixed = mixed + dot(powers.astype(bf16), values) * (picked / total)
        logs = jnp.where(lane == h, highest * SCORE_TO_LOG2 + jnp.log2(total), logs)
    out_ref[part, :] = mixed.astype(bf16)
    log_ref[part, :] = logs


def gelu_parts(hidden):
    below = 0.5 + 0.5 * lax.erf(hidden * (0.5 ** 0.5))
    density = jnp.exp2(hidden * hidden * (-0.5 * math.log2(math.e))) * ((2 * math.pi) ** (-0.5))
    return hidden * below, below + hidden * density


def forward_kernel(
    R, T,
    enc_in, dec_in, gain_ref, shift_ref, qv_bias, out_bias, fc1_bias, qkv, proj, fc1, fc2,
    o_enc, o_g1, o_q, o_k, o_v, o_a, o_l, o_mid, o_g2, o_e, o_gd, o_g3, o_ck, o_cv,
    o_m1, o_sq, o_sk, o_sv, o_sa, o_sl, o_as, o_m2, o_cq,
    w_e, w_s, w_c, w_pe, w_ps, w_f1, w_f2,
    g1, q, k, v, a, l, lt, mid, g2, e, gd, g3, ck, cv, m1, sq, sk, sv, sa, sl, slt, after, m2, cq, enc,
    *rest,
):
    rest = list(rest)
    take = lambda n: [rest.pop(0) for _ in range(n)]
    rs1, rs2, rsd = take(6), take(6), take(6)
    ag1, ag2, ag3, agd1, agd2 = take(5)
    load_sem, save_sem = take(2)
    S = T
    steps = R // S
    me, mate, opp, diag = places()
    loads = [
        pltpu.make_async_copy(src, dst, load_sem.at[i])
        for i, (src, dst) in enumerate(
            [(qkv.at[0], w_e), (qkv.at[1], w_s), (qkv.at[2], w_c), (proj.at[0], w_pe), (proj.at[1], w_ps),
             (fc1.at[0], w_f1), (fc2.at[0], w_f2)]
        )
    ]
    for load in loads:
        load.start()
    saves = []

    def save(src, dst):
        copy = pltpu.make_async_copy(src, dst, save_sem.at[len(saves)])
        copy.start()
        saves.append(copy)

    gains = gain_ref[...].astype(f32)
    shifts = shift_ref[...].astype(f32)
    branch_bias = out_bias[...].astype(f32)
    head_bias = qv_bias[...].astype(f32)
    wide_bias = fc1_bias[...].astype(f32)

    meet([("mp", mate), ("mp", opp)])

    gd1 = Gather(m1, agd1, T, S)
    m1[window(me * T, T), :] = layer_norm(dec_in[0].astype(f32), gains[2:3], shifts[2:3]).astype(bf16)
    gd1.send(0)
    ge1 = Gather(g1, ag1, R, S)

    @pl.loop(0, steps)
    def _(j):
        rows = enc_in[0, window(j * S, S), :].astype(f32)
        g1[window(me * R + j * S, S), :] = layer_norm(rows, gains[0:1], shifts[0:1]).astype(bf16)
        ge1.send(j)

    def project_block(block):
        part = window(block * R, R)
        rows = g1[part, :]
        q[part, :] = (dot(rows, w_e[0], NT) + head_bias[0, 0:1]).astype(bf16)
        k[part, :] = dot(rows, w_e[1], NT).astype(bf16)
        v[part, :] = (dot(rows, w_e[2], NT) + head_bias[0, 1:2]).astype(bf16)

    loads[0].wait()

    @pl.loop(0, steps)
    def _(j):
        ge1.mate(j)

    @pl.loop(0, 2)
    def _(i):
        project_block(me + i * (mate - me))

    gd1.mate(0)
    gd1.opp(0)
    gd1.diag(0)
    save(m1, o_m1)
    loads[1].wait()
    sq[...] = (dot(m1[...], w_s[0], NT) + head_bias[1, 0:1]).astype(bf16)
    sk[...] = dot(m1[...], w_s[1], NT).astype(bf16)
    sv[...] = (dot(m1[...], w_s[2], NT) + head_bias[1, 1:2]).astype(bf16)
    save(sq, o_sq)
    save(sk, o_sk)
    save(sv, o_sv)

    @pl.loop(0, 2)
    def _(i):
        attend_rows(sq, sk, sv, sa, sl, i * 2 * T, 2 * T, True)

    save(sa, o_sa)
    slt[...] = jnp.transpose(sl[...])[0:8]
    save(slt, o_sl)
    loads[4].wait()
    @pl.loop(0, steps)
    def _(j):
        ge1.opp(j)

    @pl.loop(0, steps)
    def _(j):
        ge1.diag(j)

    sd = Scatter(*rsd, T, S)
    sd.put_diag(0, dot(sa[window(diag * T, T), :], w_ps[...]))
    sd.put_opp(0, dot(sa[window(opp * T, T), :], w_ps[...]))
    sd.put_mate(0, dot(sa[window(mate * T, T), :], w_ps[...]))
    sd.put_own(0, dot(sa[window(me * T, T), :], w_ps[...]))

    @pl.loop(0, 2)
    def _(i):
        project_block(opp + i * (diag - opp))

    save(g1, o_g1)
    save(q, o_q)
    save(k, o_k)
    save(v, o_v)
    loads[3].wait()
    s1 = Scatter(*rs1, R, S)

    def attend_block(block, put):
        attend_rows(q, k, v, a, l, block * R, R, False)

        @pl.loop(0, steps)
        def _(j):
            put(j, dot(a[window(block * R + j * S, S), :], w_pe[...]))

    def attend_chunk(block, j):
        attend_rows(q, k, v, a, l, block * R + j * S, S, False)
        return dot(a[window(block * R + j * S, S), :], w_pe[...])

    @pl.loop(0, steps)
    def _(j):
        s1.put_diag(j, attend_chunk(diag, j))
        s1.put_opp(j, attend_chunk(opp, j))

    after[...] = dec_in[0].astype(f32) + sd.total(0) + branch_bias[2:3]
    gd2 = Gather(m2, agd2, T, S)
    m2[window(me * T, T), :] = layer_norm(after[...], gains[3:4], shifts[3:4]).astype(bf16)
    gd2.send(0)
    save(after, o_as)

    attend_block(mate, s1.put_mate)
    attend_block(me, s1.put_own)
    lt[...] = jnp.transpose(l[...])[0:8]
    save(lt, o_l)
    save(a, o_a)

    ge2 = Gather(g2, ag2, R, S)

    @pl.loop(0, steps)
    def _(j):
        part = window(j * S, S)
        rows = enc_in[0, part, :].astype(f32) + s1.total(j) + branch_bias[0:1]
        mid[part, :] = rows
        g2[window(me * R + j * S, S), :] = layer_norm(rows, gains[1:2], shifts[1:2]).astype(bf16)
        ge2.send(j)

    save(mid, o_mid)
    gd2.mate(0)
    gd2.opp(0)
    gd2.diag(0)
    loads[2].wait()
    cq[...] = (dot(m2[...], w_c[0], NT) + head_bias[2, 0:1]).astype(bf16)
    save(m2, o_m2)
    save(cq, o_cq)
    loads[5].wait()
    loads[6].wait()
    s2 = Scatter(*rs2, R, S)

    def feed(block, j):
        part = window(block * R + j * S, S)
        hidden = dot(g2[part, :], w_f1[...]) + wide_bias[0:1]
        active, slope = gelu_parts(hidden)
        active = active.astype(bf16)
        e[part, :] = active
        gd[part, :] = slope.astype(bf16)
        return dot(active, w_f2[...])

    @pl.loop(0, steps)
    def _(j):
        s2.put_own(j, feed(me, j))

    @pl.loop(0, steps)
    def _(j):
        ge2.mate(j)
        s2.put_mate(j, feed(mate, j))

    @pl.loop(0, steps)
    def _(j):
        ge2.opp(j)
        ge2.diag(j)
        s2.put_diag(j, feed(diag, j))
        s2.put_opp(j, feed(opp, j))

    save(g2, o_g2)
    save(e, o_e)
    save(gd, o_gd)
    ge3 = Gather(g3, ag3, R, S)

    @pl.loop(0, steps)
    def _(j):
        part = window(j * S, S)
        rows = (mid[part, :] + s2.total(j) + branch_bias[1:2]).astype(bf16)
        enc[part, :] = rows
        g3[window(me * R + j * S, S), :] = rows
        ge3.send(j)

    save(enc, o_enc)

    def cross_block(block):
        part = window(block * R, R)
        rows = g3[part, :]
        ck[part, :] = dot(rows, w_c[1], NT).astype(bf16)
        cv[part, :] = (dot(rows, w_c[2], NT) + head_bias[2, 1:2]).astype(bf16)

    @pl.loop(0, steps)
    def _(j):
        ge3.mate(j)

    @pl.loop(0, 2)
    def _(i):
        cross_block(me + i * (mate - me))

    @pl.loop(0, steps)
    def _(j):
        ge3.opp(j)

    @pl.loop(0, steps)
    def _(j):
        ge3.diag(j)

    @pl.loop(0, 2)
    def _(i):
        cross_block(opp + i * (diag - opp))

    save(g3, o_g3)
    save(ck, o_ck)
    save(cv, o_cv)

    @pl.loop(0, steps)
    def _(j):
        for each in (ge1, s1, ge2, s2, ge3):
            each.close(j)

    for each in (gd1, sd, gd2):
        each.close(0)
    for copy in saves:
        copy.wait()


def forward_call(enc_in, dec_in, norm_gain, norm_shift, qv_bias, out_bias, fc1_bias, qkv, proj, fc1, fc2):
    R, D = enc_in.shape[1:]
    T = dec_in.shape[1]
    W = qkv.shape[2]
    F = fc1.shape[-1]
    steps = R // T
    V = lambda *shape: pltpu.VMEM(shape, bf16)
    V32 = lambda *shape: pltpu.VMEM(shape, f32)
    B = lambda *shape: jax.ShapeDtypeStruct(shape, bf16)
    B32 = lambda *shape: jax.ShapeDtypeStruct(shape, f32)
    N, M = 4 * R, 4 * T
    outs = dict(
        enc=B(R, D), g1=B(N, D), q=B(N, W), k=B(N, W), v=B(N, W), a=B(N, W), l=B32(8, N), mid=B32(R, D),
        g2=B(N, D), e=B(N, F), gd=B(N, F), g3=B(N, D), ck=B(N, W), cv=B(N, W),
        m1=B(M, D), sq=B(M, W), sk=B(M, W), sv=B(M, W), sa=B(M, W), sl=B32(8, M), after=B32(T, D),
        m2=B(M, D), cq=B(M, W),
    )
    scratch = [
        V(3, W, D), V(3, W, D), V(3, W, D), V(W, D), V(W, D), V(D, F), V(F, D),
        V(N, D), V(N, W), V(N, W), V(N, W), V(N, W), V32(N, 128), V32(8, N), V32(R, D), V(N, D), V(N, F), V(N, F),
        V(N, D), V(N, W), V(N, W),
        V(M, D), V(M, W), V(M, W), V(M, W), V(M, W), V32(M, 128), V32(8, M), V32(T, D), V(M, D), V(M, W), V(R, D),
    ]
    scratch += scatter_shapes(R, D, steps) + scatter_shapes(R, D, steps) + scatter_shapes(T, D, 1)
    scratch += [pltpu.SemaphoreType.DMA((6, steps))] * 3 + [pltpu.SemaphoreType.DMA((6, 1))] * 2
    scratch += [pltpu.SemaphoreType.DMA((7,)), pltpu.SemaphoreType.DMA((len(outs),))]
    results = pl.pallas_call(
        functools.partial(forward_kernel, R, T),
        out_shape=list(outs.values()),
        in_specs=[VMEM] * 7 + [ANY] * 4,
        out_specs=[ANY] * len(outs),
        scratch_shapes=scratch,
        compiler_params=pltpu.CompilerParams(
            collective_id=0, has_side_effects=True, vmem_limit_bytes=60 << 20
        ),
        name="encoder_forward",
    )(enc_in, dec_in, norm_gain, norm_shift, qv_bias, out_bias, fc1_bias, qkv, proj, fc1, fc2)
    return dict(zip(outs, results))


def add_rows(ref, row, value):
    ref[row:row + 1, :] = ref[row:row + 1, :] + value


def column_sums(value):
    return jnp.sum(value, axis=0, keepdims=True)


def matrix_sums(ref):
    ones = jnp.ones((16, ref.shape[0]), bf16)
    return dot(ones, ref[...])[0:1]


def norm_back(rows_in, gain_row, gradient):
    average = jnp.mean(rows_in, axis=-1, keepdims=True)
    centred = rows_in - average
    spread = jnp.mean(centred * centred, axis=-1, keepdims=True)
    scale = lax.rsqrt(spread + epsilon)
    hat = centred * scale
    inner = gradient * gain_row
    first = jnp.mean(inner, axis=-1, keepdims=True)
    second = jnp.mean(inner * hat, axis=-1, keepdims=True)
    return (inner - first - hat * second) * scale, column_sums(gradient * hat), column_sums(gradient)


def head_sums(a_ref, g_ref):
    width = a_ref.shape[1]
    row = lax.broadcasted_iota(jnp.int32, (8, width), 0)
    lane = lax.broadcasted_iota(jnp.int32, (8, width), 1)
    picker = jnp.where((lane >= row * HEAD) & (lane < (row + 1) * HEAD), 1.0, 0.0).astype(f32)
    both = a_ref[...].astype(f32) * g_ref[...].astype(f32)
    return lax.dot_general(picker, both, NT, precision=lax.Precision.HIGHEST, preferred_element_type=f32)


def attend_back_rows(q_ref, k_ref, v_ref, ga_ref, log_ref, sum_ref, gqt_ref, gk_ref, gv_ref, start, size, causal):
    width = q_ref.shape[1]
    part = window(start, size)
    queries = q_ref[...]
    grads = ga_ref[...]
    keys = k_ref[part, :]
    values = v_ref[part, :]
    turned = jnp.transpose(keys.astype(f32)).astype(bf16)
    gk = jnp.zeros((size, width), f32)
    gv = jnp.zeros((size, width), f32)
    for h in range(width // HEAD):
        picked = head_row(width, h)
        scores = dot(keys * picked.astype(bf16), queries, NT)
        weights = jnp.exp2(scores * SCORE_TO_LOG2 - log_ref[h:h + 1, :])
        if causal:
            key_index = lax.broadcasted_iota(jnp.int32, scores.shape, 0) + start
            query_index = lax.broadcasted_iota(jnp.int32, scores.shape, 1)
            weights = jnp.where(key_index <= query_index, weights, 0.0)
        slopes = dot(values * picked.astype(bf16), grads, NT)
        score_grads = (weights * (slopes - sum_ref[h:h + 1, :])).astype(bf16)
        gk = gk + dot(score_grads, queries) * (picked * SCALE)
        gv = gv + dot(weights.astype(bf16), grads) * picked
        some = slice(h * HEAD, (h + 1) * HEAD)
        gqt_ref[some, :] = gqt_ref[some, :] + dot(turned[some, :], score_grads)
    gk_ref[part, :] = gk.astype(bf16)
    gv_ref[part, :] = gv.astype(bf16)


def start_all(pairs, sems):
    copies = [pltpu.make_async_copy(src, dst, sems.at[i]) for i, (src, dst) in enumerate(pairs)]
    for copy in copies:
        copy.start()
    return copies


X_FIRST, Z_FIRST = (0, 1, 2), (1, 0, 2)
GAIN, SHIFT, OUT_BIAS, FC1_BIAS, QV_BIAS, SMALL = 0, 5, 10, 16, 18, 32


def decoder_kernel(
    R, T, clips,
    dec_cot, dec_len, gain_ref, shift_ref, out_bias, fc1_bias, after, cl_unused,
    qkv, proj, fc1, fc2, enc_cot, i_cq, i_ck, i_cv, i_m2, i_g3,
    o_dec, o_renc, o_rself, o_fc1, o_fc2, o_cross, o_small,
    w_c, w_p, w_f1, w_f2, cq, ck, cv, m2, g3, cot,
    z3, z2, m3, ca, cl, clt, cs, second, r3, r2, dg, gu, ga, gqt, gq, gk, gv, renc, rself, dec,
    fc1_g, fc2_g, cross, small,
    *rest,
):
    rest = list(rest)
    take = lambda n: [rest.pop(0) for _ in range(n)]
    rsc, rsf, rsb, rsm, rsq = take(6), take(6), take(6), take(6), take(6)
    agz3, agm3, agz2 = take(3)
    red_fc1, red_fc2 = take(2), take(2)
    load_sem, save_sem = take(2)
    S = T
    steps = R // S
    N, M = 4 * R, 4 * T
    me, mate, opp, diag = places()
    own = window(me * T, T)
    load_c, load_p, load_f1, load_f2, load_cq, load_ck, load_cv, load_m2, load_g3, load_cot = start_all(
        [(qkv.at[2], w_c), (proj.at[2], w_p), (fc1.at[1], w_f1), (fc2.at[1], w_f2), (i_cq, cq), (i_ck, ck),
         (i_cv, cv), (i_m2, m2), (i_g3, g3), (enc_cot.at[0], cot)], load_sem,
    )
    saves = []

    def save(src, dst):
        copy = pltpu.make_async_copy(src, dst, save_sem.at[len(saves)])
        copy.start()
        saves.append(copy)

    gains = gain_ref[...].astype(f32)
    shifts = shift_ref[...].astype(f32)
    branch_bias = out_bias[...].astype(f32)
    wide_bias = fc1_bias[...].astype(f32)
    small[...] = jnp.zeros_like(small)
    gqt[...] = jnp.zeros_like(gqt)

    r_fc1 = Reduce(fc1_g, *red_fc1, None, X_FIRST, clips)
    r_fc2 = Reduce(fc2_g, *red_fc2, None, Z_FIRST, clips)
    meet([("mp", mate), ("mp", opp)] + clip_partners(clips))
    position = lax.broadcasted_iota(jnp.int32, (T, 1), 0) + me * T
    valid = jnp.where(position < dec_len[...], 1.0, 0.0).astype(f32)
    r3[...] = dec_cot[0].astype(f32) * valid
    z3[own, :] = r3[...].astype(bf16)
    gz3 = Gather(z3, agz3, T, S)
    gz3.send(0)
    add_rows(small, OUT_BIAS + 4, column_sums(z3[own, :].astype(f32)))

    load_cq.wait()
    load_ck.wait()
    load_cv.wait()

    @pl.loop(0, 2)
    def _(i):
        attend_rows(cq, ck, cv, ca, cl, i * 2 * T, 2 * T, False)

    clt[...] = jnp.transpose(cl[...])[0:8]
    load_p.wait()

    def scatter_rows(scatter, product):
        scatter.put_diag(0, product(diag))
        scatter.put_opp(0, product(opp))
        scatter.put_mate(0, product(mate))
        scatter.put_own(0, product(me))

    sc = Scatter(*rsc, T, S)
    scatter_rows(sc, lambda b: dot(ca[window(b * T, T), :], w_p[...]))
    gz3.mate(0)
    gz3.opp(0)
    gz3.diag(0)
    load_f1.wait()
    load_f2.wait()
    second[...] = after[...] + sc.total(0) + branch_bias[3:4]
    m3[own, :] = layer_norm(second[...], gains[4:5], shifts[4:5]).astype(bf16)
    gm3 = Gather(m3, agm3, T, S)
    gm3.send(0)

    sf = Scatter(*rsf, T, S)
    sb = Scatter(*rsb, T, S)

    def feed(block, put_back, put_on):
        part = window(block * T, T)
        hidden = dot(m3[part, :], w_f1[...]) + wide_bias[1:2]
        active, slope = gelu_parts(hidden)
        active = active.astype(bf16)
        dg[part, :] = active
        back = (dot(z3[part, :], w_f2[...], NT) * slope).astype(bf16)
        gu[part, :] = back
        put_back(0, dot(back, w_f1[...], NT))
        put_on(0, dot(active, w_f2[...]))

    feed(me, sb.put_own, sf.put_own)
    gm3.mate(0)
    feed(mate, sb.put_mate, sf.put_mate)
    gm3.opp(0)
    gm3.diag(0)
    feed(diag, sb.put_diag, sf.put_diag)
    feed(opp, sb.put_opp, sf.put_opp)

    fc1_g[...] = dot(m3[...], gu[...], TN).astype(bf16)
    r_fc1.begin()
    fc2_g[...] = dot(dg[...], z3[...], TN).astype(bf16)
    r_fc2.begin()
    gv_rows, gain_sum, shift_sum = norm_back(second[...], gains[4:5], sb.total(0))
    add_rows(small, GAIN + 4, gain_sum)
    add_rows(small, SHIFT + 4, shift_sum)
    r2[...] = r3[...] + gv_rows
    z2[own, :] = r2[...].astype(bf16)
    gz2 = Gather(z2, agz2, T, S)
    gz2.send(0)
    add_rows(small, OUT_BIAS + 3, column_sums(z2[own, :].astype(f32)))
    add_rows(small, FC1_BIAS + 1, matrix_sums(gu))
    gz2.mate(0)
    gz2.opp(0)
    gz2.diag(0)

    ga[...] = dot(z2[...], w_p[...], NT).astype(bf16)
    cs[...] = head_sums(ca, ga)
    load_c.wait()
    sm = Scatter(*rsm, R, S)

    def back_block(block, put):
        attend_back_rows(cq, ck, cv, ga, clt, cs, gqt, gk, gv, block * R, R, False)

        @pl.loop(0, steps)
        def _(j):
            part = window(block * R + j * S, S)
            put(j, dot(gk[part, :], w_c[1]) + dot(gv[part, :], w_c[2]))

    back_block(diag, sm.put_diag)
    back_block(opp, sm.put_opp)
    back_block(mate, sm.put_mate)
    back_block(me, sm.put_own)
    r_fc1.stage(0)
    r_fc2.stage(0)
    gq[...] = (jnp.transpose(gqt[...]) * SCALE).astype(bf16)
    sq = Scatter(*rsq, T, S)
    scatter_rows(sq, lambda b: dot(gq[window(b * T, T), :], w_c[0]))
    dec[...] = ((second[...] + sf.total(0) + branch_bias[4:5]) * valid).astype(bf16)
    save(dec, o_dec)
    load_m2.wait()
    load_g3.wait()
    cross[0:192, :] = dot(gq[...], m2[...], TN).astype(bf16)
    cross[192:384, :] = dot(gk[...], g3[...], TN).astype(bf16)
    cross[384:576, :] = dot(gv[...], g3[...], TN).astype(bf16)
    cross[576:768, :] = dot(ca[...], z2[...], TN).astype(bf16)
    small[QV_BIAS + 4:QV_BIAS + 5, 0:192] = matrix_sums(gq)
    small[QV_BIAS + 5:QV_BIAS + 6, 0:192] = matrix_sums(gv)
    r_fc1.stage(1)
    r_fc2.stage(1)
    gv_rows, gain_sum, shift_sum = norm_back(after[...], gains[3:4], sq.total(0))
    add_rows(small, GAIN + 3, gain_sum)
    add_rows(small, SHIFT + 3, shift_sum)
    rself[...] = r2[...] + gv_rows
    load_cot.wait()

    @pl.loop(0, steps)
    def _(j):
        part = window(j * S, S)
        renc[part, :] = cot[part, :].astype(f32) + sm.total(j)
        sm.close(j)

    for src, dst in ((renc, o_renc), (rself, o_rself), (cross, o_cross), (small, o_small)):
        save(src, dst)
    r_fc1.stage(2)
    r_fc2.stage(2)
    save(fc1_g, o_fc1)
    save(fc2_g, o_fc2)
    for each in (gz3, sc, gm3, sf, sb, gz2, sq):
        each.close(0)
    for copy in saves:
        copy.wait()


def decoder_call(kept, clips, dec_cot, dec_len, norm_gain, norm_shift, out_bias, fc1_bias, turned, proj, fc1, fc2, enc_cot):
    R, D = enc_cot.shape[1:]
    T = dec_cot.shape[1]
    W = turned.shape[2]
    F = fc1.shape[-1]
    steps = R // T
    V = lambda *shape: pltpu.VMEM(shape, bf16)
    V32 = lambda *shape: pltpu.VMEM(shape, f32)
    B = lambda *shape: jax.ShapeDtypeStruct(shape, bf16)
    B32 = lambda *shape: jax.ShapeDtypeStruct(shape, f32)
    N, M = 4 * R, 4 * T
    outs = dict(dec=B(T, D), renc=B32(R, D), rself=B32(T, D), fc1=B(D, F), fc2=B(F, D), cross=B(4 * W, D), small=B32(SMALL, D))
    scratch = [
        V(3, W, D), V(W, D), V(D, F), V(F, D), V(M, W), V(N, W), V(N, W), V(M, D), V(N, D), V(R, D),
        V(M, D), V(M, D), V(M, D), V(M, W), V32(M, 128), V32(8, M), V32(8, M), V32(T, D), V32(T, D), V32(T, D),
        V(M, F), V(M, F), V(M, W), V32(W, M), V(M, W), V(N, W), V(N, W), V32(R, D), V32(T, D), V(T, D),
        V(D, F), V(F, D), V(4 * W, D), V32(SMALL, D),
    ]
    for rows, count in ((T, 1), (T, 1), (T, 1), (R, steps), (T, 1)):
        scratch += scatter_shapes(rows, D, count)
    scratch += [pltpu.SemaphoreType.DMA((6, 1))] * 3
    scratch += add_shapes(D, clips) + add_shapes(F, clips)
    scratch += [pltpu.SemaphoreType.DMA((10,)), pltpu.SemaphoreType.DMA((len(outs),))]
    results = pl.pallas_call(
        functools.partial(decoder_kernel, R, T, clips),
        out_shape=list(outs.values()),
        in_specs=[VMEM, pl.BlockSpec(memory_space=pltpu.VMEM)] + [VMEM] * 6 + [ANY] * 10,
        out_specs=[ANY] * len(outs),
        scratch_shapes=scratch,
        compiler_params=pltpu.CompilerParams(
            collective_id=1, has_side_effects=True, vmem_limit_bytes=60 << 20
        ),
        name="decoder_back",
    )(
        dec_cot, dec_len.reshape(1, 1), norm_gain, norm_shift, out_bias, fc1_bias, kept["after"], kept["sl"],
        turned, proj, fc1, fc2, enc_cot, kept["cq"], kept["ck"], kept["cv"], kept["m2"], kept["g3"],
    )
    return dict(zip(outs, results))


class Reduce:
    def __init__(self, buf, land, sems, free, order, clips):
        self.buf, self.land, self.sems, self.free = buf, land, sems, free
        bits = clips.bit_length() - 1
        self.halving = min(3, bits)
        index = lax.axis_index("dp")
        start, size, offset = 0, buf.shape[0], 0
        self.steps = []
        for t, b in enumerate([b for b in order if b < self.halving] + list(range(self.halving, bits))):
            bit = lax.rem(index // (1 << b), 2)
            partner = index + (1 - 2 * bit) * (1 << b)
            if t < self.halving:
                size //= 2
                keep, give = start + bit * size, start + (1 - bit) * size
                start = keep
            else:
                keep = give = start
            self.steps.append((partner, keep, give, offset, size))
            offset += size

    def out(self, t):
        partner, keep, give, offset, size = self.steps[t]
        return remote(
            self.buf.at[window(give, size)], self.land.at[window(offset, size)],
            self.sems.at[0, t], self.sems.at[1, t], "dp", partner,
        )

    def back(self, t, start):
        partner, size = self.steps[t][0], self.steps[t][4]
        part = self.buf.at[window(start, size)]
        return remote(part, part, self.sems.at[2, t], self.sems.at[3, t], "dp", partner)

    def release(self, t):
        pl.semaphore_signal(
            self.free.at[t], inc=1, device_id={"dp": self.steps[t][0]}, device_id_type=pl.DeviceIdType.MESH
        )

    def begin(self):
        self.out(0).start()

    def resume(self):
        for t in range(self.halving):
            self.release(t)
        self.give_back(self.halving - 1)

    def give_back(self, t):
        pl.semaphore_wait(self.free.at[t], 1)
        self.back(t, self.steps[t][1]).start()

    def add(self, t):
        partner, keep, give, offset, size = self.steps[t]
        copy = self.out(t)
        copy.wait_recv()
        copy.wait_send()
        if self.free is not None and t < self.halving:
            self.release(t)
        chunk = size
        while chunk > 192:
            chunk //= 2

        @pl.loop(0, size // chunk)
        def _(i):
            part = window(keep + i * chunk, chunk)
            brought = self.land[window(offset + i * chunk, chunk), :].astype(f32)
            self.buf[part, :] = (self.buf[part, :].astype(f32) + brought).astype(bf16)

    def stage(self, i):
        if i < self.halving:
            for t in [i] if i + 1 < self.halving else range(i, len(self.steps)):
                self.add(t)
                if t + 1 < len(self.steps):
                    self.out(t + 1).start()
            if i + 1 == self.halving and self.free is not None:
                self.give_back(i)
        else:
            t = 2 * self.halving - 1 - i
            self.back(t, self.steps[t][2]).wait_recv()
            self.back(t, self.steps[t][1]).wait_send()
            if t > 0:
                self.give_back(t - 1)


def bit_count(clips):
    return clips.bit_length() - 1


def land_rows(rows, clips):
    return rows - rows // 8 + (rows // 8) * max(0, bit_count(clips) - 3)


def add_shapes(rows, clips):
    return [pltpu.VMEM((land_rows(rows, clips), 768), bf16), pltpu.SemaphoreType.DMA((2, bit_count(clips)))]


def back_shapes(clips):
    return [pltpu.SemaphoreType.DMA((4, bit_count(clips))), pltpu.SemaphoreType.REGULAR((3,))]


def reduce_shapes(rows, clips):
    return [pltpu.VMEM((land_rows(rows, clips), 768), bf16)] + back_shapes(clips)


def clip_partners(clips):
    index = lax.axis_index("dp")
    partners = []
    for b in range(bit_count(clips)):
        bit = lax.rem(index // (1 << b), 2)
        partners.append(("dp", index + (1 - 2 * bit) * (1 << b)))
    return partners


class Small:
    def __init__(self, buf, land, sems, clips, shared):
        self.buf, self.land, self.sems, self.shared = buf, land, sems, shared
        me, mate, opp, diag = places()
        self.partners = [("mp", mate), ("mp", opp)] + clip_partners(clips)

    def copy(self, t):
        axis, index = self.partners[t]
        rows = pl.ds(0, self.shared if axis == "mp" else self.buf.shape[1])
        return remote(
            self.buf.at[t, rows], self.land.at[t, rows], self.sems.at[0, t], self.sems.at[1, t], axis, index
        )

    def start(self, t):
        self.copy(t).start()

    def finish(self, t):
        self.copy(t).wait()
        rows = self.shared if self.partners[t][0] == "mp" else self.buf.shape[1]
        self.buf[t + 1] = self.buf[t]
        self.buf[t + 1, 0:rows, :] = self.buf[t, 0:rows, :] + self.land[t, 0:rows, :]
        if t + 1 < len(self.partners):
            self.start(t + 1)


def encoder_kernel(
    R, T, clips,
    gain_ref, enc_in, dec_in, small_in,
    qkv, proj, fc1, fc2, i_renc, i_rself, i_fc1, i_fc2, i_cross,
    i_g1, i_q, i_k, i_v, i_a, i_l, i_mid, i_g2, i_e, i_gd, i_m1, i_sq, i_sk, i_sv, i_sa, i_sl,
    o_enc, o_dec, o_qkv, o_proj, o_fc1, o_fc2, o_small,
    w_e, w_s, w_pe, w_ps, w_f1, w_f2, renc, rself, fc1_g, fc2_g, cross, g1, q, k, v, a, l, mid, g2, e, gd, m1, sq, sk, sv, sa, sl,
    z1, z2, zs, self_b, e1a, e1b, e2a, e2b, ga, gq, gk, gv, gqt, ss, sga, sgq, sgk, sgv, sgqt, cs, rmid, sums,
    *rest,
):
    rest = list(rest)
    take = lambda n: [rest.pop(0) for _ in range(n)]
    rs1, rs2, rsd = take(6), take(6), take(6)
    ag1, ag2, ags = take(3)
    red_fc1, red_fc2 = take(2), take(2)
    red_cross, red_self, red_e1a, red_e1b, red_e2a, red_e2b = [take(3) for _ in range(6)]
    small_land, small_sem = take(2)
    load_sem, save_sem = take(2)
    S = T
    steps = R // S
    me, mate, opp, diag = places()
    pairs = dict(
        renc=(i_renc, renc), rself=(i_rself, rself), f2=(fc2.at[0], w_f2), f1=(fc1.at[0], w_f1), gd=(i_gd, gd),
        fc1=(i_fc1, fc1_g), fc2=(i_fc2, fc2_g), cross=(i_cross, cross), s=(qkv.at[1], w_s), ps=(proj.at[1], w_ps),
        m1=(i_m1, m1), sq=(i_sq, sq), sk=(i_sk, sk), sv=(i_sv, sv), sa=(i_sa, sa), sl=(i_sl, sl),
        e=(i_e, e), g2=(i_g2, g2), mid=(i_mid, mid), pe=(proj.at[0], w_pe), q=(i_q, q), k=(i_k, k), v=(i_v, v),
        a=(i_a, a), l=(i_l, l), e_w=(qkv.at[0], w_e), g1=(i_g1, g1),
    )
    loads = dict(zip(pairs, start_all(list(pairs.values()), load_sem)))

    def need(*names):
        for name in names:
            loads[name].wait()

    saves = []

    def save(src, dst):
        copy = pltpu.make_async_copy(src, dst, save_sem.at[len(saves)])
        copy.start()
        saves.append(copy)

    gains = gain_ref[...].astype(f32)
    sums[0] = small_in[...]
    small = sums.at[0]
    gqt[...] = jnp.zeros_like(gqt)
    sgqt[...] = jnp.zeros_like(sgqt)
    d1a = Reduce(fc1_g, None, *red_fc1, X_FIRST, clips)
    d1b = Reduce(fc2_g, None, *red_fc2, Z_FIRST, clips)
    rc = Reduce(cross, *red_cross, X_FIRST, clips)
    rs = Reduce(self_b, *red_self, X_FIRST, clips)
    re1a = Reduce(e1a, *red_e1a, X_FIRST, clips)
    re1b = Reduce(e1b, *red_e1b, Z_FIRST, clips)
    re2a = Reduce(e2a, *red_e2a, Z_FIRST, clips)
    re2b = Reduce(e2b, *red_e2b, X_FIRST, clips)
    total = Small(sums, small_land, small_sem, clips, 16)
    meet(total.partners)

    need("renc")
    gz1 = Gather(z1, ag1, R, S)

    @pl.loop(0, steps)
    def _(j):
        rows = renc[window(j * S, S), :].astype(bf16)
        z1[window(me * R + j * S, S), :] = rows
        gz1.send(j)

    need("rself")
    zs[window(me * T, T), :] = rself[...].astype(bf16)
    gzs = Gather(zs, ags, T, S)
    gzs.send(0)
    need("cross", "fc1", "fc2")
    rc.begin()
    d1a.resume()
    d1b.resume()

    need("f2", "f1", "gd")
    s1 = Scatter(*rs1, R, S)

    def feed(block, j):
        part = window(block * R + j * S, S)
        back = (dot(z1[part, :], w_f2[...], NT) * gd[part, :].astype(f32)).astype(bf16)
        gd[part, :] = back
        return dot(back, w_f1[...], NT)

    @pl.loop(0, steps)
    def _(j):
        s1.put_own(j, feed(me, j))

    @pl.loop(0, steps)
    def _(j):
        gz1.mate(j)
        s1.put_mate(j, feed(mate, j))

    @pl.loop(0, steps)
    def _(j):
        gz1.opp(j)
        gz1.diag(j)
        s1.put_diag(j, feed(diag, j))
        s1.put_opp(j, feed(opp, j))

    d1a.stage(3)
    d1b.stage(3)
    rc.stage(0)

    gzs.mate(0)
    gzs.opp(0)
    gzs.diag(0)
    need("s", "ps", "m1", "sq", "sk", "sv", "sa", "sl")
    sga[...] = dot(zs[...], w_ps[...], NT).astype(bf16)
    ss[...] = head_sums(sa, sga)

    @pl.loop(0, 2)
    def _(i):
        attend_back_rows(sq, sk, sv, sga, sl, ss, sgqt, sgk, sgv, i * 2 * T, 2 * T, True)

    sgq[...] = (jnp.transpose(sgqt[...]) * SCALE).astype(bf16)
    sd = Scatter(*rsd, T, S)

    def self_rows(block):
        part = window(block * T, T)
        return dot(sgq[part, :], w_s[0]) + dot(sgk[part, :], w_s[1]) + dot(sgv[part, :], w_s[2])

    sd.put_diag(0, self_rows(diag))
    sd.put_opp(0, self_rows(opp))
    sd.put_mate(0, self_rows(mate))
    sd.put_own(0, self_rows(me))
    d1a.stage(4)
    self_b[0:192, :] = dot(sgq[...], m1[...], TN).astype(bf16)
    self_b[192:384, :] = dot(sgk[...], m1[...], TN).astype(bf16)
    self_b[384:576, :] = dot(sgv[...], m1[...], TN).astype(bf16)
    self_b[576:768, :] = dot(sa[...], zs[...], TN).astype(bf16)
    rs.begin()
    d1b.stage(4)
    rc.stage(1)

    need("e", "g2", "mid")
    gz2 = Gather(z2, ag2, R, S)
    for row, value in (
        (OUT_BIAS + 2, column_sums(zs[window(me * T, T), :].astype(f32))),
        (OUT_BIAS + 1, column_sums(z1[window(me * R, R), :].astype(f32))),
    ):
        add_rows(small, row, value)

    @pl.loop(0, steps)
    def _(j):
        part = window(j * S, S)
        rows, gain_sum, shift_sum = norm_back(mid[part, :], gains[1:2], s1.total(j))
        add_rows(small, GAIN + 1, gain_sum)
        add_rows(small, SHIFT + 1, shift_sum)
        rows = renc[part, :] + rows
        rmid[part, :] = rows
        z2[window(me * R + j * S, S), :] = rows.astype(bf16)
        gz2.send(j)

    e1a[...] = dot(g2[...], gd[...], TN).astype(bf16)
    re1a.begin()
    e1b[...] = dot(e[...], z1[...], TN).astype(bf16)
    re1b.begin()
    add_rows(small, FC1_BIAS, matrix_sums(gd))
    small[QV_BIAS + 2:QV_BIAS + 3, 0:192] = matrix_sums(sgq)
    small[QV_BIAS + 3:QV_BIAS + 4, 0:192] = matrix_sums(sgv)
    rows, gain_sum, shift_sum = norm_back(dec_in[0].astype(f32), gains[2:3], sd.total(0))
    add_rows(small, GAIN + 2, gain_sum)
    add_rows(small, SHIFT + 2, shift_sum)
    rself[...] = rself[...] + rows
    save(rself, o_dec)
    d1a.stage(5)
    save(fc1_g, o_fc1.at[1])
    d1b.stage(5)
    save(fc2_g, o_fc2.at[1])

    need("pe", "q", "k", "v", "a", "l", "e_w", "g1")

    def mixed_back(block):
        part = window(block * R, R)
        ga[part, :] = dot(z2[part, :], w_pe[...], NT).astype(bf16)

    mixed_back(me)

    @pl.loop(0, steps)
    def _(j):
        gz2.mate(j)

    mixed_back(mate)

    @pl.loop(0, steps)
    def _(j):
        gz2.opp(j)

    @pl.loop(0, steps)
    def _(j):
        gz2.diag(j)

    @pl.loop(0, 2)
    def _(i):
        mixed_back(opp + i * (diag - opp))

    cs[...] = head_sums(a, ga)
    for i in range(4):
        attend_back_rows(q, k, v, ga, l, cs, gqt, gk, gv, i * R, R, False)
        if i == 0:
            rc.stage(2)
        if i == 1:
            rs.stage(0)
        if i == 2:
            re1b.stage(0)
        if i == 3:
            rc.stage(3)
            re1a.stage(0)

    gq[...] = (jnp.transpose(gqt[...]) * SCALE).astype(bf16)
    s2 = Scatter(*rs2, R, S)

    def attend_rows_back(block, put):
        @pl.loop(0, steps)
        def _(j):
            part = window(block * R + j * S, S)
            put(j, dot(gq[part, :], w_e[0]) + dot(gk[part, :], w_e[1]) + dot(gv[part, :], w_e[2]))

    attend_rows_back(diag, s2.put_diag)
    attend_rows_back(opp, s2.put_opp)
    attend_rows_back(mate, s2.put_mate)
    attend_rows_back(me, s2.put_own)
    rs.stage(1)
    e2a[0:192, :] = dot(gq[...], g1[...], TN).astype(bf16)
    e2a[192:384, :] = dot(gk[...], g1[...], TN).astype(bf16)
    re2a.begin()
    re1b.stage(1)
    e2b[0:192, :] = dot(gv[...], g1[...], TN).astype(bf16)
    e2b[192:384, :] = dot(a[...], z2[...], TN).astype(bf16)
    re2b.begin()
    rc.stage(4)
    small[QV_BIAS:QV_BIAS + 1, 0:192] = matrix_sums(gq)
    small[QV_BIAS + 1:QV_BIAS + 2, 0:192] = matrix_sums(gv)
    add_rows(small, OUT_BIAS, column_sums(z2[window(me * R, R), :].astype(f32)))

    @pl.loop(0, steps)
    def _(j):
        part = window(j * S, S)
        rows, gain_sum, shift_sum = norm_back(enc_in[0, part, :].astype(f32), gains[0:1], s2.total(j))
        add_rows(small, GAIN, gain_sum)
        add_rows(small, SHIFT, shift_sum)
        rmid[part, :] = rmid[part, :] + rows

    save(rmid, o_enc)
    total.start(0)
    re1a.stage(1)
    re2b.stage(0)
    total.finish(0)
    rs.stage(2)
    re2a.stage(0)
    total.finish(1)
    re1b.stage(2)
    rc.stage(5)
    save(cross.at[0:576], o_qkv.at[2])
    save(cross.at[576:768], o_proj.at[2])
    re1a.stage(2)
    total.finish(2)
    re2a.stage(1)
    re2b.stage(1)
    for t in range(3, len(total.partners)):
        total.finish(t)
        if t == 3:
            rs.stage(3)
    save(sums.at[len(total.partners)], o_small)
    re1b.stage(3)
    re1a.stage(3)
    re2a.stage(2)
    re1b.stage(4)
    re2b.stage(2)
    rs.stage(4)
    re1a.stage(4)
    re2a.stage(3)
    rs.stage(5)
    save(self_b.at[0:576], o_qkv.at[1])
    save(self_b.at[576:768], o_proj.at[1])
    re1b.stage(5)
    save(e1b, o_fc2.at[0])
    re2b.stage(3)
    re1a.stage(5)
    save(e1a, o_fc1.at[0])
    re2b.stage(4)
    re2a.stage(4)
    re2b.stage(5)
    save(e2b.at[0:192], o_qkv.at[0, 384:576])
    save(e2b.at[192:384], o_proj.at[0])
    re2a.stage(5)
    save(e2a, o_qkv.at[0, 0:384])

    @pl.loop(0, steps)
    def _(j):
        for each in (gz1, s1, gz2, s2):
            each.close(j)

    for each in (gzs, sd):
        each.close(0)
    for copy in saves:
        copy.wait()


def encoder_call(kept, back, clips, norm_gain, enc_in, dec_in, turned, proj, fc1, fc2):
    R, D = enc_in.shape[1:]
    T = dec_in.shape[1]
    W = turned.shape[2]
    F = fc1.shape[-1]
    steps = R // T
    V = lambda *shape: pltpu.VMEM(shape, bf16)
    V32 = lambda *shape: pltpu.VMEM(shape, f32)
    B = lambda *shape: jax.ShapeDtypeStruct(shape, bf16)
    B32 = lambda *shape: jax.ShapeDtypeStruct(shape, f32)
    N, M = 4 * R, 4 * T
    partners = 2 + clips.bit_length() - 1
    outs = dict(
        enc=B32(R, D), dec=B32(T, D), qkv=B(3, 3 * W, D), proj=B(3, W, D), fc1=B(2, D, F), fc2=B(2, F, D),
        small=B32(SMALL, D),
    )
    scratch = [
        V(3, W, D), V(3, W, D), V(W, D), V(W, D), V(D, F), V(F, D), V32(R, D), V32(T, D), V(D, F), V(F, D), V(4 * W, D),
        V(N, D), V(N, W), V(N, W), V(N, W), V(N, W), V32(8, N), V32(R, D), V(N, D), V(N, F), V(N, F),
        V(M, D), V(M, W), V(M, W), V(M, W), V(M, W), V32(8, M),
        V(N, D), V(N, D), V(M, D), V(4 * W, D), V(D, F), V(F, D), V(2 * W, D), V(2 * W, D), V(N, W), V(N, W), V(N, W), V(N, W),
        V32(W, N), V32(8, M), V(M, W), V(M, W), V(M, W), V(M, W), V32(W, M), V32(8, N), V32(R, D),
        V32(partners + 1, SMALL, D),
    ]
    for rows, count in ((R, steps), (R, steps), (T, 1)):
        scratch += scatter_shapes(rows, D, count)
    scratch += [pltpu.SemaphoreType.DMA((6, steps))] * 2 + [pltpu.SemaphoreType.DMA((6, 1))]
    scratch += back_shapes(clips) + back_shapes(clips)
    for rows in (4 * W, 4 * W, D, F, 2 * W, 2 * W):
        scratch += reduce_shapes(rows, clips)
    scratch += [pltpu.VMEM((partners, SMALL, D), f32), pltpu.SemaphoreType.DMA((2, partners))]
    scratch += [pltpu.SemaphoreType.DMA((27,)), pltpu.SemaphoreType.DMA((16,))]
    names = ("g1", "q", "k", "v", "a", "l", "mid", "g2", "e", "gd", "m1", "sq", "sk", "sv", "sa", "sl")
    results = pl.pallas_call(
        functools.partial(encoder_kernel, R, T, clips),
        out_shape=list(outs.values()),
        in_specs=[VMEM] * 4 + [ANY] * 25,
        out_specs=[ANY] * len(outs),
        scratch_shapes=scratch,
        compiler_params=pltpu.CompilerParams(
            collective_id=2, has_side_effects=True, vmem_limit_bytes=63 << 20
        ),
        name="encoder_back",
    )(
        norm_gain, enc_in, dec_in, back["small"], turned, proj, fc1, fc2, back["renc"], back["rself"], back["fc1"],
        back["fc2"], back["cross"], *[kept[name] for name in names],
    )
    return dict(zip(outs, results))


def finish_kernel(
    i_enc, i_dec, i_encg, i_decg, small, i_qkv, i_proj, i_fc1, i_fc2,
    o_enc, o_dec, o_encg, o_decg, o_gain, o_shift, o_qkv, o_qvb, o_proj, o_bias, o_fc1, o_fc1b, o_fc2,
    narrow, wide, r_enc, r_dec, r_encg, r_decg, row_sem, in_sem, out_sem,
):
    chunk = narrow.shape[1]
    parts = []
    for src, dst in ((i_qkv, o_qkv), (i_proj, o_proj), (i_fc1, o_fc1), (i_fc2, o_fc2)):
        for i in range(src.shape[0]):
            for start in range(0, src.shape[1], chunk):
                parts.append((src.at[i, pl.ds(start, chunk)], dst.at[i, pl.ds(start, chunk)]))
    loads = [pltpu.make_async_copy(src, narrow.at[n], in_sem.at[n]) for n, (src, _) in enumerate(parts)]
    stores = [pltpu.make_async_copy(wide.at[n], dst, out_sem.at[n]) for n, (_, dst) in enumerate(parts)]
    pairs = ((i_enc, r_enc, o_enc), (i_dec, r_dec, o_dec), (i_encg, r_encg, o_encg), (i_decg, r_decg, o_decg))
    moves = [pltpu.make_async_copy(src, held, row_sem.at[0, n]) for n, (src, held, _) in enumerate(pairs)]
    passes = [pltpu.make_async_copy(held, dst.at[0], row_sem.at[1, n]) for n, (_, held, dst) in enumerate(pairs)]
    for copy in loads + moves:
        copy.start()
    o_gain[...] = small[GAIN:GAIN + 5, :]
    o_shift[...] = small[SHIFT:SHIFT + 5, :]
    o_bias[...] = small[OUT_BIAS:OUT_BIAS + 5, :]
    o_fc1b[...] = small[FC1_BIAS:FC1_BIAS + 2, :]
    for i in range(3):
        o_qvb[i] = small[QV_BIAS + 2 * i:QV_BIAS + 2 * i + 2, 0:o_qvb.shape[2]]
    for n, (load, store) in enumerate(zip(loads, stores)):
        load.wait()
        wide[n] = narrow[n].astype(f32)
        store.start()
    for move, copy in zip(moves, passes):
        move.wait()
        copy.start()
    for copy in passes + stores:
        copy.wait()


def finish_call(kept, back, last, W):
    R, D = last["enc"].shape
    T = last["dec"].shape[0]
    F = last["fc1"].shape[2]
    chunk = W
    count = sum(last[name].shape[0] * last[name].shape[1] // chunk for name in ("qkv", "proj", "fc1", "fc2"))
    B32 = lambda *shape: jax.ShapeDtypeStruct(shape, f32)
    shapes = [
        jax.ShapeDtypeStruct((1, R, D), bf16), jax.ShapeDtypeStruct((1, T, D), bf16), B32(1, R, D), B32(1, T, D),
        B32(5, D), B32(5, D), B32(3, 3 * W, D), B32(3, 2, W), B32(3, W, D), B32(5, D), B32(2, D, F), B32(2, F), B32(2, F, D),
    ]
    whole = [ANY, ANY, ANY, ANY, VMEM, VMEM, ANY, VMEM, ANY, VMEM, ANY, VMEM, ANY]
    return pl.pallas_call(
        finish_kernel,
        out_shape=shapes,
        in_specs=[ANY] * 4 + [VMEM] + [ANY] * 4,
        out_specs=whole,
        scratch_shapes=[
            pltpu.VMEM((count, chunk, D), bf16), pltpu.VMEM((count, chunk, D), f32),
            pltpu.VMEM((R, D), bf16), pltpu.VMEM((T, D), bf16), pltpu.VMEM((R, D), f32), pltpu.VMEM((T, D), f32),
            pltpu.SemaphoreType.DMA((2, 4)), pltpu.SemaphoreType.DMA((count,)), pltpu.SemaphoreType.DMA((count,)),
        ],
        compiler_params=pltpu.CompilerParams(vmem_limit_bytes=60 << 20),
        name="finish",
    )(
        kept["enc"], back["dec"], last["enc"], last["dec"], last["small"],
        last["qkv"], last["proj"], last["fc1"], last["fc2"],
    )


def on_device(
    clips,
    enc_in, dec_in, dec_len, norm_gain, norm_shift, qkv, qv_bias, proj, out_bias, fc1, fc1_bias, fc2, enc_cot, dec_cot,
):
    turned = jnp.swapaxes(qkv, 2, 3)
    kept = forward_call(
        enc_in, dec_in, norm_gain, norm_shift, qv_bias, out_bias, fc1_bias, turned, proj, fc1, fc2
    )
    back = decoder_call(
        kept, clips, dec_cot, dec_len, norm_gain, norm_shift, out_bias, fc1_bias, turned, proj, fc1, fc2, enc_cot
    )
    last = encoder_call(kept, back, clips, norm_gain, enc_in, dec_in, turned, proj, fc1, fc2)
    W, D = turned.shape[2:]
    outs = list(finish_call(kept, back, last, W))
    outs[6] = jnp.swapaxes(outs[6].reshape(3, 3, W, D), 2, 3)
    return tuple(outs)


def solution(mesh):
    rows = P("dp", "mp", None)
    columns = P(None, None, None, "mp")
    return jax.shard_map(
        functools.partial(on_device, mesh.shape["dp"]),
        mesh=mesh,
        in_specs=(
            rows, rows, P("dp"), P(), P(), columns, P(None, None, "mp"), P(None, "mp", None), P(),
            P(None, None, "mp"), P(None, "mp"), P(None, "mp", None), rows, rows,
        ),
        out_specs=(
            rows, rows, rows, rows, P(), P(), columns, P(None, None, "mp"), P(None, "mp", None), P(),
            P(None, None, "mp"), P(None, "mp"), P(None, "mp", None),
        ),
        check_vma=False,
    )
```

```python
import functools
import math

import jax
import jax.numpy as jnp
from jax import lax
from jax.experimental import pallas as pl
from jax.experimental.pallas import tpu as pltpu
from jax.sharding import PartitionSpec as P

HEAD = 64
epsilon = 1e-05
masked_score = -1e30
f32 = jnp.float32
bf16 = jnp.bfloat16
NN = (((1,), (0,)), ((), ()))
NT = (((1,), (1,)), ((), ()))
TN = (((0,), (0,)), ((), ()))
SCALE = HEAD ** (-0.5)
SCORE_TO_LOG2 = SCALE * math.log2(math.e)
ANY = pl.BlockSpec(memory_space=pl.ANY)
VMEM = pl.BlockSpec(memory_space=pltpu.VMEM)


def dot(a, b, dims=NN):
    return lax.dot_general(a, b, dims, preferred_element_type=f32)


def window(start, size):
    return pl.ds(pl.multiple_of(start, 16), size)


def places():
    me = lax.axis_index("mp")
    core = lax.rem(me, 2)
    mate = me + 1 - 2 * core
    opp = lax.rem(me + 2, 4)
    diag = lax.rem(mate + 2, 4)
    return me, mate, opp, diag


def remote(src, dst, sent, landed, axis, index):
    return pltpu.make_async_remote_copy(
        src_ref=src,
        dst_ref=dst,
        send_sem=sent,
        recv_sem=landed,
        device_id={axis: index},
        device_id_type=pl.DeviceIdType.MESH,
    )


class Gather:
    def __init__(self, buf, sems, rows, step):
        self.buf, self.sems, self.rows, self.step = buf, sems, rows, step
        self.me, self.mate_id, self.opp_id, self.diag_id = places()

    def at(self, block, j):
        return window(block * self.rows + j * self.step, self.step)

    def copy(self, kind, block, j, target):
        part = self.buf.at[self.at(block, j)]
        return remote(part, part, self.sems.at[2 * kind, j], self.sems.at[2 * kind + 1, j], "mp", target)

    def send(self, j):
        self.copy(0, self.me, j, self.opp_id).start()
        self.copy(1, self.me, j, self.mate_id).start()

    def mate(self, j):
        self.copy(1, self.mate_id, j, self.mate_id).wait_recv()

    def opp(self, j):
        self.copy(0, self.opp_id, j, self.opp_id).wait_recv()
        self.copy(2, self.opp_id, j, self.mate_id).start()

    def diag(self, j):
        self.copy(2, self.diag_id, j, self.mate_id).wait_recv()

    def close(self, j):
        self.copy(0, self.me, j, self.opp_id).wait_send()
        self.copy(1, self.me, j, self.mate_id).wait_send()
        self.copy(2, self.opp_id, j, self.mate_id).wait_send()


class Scatter:
    def __init__(self, own, send, land, ysend, yland, sems, rows, step):
        self.own, self.out, self.land, self.ysend, self.yland = own, send, land, ysend, yland
        self.sems, self.rows, self.step = sems, rows, step
        self.me, self.mate_id, self.opp_id, self.diag_id = places()

    def near(self, half, j):
        part = window(half * self.rows + j * self.step, self.step)
        return remote(
            self.out.at[part], self.land.at[part],
            self.sems.at[2 * half, j], self.sems.at[2 * half + 1, j], "mp", self.mate_id,
        )

    def far(self, j):
        part = window(j * self.step, self.step)
        return remote(
            self.ysend.at[part], self.yland.at[part],
            self.sems.at[4, j], self.sems.at[5, j], "mp", self.opp_id,
        )

    def put_diag(self, j, value):
        self.out[window(j * self.step, self.step), :] = value.astype(bf16)
        self.near(0, j).start()

    def put_opp(self, j, value):
        part = window(j * self.step, self.step)
        self.near(0, j).wait_recv()
        self.ysend[part, :] = (value + self.land[part, :].astype(f32)).astype(bf16)
        self.far(j).start()

    def put_mate(self, j, value):
        self.out[window(self.rows + j * self.step, self.step), :] = value.astype(bf16)
        self.near(1, j).start()

    def put_own(self, j, value):
        self.own[window(j * self.step, self.step), :] = value

    def total(self, j):
        self.near(1, j).wait_recv()
        self.far(j).wait_recv()
        part = window(j * self.step, self.step)
        near = self.land[window(self.rows + j * self.step, self.step), :].astype(f32)
        return self.own[part, :] + near + self.yland[part, :].astype(f32)

    def close(self, j):
        self.near(0, j).wait_send()
        self.near(1, j).wait_send()
        self.far(j).wait_send()


def scatter_shapes(rows, width, steps):
    return [
        pltpu.VMEM((rows, width), f32),
        pltpu.VMEM((2 * rows, width), bf16),
        pltpu.VMEM((2 * rows, width), bf16),
        pltpu.VMEM((rows, width), bf16),
        pltpu.VMEM((rows, width), bf16),
        pltpu.SemaphoreType.DMA((6, steps)),
    ]


def meet(partners):
    barrier = pltpu.get_barrier_semaphore()
    for axis, index in partners:
        pl.semaphore_signal(barrier, inc=1, device_id={axis: index}, device_id_type=pl.DeviceIdType.MESH)
    pl.semaphore_wait(barrier, len(partners))


def layer_norm(rows_in, gain_row, shift_row):
    average = jnp.mean(rows_in, axis=-1, keepdims=True)
    centred = rows_in - average
    spread = jnp.mean(centred * centred, axis=-1, keepdims=True)
    return centred * lax.rsqrt(spread + epsilon) * gain_row + shift_row


def head_row(width, h):
    lane = lax.broadcasted_iota(jnp.int32, (1, width), 1)
    return jnp.where((lane >= h * HEAD) & (lane < (h + 1) * HEAD), 1.0, 0.0).astype(f32)


def attend_rows(q_ref, k_ref, v_ref, out_ref, log_ref, start, size, causal):
    width = q_ref.shape[1]
    part = window(start, size)
    queries = q_ref[part, :]
    keys = k_ref[...]
    values = v_ref[...]
    lane = lax.broadcasted_iota(jnp.int32, (size, log_ref.shape[1]), 1)
    mixed = jnp.zeros((size, width), f32)
    logs = jnp.zeros((size, log_ref.shape[1]), f32)
    for h in range(width // HEAD):
        picked = head_row(width, h)
        scores = dot(queries * picked.astype(bf16), keys, NT)
        if causal:
            row_index = lax.broadcasted_iota(jnp.int32, scores.shape, 0) + start
            col_index = lax.broadcasted_iota(jnp.int32, scores.shape, 1)
            scores = jnp.where(col_index <= row_index, scores, masked_score)
        highest = jnp.max(scores, axis=-1, keepdims=True)
        powers = jnp.exp2((scores - highest) * SCORE_TO_LOG2)
        total = jnp.sum(powers, axis=-1, keepdims=True)
        mixed = mixed + dot(powers.astype(bf16), values) * (picked / total)
        logs = jnp.where(lane == h, highest * SCORE_TO_LOG2 + jnp.log2(total), logs)
    out_ref[part, :] = mixed.astype(bf16)
    log_ref[part, :] = logs


def gelu_parts(hidden):
    below = 0.5 + 0.5 * lax.erf(hidden * (0.5 ** 0.5))
    density = jnp.exp2(hidden * hidden * (-0.5 * math.log2(math.e))) * ((2 * math.pi) ** (-0.5))
    return hidden * below, below + hidden * density


def add_rows(ref, row, value):
    ref[row:row + 1, :] = ref[row:row + 1, :] + value


def column_sums(value):
    return jnp.sum(value, axis=0, keepdims=True)


def matrix_sums(ref):
    ones = jnp.ones((16, ref.shape[0]), bf16)
    return dot(ones, ref[...])[0:1]


def norm_back(rows_in, gain_row, gradient):
    average = jnp.mean(rows_in, axis=-1, keepdims=True)
    centred = rows_in - average
    spread = jnp.mean(centred * centred, axis=-1, keepdims=True)
    scale = lax.rsqrt(spread + epsilon)
    hat = centred * scale
    inner = gradient * gain_row
    first = jnp.mean(inner, axis=-1, keepdims=True)
    second = jnp.mean(inner * hat, axis=-1, keepdims=True)
    return (inner - first - hat * second) * scale, column_sums(gradient * hat), column_sums(gradient)


def head_sums(a_ref, g_ref):
    width = a_ref.shape[1]
    row = lax.broadcasted_iota(jnp.int32, (8, width), 0)
    lane = lax.broadcasted_iota(jnp.int32, (8, width), 1)
    picker = jnp.where((lane >= row * HEAD) & (lane < (row + 1) * HEAD), 1.0, 0.0).astype(f32)
    both = a_ref[...].astype(f32) * g_ref[...].astype(f32)
    return lax.dot_general(picker, both, NT, precision=lax.Precision.HIGHEST, preferred_element_type=f32)


def attend_back_rows(q_ref, k_ref, v_ref, ga_ref, log_ref, sum_ref, gqt_ref, gk_ref, gv_ref, start, size, causal):
    width = q_ref.shape[1]
    part = window(start, size)
    queries = q_ref[...]
    grads = ga_ref[...]
    keys = k_ref[part, :]
    values = v_ref[part, :]
    turned = jnp.transpose(keys.astype(f32)).astype(bf16)
    gk = jnp.zeros((size, width), f32)
    gv = jnp.zeros((size, width), f32)
    for h in range(width // HEAD):
        picked = head_row(width, h)
        scores = dot(keys * picked.astype(bf16), queries, NT)
        weights = jnp.exp2(scores * SCORE_TO_LOG2 - log_ref[h:h + 1, :])
        if causal:
            key_index = lax.broadcasted_iota(jnp.int32, scores.shape, 0) + start
            query_index = lax.broadcasted_iota(jnp.int32, scores.shape, 1)
            weights = jnp.where(key_index <= query_index, weights, 0.0)
        slopes = dot(values * picked.astype(bf16), grads, NT)
        score_grads = (weights * (slopes - sum_ref[h:h + 1, :])).astype(bf16)
        gk = gk + dot(score_grads, queries) * (picked * SCALE)
        gv = gv + dot(weights.astype(bf16), grads) * picked
        some = slice(h * HEAD, (h + 1) * HEAD)
        gqt_ref[some, :] = gqt_ref[some, :] + dot(turned[some, :], score_grads)
    gk_ref[part, :] = gk.astype(bf16)
    gv_ref[part, :] = gv.astype(bf16)


class Reduce:
    def __init__(self, buf, land, sems, free, order, clips):
        self.buf, self.land, self.sems, self.free = buf, land, sems, free
        bits = bit_count(clips)
        self.halving = min(3, bits)
        index = lax.axis_index("dp")
        start, size, offset = 0, buf.shape[0], 0
        self.steps = []
        for t, b in enumerate([b for b in order if b < self.halving] + list(range(self.halving, bits))):
            bit = lax.rem(index // (1 << b), 2)
            partner = index + (1 - 2 * bit) * (1 << b)
            if t < self.halving:
                size //= 2
                keep, give = start + bit * size, start + (1 - bit) * size
                start = keep
            else:
                keep = give = start
                offset = 0
            self.steps.append((partner, keep, give, offset, size))
            offset += size

    def out(self, t):
        partner, keep, give, offset, size = self.steps[t]
        return remote(
            self.buf.at[window(give, size)], self.land.at[window(offset, size)],
            self.sems.at[0, t], self.sems.at[1, t], "dp", partner,
        )

    def back(self, t, start):
        partner, size = self.steps[t][0], self.steps[t][4]
        part = self.buf.at[window(start, size)]
        return remote(part, part, self.sems.at[2, t], self.sems.at[3, t], "dp", partner)

    def start(self, i):
        if i < self.halving:
            self.out(i).start()
        else:
            t = 2 * self.halving - 1 - i
            pl.semaphore_wait(self.free.at[t], 1)
            self.back(t, self.steps[t][1]).start()

    def release(self, t):
        pl.semaphore_signal(
            self.free.at[t], inc=1, device_id={"dp": self.steps[t][0]}, device_id_type=pl.DeviceIdType.MESH
        )

    def add(self, t):
        partner, keep, give, offset, size = self.steps[t]
        copy = self.out(t)
        copy.wait_recv()
        copy.wait_send()
        if t < self.halving:
            self.release(t)
        chunk = size
        while chunk > 192:
            chunk //= 2

        @pl.loop(0, size // chunk)
        def _(i):
            part = window(keep + i * chunk, chunk)
            brought = self.land[window(offset + i * chunk, chunk), :].astype(f32)
            self.buf[part, :] = (self.buf[part, :].astype(f32) + brought).astype(bf16)

    def finish(self, i):
        if i < self.halving:
            self.add(i)
            if i + 1 == self.halving:
                for t in range(self.halving, len(self.steps)):
                    self.release(t)
                    pl.semaphore_wait(self.free.at[t], 1)
                    self.out(t).start()
                    self.add(t)
        else:
            t = 2 * self.halving - 1 - i
            self.back(t, self.steps[t][2]).wait_recv()
            self.back(t, self.steps[t][1]).wait_send()


def bit_count(clips):
    return clips.bit_length() - 1


def land_rows(rows, clips):
    return rows - (rows >> min(3, bit_count(clips)))


def clip_partners(clips):
    index = lax.axis_index("dp")
    partners = []
    for b in range(bit_count(clips)):
        bit = lax.rem(index // (1 << b), 2)
        partners.append(("dp", index + (1 - 2 * bit) * (1 << b)))
    return partners


class Small:
    def __init__(self, buf, land, sems, clips, shared):
        self.buf, self.land, self.sems, self.shared = buf, land, sems, shared
        me, mate, opp, diag = places()
        self.partners = [("mp", mate), ("mp", opp)] + clip_partners(clips)

    def copy(self, t):
        axis, index = self.partners[t]
        rows = pl.ds(0, self.shared if axis == "mp" else self.buf.shape[0])
        return remote(
            self.buf.at[rows], self.land.at[t, rows], self.sems.at[0, t], self.sems.at[1, t], axis, index
        )

    def start(self, t):
        self.copy(t).start()

    def finish(self, t):
        self.copy(t).wait()
        rows = self.shared if self.partners[t][0] == "mp" else self.buf.shape[0]
        self.buf[0:rows, :] = self.buf[0:rows, :] + self.land[t, 0:rows, :]
        if t == 4:
            for later in range(5, len(self.partners)):
                self.start(later)
                self.finish(later)


class Refs:
    def __init__(self, names, refs):
        self.__dict__.update(zip(names, refs, strict=True))


def forward_kernel(R, T, names, *refs):
    r = Refs(names, refs)
    S = T
    steps = R // S
    me, mate, opp, diag = places()
    sources = dict(
        w_e=r.qkv.at[0], w_s=r.qkv.at[1], w_c=r.qkv.at[2], w_pe=r.proj.at[0], w_ps=r.proj.at[1], w_pc=r.proj.at[2],
        w_f1=r.fc1.at[0], w_f2=r.fc2.at[0],
    )
    loads = {
        name: pltpu.make_async_copy(src, getattr(r, name), r.load_sem.at[i])
        for i, (name, src) in enumerate(sources.items())
    }
    for load in loads.values():
        load.start()
    saves = []

    def save(*kept):
        for name in kept:
            copy = pltpu.make_async_copy(getattr(r, name), getattr(r, "o_" + name), r.save_sem.at[len(saves)])
            copy.start()
            saves.append(copy)

    gains = r.gain[...].astype(f32)
    shifts = r.shift[...].astype(f32)
    branch_bias = r.out_bias[...].astype(f32)
    head_bias = r.qv_bias[...].astype(f32)
    wide_bias = r.fc1_bias[...].astype(f32)
    own = window(me * T, T)

    meet([("mp", mate), ("mp", opp)])

    gd1 = Gather(r.m1, r.agd1, T, S)
    r.m1[own, :] = layer_norm(r.dec_in[0].astype(f32), gains[2:3], shifts[2:3]).astype(bf16)
    gd1.send(0)
    ge1 = Gather(r.g1, r.ag1, R, S)

    @pl.loop(0, steps)
    def _(j):
        rows = r.enc_in[0, window(j * S, S), :].astype(f32)
        r.g1[window(me * R + j * S, S), :] = layer_norm(rows, gains[0:1], shifts[0:1]).astype(bf16)
        ge1.send(j)

    def project_block(block):
        part = window(block * R, R)
        rows = r.g1[part, :]
        r.q[part, :] = (dot(rows, r.w_e[0], NT) + head_bias[0, 0:1]).astype(bf16)
        r.k[part, :] = dot(rows, r.w_e[1], NT).astype(bf16)
        r.v[part, :] = (dot(rows, r.w_e[2], NT) + head_bias[0, 1:2]).astype(bf16)

    loads["w_e"].wait()

    @pl.loop(0, steps)
    def _(j):
        ge1.mate(j)

    @pl.loop(0, 2)
    def _(i):
        project_block(me + i * (mate - me))

    gd1.mate(0)
    gd1.opp(0)
    gd1.diag(0)
    save("m1")
    loads["w_s"].wait()
    r.sq[...] = (dot(r.m1[...], r.w_s[0], NT) + head_bias[1, 0:1]).astype(bf16)
    r.sk[...] = dot(r.m1[...], r.w_s[1], NT).astype(bf16)
    r.sv[...] = (dot(r.m1[...], r.w_s[2], NT) + head_bias[1, 1:2]).astype(bf16)
    save("sq", "sk", "sv")

    @pl.loop(0, 2)
    def _(i):
        attend_rows(r.sq, r.sk, r.sv, r.sa, r.slc, i * 2 * T, 2 * T, True)

    save("sa")
    r.sl[...] = jnp.transpose(r.slc[...])[0:8]
    save("sl")
    loads["w_ps"].wait()

    @pl.loop(0, steps)
    def _(j):
        ge1.opp(j)

    sd = Scatter(*r.rsd, T, S)
    sd.put_diag(0, dot(r.sa[window(diag * T, T), :], r.w_ps[...]))
    sd.put_opp(0, dot(r.sa[window(opp * T, T), :], r.w_ps[...]))
    sd.put_mate(0, dot(r.sa[window(mate * T, T), :], r.w_ps[...]))
    sd.put_own(0, dot(r.sa[own, :], r.w_ps[...]))

    @pl.loop(0, steps)
    def _(j):
        ge1.diag(j)

    @pl.loop(0, 2)
    def _(i):
        project_block(opp + i * (diag - opp))

    save("g1", "q", "k", "v")
    loads["w_pe"].wait()
    s1 = Scatter(*r.rs1, R, S)

    def attend_chunk(block, j):
        attend_rows(r.q, r.k, r.v, r.a, r.lc, block * R + j * S, S, False)
        return dot(r.a[window(block * R + j * S, S), :], r.w_pe[...])

    def attend_block(block, put):
        attend_rows(r.q, r.k, r.v, r.a, r.lc, block * R, R, False)

        @pl.loop(0, steps)
        def _(j):
            put(j, dot(r.a[window(block * R + j * S, S), :], r.w_pe[...]))

    @pl.loop(0, steps)
    def _(j):
        s1.put_diag(j, attend_chunk(diag, j))
        s1.put_opp(j, attend_chunk(opp, j))

    attend_block(mate, s1.put_mate)
    r.after[...] = r.dec_in[0].astype(f32) + sd.total(0) + branch_bias[2:3]
    gd2 = Gather(r.m2, r.agd2, T, S)
    r.m2[own, :] = layer_norm(r.after[...], gains[3:4], shifts[3:4]).astype(bf16)
    gd2.send(0)
    save("after")
    attend_block(me, s1.put_own)

    ge2 = Gather(r.g2, r.ag2, R, S)

    @pl.loop(0, steps)
    def _(j):
        part = window(j * S, S)
        rows = r.enc_in[0, part, :].astype(f32) + s1.total(j) + branch_bias[0:1]
        r.mid[part, :] = rows
        r.g2[window(me * R + j * S, S), :] = layer_norm(rows, gains[1:2], shifts[1:2]).astype(bf16)
        ge2.send(j)

    r.l[...] = jnp.transpose(r.lc[...])[0:8]
    save("mid", "l", "a")
    loads["w_f1"].wait()
    loads["w_f2"].wait()
    s2 = Scatter(*r.rs2, R, S)

    def feed(block, j):
        part = window(block * R + j * S, S)
        hidden = dot(r.g2[part, :], r.w_f1[...]) + wide_bias[0:1]
        active, slope = gelu_parts(hidden)
        active = active.astype(bf16)
        r.e[part, :] = active
        r.gd[part, :] = slope.astype(bf16)
        return dot(active, r.w_f2[...])

    @pl.loop(0, steps)
    def _(j):
        s2.put_own(j, feed(me, j))

    @pl.loop(0, steps)
    def _(j):
        ge2.mate(j)
        s2.put_mate(j, feed(mate, j))

    @pl.loop(0, steps)
    def _(j):
        ge2.opp(j)
        ge2.diag(j)
        s2.put_diag(j, feed(diag, j))
        s2.put_opp(j, feed(opp, j))

    save("g2", "e", "gd")
    gd2.mate(0)
    gd2.opp(0)
    gd2.diag(0)
    loads["w_c"].wait()
    r.cq[...] = (dot(r.m2[...], r.w_c[0], NT) + head_bias[2, 0:1]).astype(bf16)
    save("m2", "cq")
    ge3 = Gather(r.g3, r.ag3, R, S)

    @pl.loop(0, steps)
    def _(j):
        part = window(j * S, S)
        rows = (r.mid[part, :] + s2.total(j) + branch_bias[1:2]).astype(bf16)
        r.enc[part, :] = rows
        r.g3[window(me * R + j * S, S), :] = rows
        ge3.send(j)

    save("enc")
    position = lax.broadcasted_iota(jnp.int32, (T, 1), 0) + me * T
    valid = jnp.where(position < r.dec_len[...], 1.0, 0.0).astype(f32)
    r.r3[...] = r.dec_cot[0].astype(f32) * valid
    r.z3[own, :] = r.r3[...].astype(bf16)
    gz3 = Gather(r.z3, r.agz3, T, S)
    gz3.send(0)
    save("r3")

    def cross_block(block):
        part = window(block * R, R)
        rows = r.g3[part, :]
        r.ck[part, :] = dot(rows, r.w_c[1], NT).astype(bf16)
        r.cv[part, :] = (dot(rows, r.w_c[2], NT) + head_bias[2, 1:2]).astype(bf16)

    @pl.loop(0, steps)
    def _(j):
        ge3.mate(j)

    @pl.loop(0, 2)
    def _(i):
        cross_block(me + i * (mate - me))

    @pl.loop(0, steps)
    def _(j):
        ge3.opp(j)

    gz3.mate(0)
    gz3.opp(0)

    @pl.loop(0, steps)
    def _(j):
        ge3.diag(j)

    @pl.loop(0, 2)
    def _(i):
        cross_block(opp + i * (diag - opp))

    save("g3", "ck", "cv")

    loads["w_pc"].wait()
    sc = Scatter(*r.rsc, T, S)

    def cross_rows(block):
        attend_rows(r.cq, r.ck, r.cv, r.ca, r.clc, block * T, T, False)
        return dot(r.ca[window(block * T, T), :], r.w_pc[...])

    sc.put_diag(0, cross_rows(diag))
    sc.put_opp(0, cross_rows(opp))
    sc.put_mate(0, cross_rows(mate))
    sc.put_own(0, cross_rows(me))
    r.cl[...] = jnp.transpose(r.clc[...])[0:8]
    gz3.diag(0)
    save("ca", "cl", "z3")
    r.second[...] = r.after[...] + sc.total(0) + branch_bias[3:4]
    save("second")

    @pl.loop(0, steps)
    def _(j):
        for each in (ge1, s1, ge2, s2, ge3):
            each.close(j)

    for each in (gd1, sd, gd2, gz3, sc):
        each.close(0)
    for copy in saves:
        copy.wait()


def call_kernel(kernel, name, collective_id, operands, vmem_names, outs, scratch, vmem_limit, remote_ops=True):
    names = list(operands) + ["o_" + key for key in outs]
    flat, groups = [], []
    for key, spec in scratch.items():
        group = spec if isinstance(spec, list) else [spec]
        groups.append((key, len(group), isinstance(spec, list)))
        flat += group

    def body(*refs):
        head, tail = list(refs[:len(names)]), list(refs[len(names):])
        all_names, all_refs = list(names), head
        for key, count, is_list in groups:
            part, tail = tail[:count], tail[count:]
            all_names.append(key)
            all_refs.append(part if is_list else part[0])
        kernel(all_names, *all_refs)

    results = pl.pallas_call(
        body,
        out_shape=list(outs.values()),
        in_specs=[VMEM if key in vmem_names else ANY for key in operands],
        out_specs=[ANY] * len(outs),
        scratch_shapes=flat,
        compiler_params=pltpu.CompilerParams(
            collective_id=collective_id, has_side_effects=True, vmem_limit_bytes=vmem_limit
        ),
        name=name,
    )(*operands.values())
    return dict(zip(outs, results))


def V(*shape):
    return pltpu.VMEM(shape, bf16)


def V32(*shape):
    return pltpu.VMEM(shape, f32)


def B(*shape):
    return jax.ShapeDtypeStruct(shape, bf16)


def B32(*shape):
    return jax.ShapeDtypeStruct(shape, f32)


def dma(*shape):
    return pltpu.SemaphoreType.DMA(shape)


def forward_call(operands, R, T, D, W, F):
    steps = R // T
    N, M = 4 * R, 4 * T
    outs = dict(
        enc=B(R, D), g1=B(N, D), q=B(N, W), k=B(N, W), v=B(N, W), a=B(N, W), l=B32(8, N), mid=B32(R, D),
        g2=B(N, D), e=B(N, F), gd=B(N, F), g3=B(N, D), ck=B(N, W), cv=B(N, W),
        m1=B(M, D), sq=B(M, W), sk=B(M, W), sv=B(M, W), sa=B(M, W), sl=B32(8, M), after=B32(T, D),
        m2=B(M, D), cq=B(M, W), ca=B(M, W), cl=B32(8, M), z3=B(M, D), r3=B32(T, D), second=B32(T, D),
    )
    scratch = {key: pltpu.VMEM(shape.shape, shape.dtype) for key, shape in outs.items()}
    scratch |= dict(
        w_e=V(3, W, D), w_s=V(3, W, D), w_c=V(3, W, D), w_pe=V(W, D), w_ps=V(W, D), w_pc=V(W, D),
        w_f1=V(D, F), w_f2=V(F, D), lc=V32(N, 128), slc=V32(M, 128), clc=V32(M, 128),
        rs1=scatter_shapes(R, D, steps), rs2=scatter_shapes(R, D, steps), rsd=scatter_shapes(T, D, 1),
        rsc=scatter_shapes(T, D, 1), ag1=dma(6, steps), ag2=dma(6, steps), ag3=dma(6, steps),
        agd1=dma(6, 1), agd2=dma(6, 1), agz3=dma(6, 1), load_sem=dma(8), save_sem=dma(len(outs)),
    )
    kept_in_hbm = ("qkv", "proj", "fc1", "fc2")
    return call_kernel(
        functools.partial(forward_kernel, R, T), "forward", 0, operands,
        [key for key in operands if key not in kept_in_hbm], outs, scratch, 60 << 20,
    )


SCHEDULE = (
    0, 1, 2, 3, 4, 6, 5, "b+0", "a+0", 7, 8, 9, "a-0", "a+1", "b-0", "b+1", 11, 12, 13, "a-1", "a+2", 17, "b-1", 14,
    "c+0", 18, "b+2", 10, 19, 20, "a-2", "a+3", 21, 16, 22, "b-2", "c-0", "b+3", "c+1", 23, 24, "a-3", "b-3", "b+4",
    25, "a+4", 26, "c-1", 33, 29, 30, "b-4", "b+5", 28, "c+2", "a-4", "s+0", 32, 31, "c-2", 15, "f+0", 35, 36, 37,
    "a+5", 27, 38, "e+0", 39, "s-0", 40, "c+3", "s+1", 41, 42, 43, 34, "c-3", "c+4", 47, 46, "h+0", "g+0", "s-1",
    "s+2", "f-0", "e-0", "e+1", "f+1", 44, "s-2", "c-4", "s+3", "s-3", "s+4", "b-5", "e-1", "e+2", 45, "c+5", 49,
    "f-1", 48, "f+2", "e-2", 50, "g-0", "h-0", 51, "h+1", "e+3", "m+0", "m-0", "s-4", "s+5", "f-2", "a-5", "f+3",
    "g+1", "m+1", "m-1", "h-1", "h+2", "e-3", "e+4", "m+2", "g-1", "f-3", "m-2", "g+2", "f+4", "g-2", "g+3", "h-2",
    "m+3", "e-4", "e+5", "f-4", "h+3", "g-3", 52, "g+4", "h-3", "m-3", "h+4", "f+5", "g-4", "s-5", "m+4", "g+5",
    "c-5", "h-4", "h+5", "m-4", "g-5", "f-5", "h-5", "e-5",
)


GAIN, SHIFT, OUT_BIAS, FC1_BIAS, QV_BIAS, SMALL = 0, 5, 10, 16, 18, 24
X_FIRST, Z_FIRST = (0, 1, 2), (1, 0, 2)


def backward_kernel(R, T, clips, names, *refs):
    r = Refs(names, refs)
    S = T
    steps = R // S
    me, mate, opp, diag = places()
    own = window(me * T, T)
    sources = dict(
        second=r.i_second, d_f1=r.fc1.at[1], d_f2=r.fc2.at[1], z3=r.i_z3, r3=r.i_r3, w_pc=r.proj.at[2], ca=r.i_ca,
        cl=r.i_cl, cq=r.i_cq, ck=r.i_ck, cv=r.i_cv, w_c=r.qkv.at[2], g3=r.i_g3, after=r.i_after,
        cot=r.enc_cot.at[0], w_f1=r.fc1.at[0], w_f2=r.fc2.at[0], gd=r.i_gd, w_s=r.qkv.at[1], w_ps=r.proj.at[1],
        sq=r.i_sq, sk=r.i_sk, sv=r.i_sv, sa=r.i_sa, sl=r.i_sl, e=r.i_e, g2=r.i_g2, mid=r.i_mid,
        w_pe=r.proj.at[0], q=r.i_q, a=r.i_a, l=r.i_l, w_e=r.qkv.at[0],
    )
    late = dict(m2=(r.i_m2, r.gu), m1=(r.i_m1, r.dg), g1=(r.i_g1, r.g3), k=(r.i_k, r.ck), v=(r.i_v, r.cv))
    late["frames"] = (r.enc_in.at[0], r.cot)
    loads = {
        name: pltpu.make_async_copy(src, getattr(r, name), r.load_sem.at[i])
        for i, (name, src) in enumerate(sources.items())
    }
    for load in loads.values():
        load.start()
    for i, (name, (src, dst)) in enumerate(late.items()):
        loads[name] = pltpu.make_async_copy(src, dst, r.late_sem.at[i])

    def fetch(*wanted):
        for name in wanted:
            loads[name].start()

    def need(*wanted):
        for name in wanted:
            loads[name].wait()

    saves = []

    def save(src, dst):
        copy = pltpu.make_async_copy(src, dst, r.save_sem.at[len(saves)])
        copy.start()
        saves.append(copy)

    gains = r.gain[...].astype(f32)
    shifts = r.shift[...].astype(f32)
    branch_bias = r.out_bias[...].astype(f32)
    wide_bias = r.fc1_bias[...].astype(f32)
    small = r.sums
    small[...] = jnp.zeros_like(small)
    r.cgqt[...] = jnp.zeros_like(r.cgqt)
    r.sgqt[...] = jnp.zeros_like(r.sgqt)
    r.gqt[...] = jnp.zeros_like(r.gqt)
    position = lax.broadcasted_iota(jnp.int32, (T, 1), 0) + me * T
    valid = jnp.where(position < r.dec_len[...], 1.0, 0.0).astype(f32)

    buckets = dict(
        a=Reduce(r.d1a, r.land_a, *r.red_a, X_FIRST, clips), b=Reduce(r.d1b, r.land_b, *r.red_b, Z_FIRST, clips),
        c=Reduce(r.cross, r.land_c, *r.red_c, X_FIRST, clips), s=Reduce(r.self, r.land_s, *r.red_s, X_FIRST, clips),
        e=Reduce(r.e1a, r.land_a, *r.red_e, X_FIRST, clips), f=Reduce(r.e1b, r.land_b, *r.red_f, Z_FIRST, clips),
        g=Reduce(r.e2a, r.land_g, *r.red_g, X_FIRST, clips), h=Reduce(r.e2b, r.land_h, *r.red_h, Z_FIRST, clips),
        m=Small(r.sums, r.small_land, r.small_sem, clips, 16),
    )
    gm3, gz2 = Gather(r.m3, r.agm3, T, S), Gather(r.dz2, r.agz2, T, S)
    gzs, gz1, gze = Gather(r.zs, r.ags, T, S), Gather(r.z1, r.agz1, R, S), Gather(r.z2, r.agze, R, S)
    sb, sf = Scatter(*r.near_a, r.sem_b, T, S), Scatter(*r.near_b, r.sem_f, T, S)
    sq, sd = Scatter(*r.near_c, r.sem_q, T, S), Scatter(*r.near_a, r.sem_d, T, S)
    sm, s1, s2 = [Scatter(*r.wide, sem, R, S) for sem in (r.sem_m, r.sem_1, r.sem_2)]

    def norm_sums(i, gain_sum, shift_sum):
        add_rows(small, GAIN + i, gain_sum)
        add_rows(small, SHIFT + i, shift_sum)

    pieces = []

    def each_step(work):
        for j in range(steps):
            pieces.append(functools.partial(work, j))

    def begin():
        meet(buckets["m"].partners)
        need("second")
        r.m3[own, :] = layer_norm(r.second[...], gains[4:5], shifts[4:5]).astype(bf16)
        gm3.send(0)
        need("d_f1", "d_f2", "z3")

    pieces.append(begin)

    def feed_decoder(block, put_back):
        part = window(block * T, T)
        hidden = dot(r.m3[part, :], r.d_f1[...]) + wide_bias[1:2]
        active, slope = gelu_parts(hidden)
        active = active.astype(bf16)
        r.dg[part, :] = active
        back = (dot(r.z3[part, :], r.d_f2[...], NT) * slope).astype(bf16)
        r.gu[part, :] = back
        put_back(0, dot(back, r.d_f1[...], NT))

    def feed_own():
        feed_decoder(me, sb.put_own)
        gm3.mate(0)

    def feed_mate():
        feed_decoder(mate, sb.put_mate)

    def feed_diag():
        gm3.opp(0)
        gm3.diag(0)
        feed_decoder(diag, sb.put_diag)

    def feed_opp():
        feed_decoder(opp, sb.put_opp)

    def decoder_fc1():
        r.d1a[...] = dot(r.m3[...], r.gu[...], TN).astype(bf16)

    def decoder_fc2():
        r.d1b[...] = dot(r.dg[...], r.z3[...], TN).astype(bf16)

    pieces += [feed_own, feed_mate, feed_diag, feed_opp, decoder_fc1, decoder_fc2]

    def cross_residual():
        need("r3")
        rows, gain_sum, shift_sum = norm_back(r.second[...], gains[4:5], sb.total(0))
        norm_sums(4, gain_sum, shift_sum)
        r.r3[...] = r.r3[...] + rows
        r.dz2[own, :] = r.r3[...].astype(bf16)
        gz2.send(0)
        add_rows(small, OUT_BIAS + 4, column_sums(r.z3[own, :].astype(f32)))
        add_rows(small, OUT_BIAS + 3, column_sums(r.dz2[own, :].astype(f32)))
        add_rows(small, FC1_BIAS + 1, matrix_sums(r.gu))
        need("w_pc", "ca", "cl", "cq", "ck", "cv", "w_c")

    def cross_mixed():
        gz2.mate(0)
        gz2.opp(0)
        gz2.diag(0)
        r.cga[...] = dot(r.dz2[...], r.w_pc[...], NT).astype(bf16)
        r.cs[...] = head_sums(r.ca, r.cga)

    def cross_keys(start, size):
        attend_back_rows(r.cq, r.ck, r.cv, r.cga, r.cl, r.cs, r.cgqt, r.gk, r.gv, start, size, False)

    def memory_rows(block, j):
        part = window(block * R + j * S, S)
        return dot(r.gk[part, :], r.w_c[1]) + dot(r.gv[part, :], r.w_c[2])

    def cross_far():
        @pl.loop(0, steps)
        def _(j):
            cross_keys(diag * R + j * S, S)
            sm.put_diag(j, memory_rows(diag, j))
            cross_keys(opp * R + j * S, S)
            sm.put_opp(j, memory_rows(opp, j))

    def forward_rows():
        for block, put in ((diag, sf.put_diag), (opp, sf.put_opp), (mate, sf.put_mate), (me, sf.put_own)):
            put(0, dot(r.dg[window(block * T, T), :], r.d_f2[...]))

    def cross_near(block, put):
        cross_keys(block * R, R)

        @pl.loop(0, steps)
        def _(j):
            put(j, memory_rows(block, j))

    def cross_queries():
        r.cgq[...] = (jnp.transpose(r.cgqt[...]) * SCALE).astype(bf16)
        for block, put in ((diag, sq.put_diag), (opp, sq.put_opp), (mate, sq.put_mate), (me, sq.put_own)):
            put(0, dot(r.cgq[window(block * T, T), :], r.w_c[0]))
        fetch("m2")
        need("g3", "cot")

    def cross_weights():
        need("m2")
        r.cross[0:192, :] = dot(r.cgq[...], r.gu[...], TN).astype(bf16)
        r.cross[192:384, :] = dot(r.gk[...], r.g3[...], TN).astype(bf16)
        r.cross[384:576, :] = dot(r.gv[...], r.g3[...], TN).astype(bf16)
        r.cross[576:768, :] = dot(r.ca[...], r.dz2[...], TN).astype(bf16)
        small[QV_BIAS + 4:QV_BIAS + 5, 0:192] = matrix_sums(r.cgq)
        small[QV_BIAS + 5:QV_BIAS + 6, 0:192] = matrix_sums(r.gv)

    def decoder_out():
        r.dec[...] = ((r.second[...] + sf.total(0) + branch_bias[4:5]) * valid).astype(bf16)
        save(r.dec, r.o_dec)

    def self_residual():
        need("after")
        rows, gain_sum, shift_sum = norm_back(r.after[...], gains[3:4], sq.total(0))
        norm_sums(3, gain_sum, shift_sum)
        r.r3[...] = r.r3[...] + rows
        r.zs[own, :] = r.r3[...].astype(bf16)
        gzs.send(0)
        add_rows(small, OUT_BIAS + 2, column_sums(r.zs[own, :].astype(f32)))
        sb.close(0)

    pieces += [
        cross_residual, cross_mixed, cross_far, forward_rows, lambda: cross_near(mate, sm.put_mate),
        lambda: cross_near(me, sm.put_own), cross_queries, cross_weights, decoder_out, self_residual,
    ]

    def encoder_residual(j):
        part = window(j * S, S)
        rows = r.cot[part, :].astype(f32) + sm.total(j)
        sm.close(j)
        r.renc[part, :] = rows
        r.z1[window(me * R + j * S, S), :] = rows.astype(bf16)
        gz1.send(j)

    each_step(encoder_residual)

    def feed(block, j):
        part = window(block * R + j * S, S)
        back = (dot(r.z1[part, :], r.w_f2[...], NT) * r.gd[part, :].astype(f32)).astype(bf16)
        r.gd[part, :] = back
        return dot(back, r.w_f1[...], NT)

    def encoder_feed_own():
        need("w_f1", "w_f2", "gd", "e", "g2", "mid")
        fetch("k", "v", "frames")

        @pl.loop(0, steps)
        def _(j):
            s1.put_own(j, feed(me, j))

    def encoder_feed_mate():
        @pl.loop(0, steps)
        def _(j):
            gz1.mate(j)
            s1.put_mate(j, feed(mate, j))

    def encoder_feed_far(j):
        gz1.opp(j)
        gz1.diag(j)
        s1.put_diag(j, feed(diag, j))
        s1.put_opp(j, feed(opp, j))

    pieces += [encoder_feed_own, encoder_feed_mate]
    each_step(encoder_feed_far)

    def self_mixed():
        gzs.mate(0)
        gzs.opp(0)
        gzs.diag(0)
        fetch("m1")
        need("w_s", "w_ps", "sq", "sk", "sv", "sa", "sl")
        r.sga[...] = dot(r.zs[...], r.w_ps[...], NT).astype(bf16)
        r.cs[...] = head_sums(r.sa, r.sga)

    def self_back():
        @pl.loop(0, 2)
        def _(i):
            attend_back_rows(
                r.sq, r.sk, r.sv, r.sga, r.sl, r.cs, r.sgqt, r.sgk, r.sgv, i * 2 * T, 2 * T, True
            )

        r.sgq[...] = (jnp.transpose(r.sgqt[...]) * SCALE).astype(bf16)

    def self_rows():
        for block, put in ((diag, sd.put_diag), (opp, sd.put_opp), (mate, sd.put_mate), (me, sd.put_own)):
            part = window(block * T, T)
            put(0, dot(r.sgq[part, :], r.w_s[0]) + dot(r.sgk[part, :], r.w_s[1]) + dot(r.sgv[part, :], r.w_s[2]))

    def self_weights():
        need("m1")
        r.self[0:192, :] = dot(r.sgq[...], r.dg[...], TN).astype(bf16)
        r.self[192:384, :] = dot(r.sgk[...], r.dg[...], TN).astype(bf16)
        r.self[384:576, :] = dot(r.sgv[...], r.dg[...], TN).astype(bf16)
        r.self[576:768, :] = dot(r.sa[...], r.zs[...], TN).astype(bf16)

    pieces += [self_mixed, self_back, self_rows, self_weights]

    def middle_residual(j):
        part = window(j * S, S)
        rows, gain_sum, shift_sum = norm_back(r.mid[part, :], gains[1:2], s1.total(j))
        norm_sums(1, gain_sum, shift_sum)
        s1.close(j)
        rows = r.renc[part, :] + rows
        r.mid[part, :] = rows
        r.z2[window(me * R + j * S, S), :] = rows.astype(bf16)
        gze.send(j)

    each_step(middle_residual)

    def encoder_fc1():
        r.e1a[...] = dot(r.g2[...], r.gd[...], TN).astype(bf16)

    def encoder_fc2():
        r.e1b[...] = dot(r.e[...], r.z1[...], TN).astype(bf16)

    def decoder_rows():
        add_rows(small, FC1_BIAS, matrix_sums(r.gd))
        add_rows(small, OUT_BIAS + 1, column_sums(r.z1[window(me * R, R), :].astype(f32)))
        small[QV_BIAS + 2:QV_BIAS + 3, 0:192] = matrix_sums(r.sgq)
        small[QV_BIAS + 3:QV_BIAS + 4, 0:192] = matrix_sums(r.sgv)
        rows, gain_sum, shift_sum = norm_back(r.dec_in[0].astype(f32), gains[2:3], sd.total(0))
        norm_sums(2, gain_sum, shift_sum)
        r.r3[...] = r.r3[...] + rows
        save(r.r3, r.o_decg)

    def mixed_block(block):
        part = window(block * R, R)
        r.ga[part, :] = dot(r.z2[part, :], r.w_pe[...], NT).astype(bf16)

    def mixed_near():
        fetch("g1")
        need("w_pe", "q", "k", "v", "a", "l", "w_e")
        mixed_block(me)

        @pl.loop(0, steps)
        def _(j):
            gze.mate(j)

        mixed_block(mate)

    def mixed_far():
        @pl.loop(0, steps)
        def _(j):
            gze.opp(j)

        @pl.loop(0, steps)
        def _(j):
            gze.diag(j)

        @pl.loop(0, 2)
        def _(i):
            mixed_block(opp + i * (diag - opp))

        r.es[...] = head_sums(r.a, r.ga)

    def attend_piece(i):
        attend_back_rows(r.q, r.ck, r.cv, r.ga, r.l, r.es, r.gqt, r.gk, r.gv, i * 2 * T, 2 * T, False)

    def encoder_queries():
        r.gq[...] = (jnp.transpose(r.gqt[...]) * SCALE).astype(bf16)
        need("g1")

    def attend_rows_back(block, j):
        part = window(block * R + j * S, S)
        return dot(r.gq[part, :], r.w_e[0]) + dot(r.gk[part, :], r.w_e[1]) + dot(r.gv[part, :], r.w_e[2])

    def rows_far():
        @pl.loop(0, steps)
        def _(j):
            s2.put_diag(j, attend_rows_back(diag, j))
            s2.put_opp(j, attend_rows_back(opp, j))

    def rows_near():
        @pl.loop(0, steps)
        def _(j):
            s2.put_mate(j, attend_rows_back(mate, j))
            s2.put_own(j, attend_rows_back(me, j))

    def encoder_weights_a():
        r.e2a[0:192, :] = dot(r.gq[...], r.g3[...], TN).astype(bf16)
        r.e2a[192:384, :] = dot(r.gk[...], r.g3[...], TN).astype(bf16)

    def encoder_weights_b():
        r.e2b[0:192, :] = dot(r.gv[...], r.g3[...], TN).astype(bf16)
        r.e2b[192:384, :] = dot(r.a[...], r.z2[...], TN).astype(bf16)

    def encoder_sums():
        small[QV_BIAS:QV_BIAS + 1, 0:192] = matrix_sums(r.gq)
        small[QV_BIAS + 1:QV_BIAS + 2, 0:192] = matrix_sums(r.gv)
        add_rows(small, OUT_BIAS, column_sums(r.z2[window(me * R, R), :].astype(f32)))

    def frames_residual(j):
        part = window(j * S, S)
        if j == 0:
            need("frames")
        rows, gain_sum, shift_sum = norm_back(r.cot[part, :].astype(f32), gains[0:1], s2.total(j))
        norm_sums(0, gain_sum, shift_sum)
        r.mid[part, :] = r.mid[part, :] + rows

    pieces += [encoder_fc1, encoder_fc2, decoder_rows, mixed_near, mixed_far]
    for i in range(2 * R // T):
        pieces.append(functools.partial(attend_piece, i))
    pieces += [encoder_queries, rows_far, rows_near, encoder_weights_a, encoder_weights_b, encoder_sums]
    each_step(frames_residual)
    pieces.append(lambda: save(r.mid, r.o_encg))

    last = {
        ("a", 5): [(r.d1a, r.o_fc1.at[1])],
        ("b", 5): [(r.d1b, r.o_fc2.at[1])],
        ("c", 5): [(r.cross.at[0:576], r.o_qkv.at[2]), (r.cross.at[576:768], r.o_proj.at[2])],
        ("s", 5): [(r.self.at[0:576], r.o_qkv.at[1]), (r.self.at[576:768], r.o_proj.at[1])],
        ("e", 5): [(r.e1a, r.o_fc1.at[0])],
        ("f", 5): [(r.e1b, r.o_fc2.at[0])],
        ("g", 5): [(r.e2a, r.o_qkv.at[0, 0:384])],
        ("h", 5): [(r.e2b.at[0:192], r.o_qkv.at[0, 384:576]), (r.e2b.at[192:384], r.o_proj.at[0])],
        ("m", 4): [(r.sums, r.o_small)],
    }
    for item in SCHEDULE:
        if isinstance(item, int):
            pieces[item]()
            continue
        name, sign, i = item[0], item[1], int(item[2])
        if sign == "+":
            buckets[name].start(i)
        else:
            buckets[name].finish(i)
            for pair in last.get((name, i), ()):
                save(*pair)

    @pl.loop(0, steps)
    def _(j):
        for each in (gz1, gze, s2):
            each.close(j)

    for each in (gm3, gz2, gzs, sf, sq, sd):
        each.close(0)
    for copy in saves:
        copy.wait()


def backward_call(operands, clips, R, T, D, W, F):
    steps = R // T
    N, M = 4 * R, 4 * T
    partners = 2 + bit_count(clips)
    outs = dict(
        dec=B(T, D), encg=B32(R, D), decg=B32(T, D), qkv=B(3, 3 * W, D), proj=B(3, W, D), fc1=B(2, D, F),
        fc2=B(2, F, D), small=B32(SMALL, D),
    )
    bits = bit_count(clips)
    signals = lambda: [dma(4, bits), pltpu.SemaphoreType.REGULAR((bits,))]
    near = lambda: scatter_shapes(T, D, 1)[:-1]
    land = lambda rows: V(land_rows(rows, clips), D)
    scratch = dict(
        second=V32(T, D), d_f1=V(D, F), d_f2=V(F, D), z3=V(M, D), r3=V32(T, D), w_pc=V(W, D), ca=V(M, W), cl=V32(8, M),
        cq=V(M, W), ck=V(N, W), cv=V(N, W), w_c=V(3, W, D), g3=V(N, D), after=V32(T, D), cot=V(R, D),
        w_f1=V(D, F), w_f2=V(F, D), gd=V(N, F), w_s=V(3, W, D), w_ps=V(W, D), sq=V(M, W), sk=V(M, W),
        sv=V(M, W), sa=V(M, W), sl=V32(8, M), e=V(N, F), g2=V(N, D), mid=V32(R, D), w_pe=V(W, D), q=V(N, W),
        a=V(N, W), l=V32(8, N), w_e=V(3, W, D),
        m3=V(M, D), dg=V(M, F), gu=V(M, F), dz2=V(M, D), cga=V(M, W), cs=V32(8, M), cgqt=V32(W, M),
        cgq=V(M, W), gk=V(N, W), gv=V(N, W), dec=V(T, D), zs=V(M, D), renc=V32(R, D), z1=V(N, D),
        sga=V(M, W), sgqt=V32(W, M), sgq=V(M, W), sgk=V(M, W), sgv=V(M, W), z2=V(N, D), ga=V(N, W),
        es=V32(8, N), gqt=V32(W, N), gq=V(N, W), sums=V32(SMALL, D),
        d1a=V(D, F), d1b=V(F, D), cross=V(4 * W, D), self=V(4 * W, D), e1a=V(D, F), e1b=V(F, D), e2a=V(2 * W, D),
        e2b=V(2 * W, D), land_a=land(D), land_b=land(F), land_c=land(4 * W), land_s=land(4 * W), land_g=land(2 * W),
        land_h=land(2 * W), small_land=V32(partners, SMALL, D), small_sem=dma(2, partners),
        near_a=near(), near_b=near(), near_c=near(), wide=scatter_shapes(R, D, steps)[:-1],
        sem_b=dma(6, 1), sem_f=dma(6, 1), sem_q=dma(6, 1), sem_d=dma(6, 1),
        sem_m=dma(6, steps), sem_1=dma(6, steps), sem_2=dma(6, steps),
        agm3=dma(6, 1), agz2=dma(6, 1), ags=dma(6, 1), agz1=dma(6, steps), agze=dma(6, steps),
        load_sem=dma(33), late_sem=dma(6), save_sem=dma(16),
    )
    scratch |= {"red_" + key: signals() for key in "abcsefgh"}
    in_vmem = ("gain", "shift", "out_bias", "fc1_bias", "dec_len", "dec_in")
    return call_kernel(
        functools.partial(backward_kernel, R, T, clips), "backward", 1, operands, in_vmem, outs, scratch, 63 << 20
    )


def finish_kernel(
    i_enc, i_dec, i_encg, i_decg, small, i_qkv, i_proj, i_fc1, i_fc2,
    o_enc, o_dec, o_encg, o_decg, o_gain, o_shift, o_qkv, o_qvb, o_proj, o_bias, o_fc1, o_fc1b, o_fc2,
    narrow, wide, r_enc, r_dec, r_encg, r_decg, row_sem, in_sem, out_sem,
):
    chunk = narrow.shape[1]
    parts = []
    for src, dst in ((i_qkv, o_qkv), (i_proj, o_proj), (i_fc1, o_fc1), (i_fc2, o_fc2)):
        for i in range(src.shape[0]):
            for start in range(0, src.shape[1], chunk):
                parts.append((src.at[i, pl.ds(start, chunk)], dst.at[i, pl.ds(start, chunk)]))
    loads = [pltpu.make_async_copy(src, narrow.at[n], in_sem.at[n]) for n, (src, _) in enumerate(parts)]
    stores = [pltpu.make_async_copy(wide.at[n], dst, out_sem.at[n]) for n, (_, dst) in enumerate(parts)]
    pairs = ((i_enc, r_enc, o_enc), (i_dec, r_dec, o_dec), (i_encg, r_encg, o_encg), (i_decg, r_decg, o_decg))
    moves = [pltpu.make_async_copy(src, held, row_sem.at[0, n]) for n, (src, held, _) in enumerate(pairs)]
    passes = [pltpu.make_async_copy(held, dst.at[0], row_sem.at[1, n]) for n, (_, held, dst) in enumerate(pairs)]
    for copy in loads + moves:
        copy.start()
    o_gain[...] = small[GAIN:GAIN + 5, :]
    o_shift[...] = small[SHIFT:SHIFT + 5, :]
    o_bias[...] = small[OUT_BIAS:OUT_BIAS + 5, :]
    o_fc1b[...] = small[FC1_BIAS:FC1_BIAS + 2, :]
    for i in range(3):
        o_qvb[i] = small[QV_BIAS + 2 * i:QV_BIAS + 2 * i + 2, 0:o_qvb.shape[2]]
    for n, (load, store) in enumerate(zip(loads, stores)):
        load.wait()
        wide[n] = narrow[n].astype(f32)
        store.start()
    for move, copy in zip(moves, passes):
        move.wait()
        copy.start()
    for copy in passes + stores:
        copy.wait()


def finish_call(enc_out, last, W):
    R, D = last["encg"].shape
    T = last["decg"].shape[0]
    F = last["fc1"].shape[2]
    chunk = W
    count = sum(last[name].shape[0] * last[name].shape[1] // chunk for name in ("qkv", "proj", "fc1", "fc2"))
    B32 = lambda *shape: jax.ShapeDtypeStruct(shape, f32)
    shapes = [
        jax.ShapeDtypeStruct((1, R, D), bf16), jax.ShapeDtypeStruct((1, T, D), bf16), B32(1, R, D), B32(1, T, D),
        B32(5, D), B32(5, D), B32(3, 3 * W, D), B32(3, 2, W), B32(3, W, D), B32(5, D), B32(2, D, F), B32(2, F), B32(2, F, D),
    ]
    whole = [ANY, ANY, ANY, ANY, VMEM, VMEM, ANY, VMEM, ANY, VMEM, ANY, VMEM, ANY]
    return pl.pallas_call(
        finish_kernel,
        out_shape=shapes,
        in_specs=[ANY] * 4 + [VMEM] + [ANY] * 4,
        out_specs=whole,
        scratch_shapes=[
            pltpu.VMEM((count, chunk, D), bf16), pltpu.VMEM((count, chunk, D), f32),
            pltpu.VMEM((R, D), bf16), pltpu.VMEM((T, D), bf16), pltpu.VMEM((R, D), f32), pltpu.VMEM((T, D), f32),
            pltpu.SemaphoreType.DMA((2, 4)), pltpu.SemaphoreType.DMA((count,)), pltpu.SemaphoreType.DMA((count,)),
        ],
        compiler_params=pltpu.CompilerParams(vmem_limit_bytes=60 << 20),
        name="finish",
    )(
        enc_out, last["dec"], last["encg"], last["decg"], last["small"],
        last["qkv"], last["proj"], last["fc1"], last["fc2"],
    )


def on_device(
    clips,
    enc_in, dec_in, dec_len, norm_gain, norm_shift, qkv, qv_bias, proj, out_bias, fc1, fc1_bias, fc2, enc_cot, dec_cot,
):
    turned = jnp.swapaxes(qkv, 2, 3)
    W, D = turned.shape[2:]
    R, T, F = enc_in.shape[1], dec_in.shape[1], fc1.shape[2]
    shared = dict(
        enc_in=enc_in, dec_in=dec_in, gain=norm_gain, shift=norm_shift, out_bias=out_bias, fc1_bias=fc1_bias,
        dec_len=dec_len.reshape(1, 1), qkv=turned, proj=proj, fc1=fc1, fc2=fc2,
    )
    kept = forward_call(shared | dict(qv_bias=qv_bias, dec_cot=dec_cot), R, T, D, W, F)
    carried = {"i_" + key: value for key, value in kept.items() if key != "enc"}
    last = backward_call(shared | dict(enc_cot=enc_cot) | carried, clips, R, T, D, W, F)
    outs = list(finish_call(kept["enc"], last, W))
    outs[6] = jnp.swapaxes(outs[6].reshape(3, 3, W, D), 2, 3)
    return tuple(outs)


def solution(mesh):
    rows = P("dp", "mp", None)
    columns = P(None, None, None, "mp")
    return jax.shard_map(
        functools.partial(on_device, mesh.shape["dp"]),
        mesh=mesh,
        in_specs=(
            rows, rows, P("dp"), P(), P(), columns, P(None, None, "mp"), P(None, "mp", None), P(),
            P(None, None, "mp"), P(None, "mp"), P(None, "mp", None), rows, rows,
        ),
        out_specs=(
            rows, rows, rows, rows, P(), P(), columns, P(None, None, "mp"), P(None, "mp", None), P(),
            P(None, None, "mp"), P(None, "mp"), P(None, "mp", None),
        ),
        check_vma=False,
    )
```

```python
import functools
import math

import jax
import jax.numpy as jnp
from jax import lax
from jax.experimental import pallas as pl
from jax.experimental.pallas import tpu as pltpu
from jax.sharding import PartitionSpec as P

HEAD = 64
epsilon = 1e-05
masked_score = -1e30
f32 = jnp.float32
bf16 = jnp.bfloat16
NN = (((1,), (0,)), ((), ()))
NT = (((1,), (1,)), ((), ()))
TN = (((0,), (0,)), ((), ()))
SCALE = HEAD ** (-0.5)
SCORE_TO_LOG2 = SCALE * math.log2(math.e)
ANY = pl.BlockSpec(memory_space=pl.ANY)
VMEM = pl.BlockSpec(memory_space=pltpu.VMEM)


def dot(a, b, dims=NN):
    return lax.dot_general(a, b, dims, preferred_element_type=f32)


def window(start, size):
    return pl.ds(pl.multiple_of(start, 16), size)


def places():
    me = lax.axis_index("mp")
    core = lax.rem(me, 2)
    mate = me + 1 - 2 * core
    opp = lax.rem(me + 2, 4)
    diag = lax.rem(mate + 2, 4)
    return me, mate, opp, diag


def remote(src, dst, sent, landed, axis, index):
    return pltpu.make_async_remote_copy(
        src_ref=src,
        dst_ref=dst,
        send_sem=sent,
        recv_sem=landed,
        device_id={axis: index},
        device_id_type=pl.DeviceIdType.MESH,
    )


class Gather:
    def __init__(self, buf, sems, rows, step):
        self.buf, self.sems, self.rows, self.step = buf, sems, rows, step
        self.me, self.mate_id, self.opp_id, self.diag_id = places()

    def at(self, block, j):
        return window(block * self.rows + j * self.step, self.step)

    def copy(self, kind, block, j, target):
        part = self.buf.at[self.at(block, j)]
        return remote(part, part, self.sems.at[2 * kind, j], self.sems.at[2 * kind + 1, j], "mp", target)

    def send(self, j):
        self.copy(0, self.me, j, self.opp_id).start()
        self.copy(1, self.me, j, self.mate_id).start()

    def mate(self, j):
        self.copy(1, self.mate_id, j, self.mate_id).wait_recv()

    def opp(self, j):
        self.copy(0, self.opp_id, j, self.opp_id).wait_recv()
        self.copy(2, self.opp_id, j, self.mate_id).start()

    def diag(self, j):
        self.copy(2, self.diag_id, j, self.mate_id).wait_recv()

    def close(self, j):
        self.copy(0, self.me, j, self.opp_id).wait_send()
        self.copy(1, self.me, j, self.mate_id).wait_send()
        self.copy(2, self.opp_id, j, self.mate_id).wait_send()


class Scatter:
    def __init__(self, own, send, land, ysend, yland, sems, rows, step):
        self.own, self.out, self.land, self.ysend, self.yland = own, send, land, ysend, yland
        self.sems, self.rows, self.step = sems, rows, step
        self.me, self.mate_id, self.opp_id, self.diag_id = places()

    def near(self, half, j):
        part = window(half * self.rows + j * self.step, self.step)
        return remote(
            self.out.at[part], self.land.at[part],
            self.sems.at[2 * half, j], self.sems.at[2 * half + 1, j], "mp", self.mate_id,
        )

    def far(self, j):
        part = window(j * self.step, self.step)
        return remote(
            self.ysend.at[part], self.yland.at[part],
            self.sems.at[4, j], self.sems.at[5, j], "mp", self.opp_id,
        )

    def put_diag(self, j, value):
        self.out[window(j * self.step, self.step), :] = value.astype(bf16)
        self.near(0, j).start()

    def put_opp(self, j, value):
        part = window(j * self.step, self.step)
        self.near(0, j).wait_recv()
        self.ysend[part, :] = (value + self.land[part, :].astype(f32)).astype(bf16)
        self.far(j).start()

    def put_mate(self, j, value):
        self.out[window(self.rows + j * self.step, self.step), :] = value.astype(bf16)
        self.near(1, j).start()

    def put_own(self, j, value):
        self.own[window(j * self.step, self.step), :] = value

    def total(self, j):
        self.near(1, j).wait_recv()
        self.far(j).wait_recv()
        part = window(j * self.step, self.step)
        near = self.land[window(self.rows + j * self.step, self.step), :].astype(f32)
        return self.own[part, :] + near + self.yland[part, :].astype(f32)

    def close(self, j):
        self.near(0, j).wait_send()
        self.near(1, j).wait_send()
        self.far(j).wait_send()


def scatter_shapes(rows, width, steps):
    return [
        pltpu.VMEM((rows, width), f32),
        pltpu.VMEM((2 * rows, width), bf16),
        pltpu.VMEM((2 * rows, width), bf16),
        pltpu.VMEM((rows, width), bf16),
        pltpu.VMEM((rows, width), bf16),
        pltpu.SemaphoreType.DMA((6, steps)),
    ]


def meet(partners):
    barrier = pltpu.get_barrier_semaphore()
    for axis, index in partners:
        pl.semaphore_signal(barrier, inc=1, device_id={axis: index}, device_id_type=pl.DeviceIdType.MESH)
    pl.semaphore_wait(barrier, len(partners))


def layer_norm(rows_in, gain_row, shift_row):
    average = jnp.mean(rows_in, axis=-1, keepdims=True)
    centred = rows_in - average
    spread = jnp.mean(centred * centred, axis=-1, keepdims=True)
    return centred * lax.rsqrt(spread + epsilon) * gain_row + shift_row


def head_row(width, h):
    lane = lax.broadcasted_iota(jnp.int32, (1, width), 1)
    return jnp.where((lane >= h * HEAD) & (lane < (h + 1) * HEAD), 1.0, 0.0).astype(f32)


def attend_rows(q_ref, k_ref, v_ref, out_ref, log_ref, start, size, causal):
    width = q_ref.shape[1]
    part = window(start, size)
    queries = q_ref[part, :]
    keys = k_ref[...]
    values = v_ref[...]
    lane = lax.broadcasted_iota(jnp.int32, (size, log_ref.shape[1]), 1)
    mixed = jnp.zeros((size, width), f32)
    logs = jnp.zeros((size, log_ref.shape[1]), f32)
    for h in range(width // HEAD):
        picked = head_row(width, h)
        scores = dot(queries * picked.astype(bf16), keys, NT)
        if causal:
            row_index = lax.broadcasted_iota(jnp.int32, scores.shape, 0) + start
            col_index = lax.broadcasted_iota(jnp.int32, scores.shape, 1)
            scores = jnp.where(col_index <= row_index, scores, masked_score)
        highest = jnp.max(scores, axis=-1, keepdims=True)
        powers = jnp.exp2((scores - highest) * SCORE_TO_LOG2)
        total = jnp.sum(powers, axis=-1, keepdims=True)
        mixed = mixed + dot(powers.astype(bf16), values) * (picked / total)
        logs = jnp.where(lane == h, highest * SCORE_TO_LOG2 + jnp.log2(total), logs)
    out_ref[part, :] = mixed.astype(bf16)
    log_ref[part, :] = logs


def gelu_parts(hidden):
    below = 0.5 + 0.5 * lax.erf(hidden * (0.5 ** 0.5))
    density = jnp.exp2(hidden * hidden * (-0.5 * math.log2(math.e))) * ((2 * math.pi) ** (-0.5))
    return hidden * below, below + hidden * density


def add_rows(ref, row, value):
    ref[row:row + 1, :] = ref[row:row + 1, :] + value


def column_sums(value):
    return jnp.sum(value, axis=0, keepdims=True)


def matrix_sums(ref):
    ones = jnp.ones((16, ref.shape[0]), bf16)
    return dot(ones, ref[...])[0:1]


def norm_back(rows_in, gain_row, gradient):
    average = jnp.mean(rows_in, axis=-1, keepdims=True)
    centred = rows_in - average
    spread = jnp.mean(centred * centred, axis=-1, keepdims=True)
    scale = lax.rsqrt(spread + epsilon)
    hat = centred * scale
    inner = gradient * gain_row
    first = jnp.mean(inner, axis=-1, keepdims=True)
    second = jnp.mean(inner * hat, axis=-1, keepdims=True)
    return (inner - first - hat * second) * scale, column_sums(gradient * hat), column_sums(gradient)


def head_sums(a_ref, g_ref):
    width = a_ref.shape[1]
    row = lax.broadcasted_iota(jnp.int32, (8, width), 0)
    lane = lax.broadcasted_iota(jnp.int32, (8, width), 1)
    picker = jnp.where((lane >= row * HEAD) & (lane < (row + 1) * HEAD), 1.0, 0.0).astype(f32)
    both = a_ref[...].astype(f32) * g_ref[...].astype(f32)
    return lax.dot_general(picker, both, NT, precision=lax.Precision.HIGHEST, preferred_element_type=f32)


def attend_back_rows(q_ref, k_ref, v_ref, ga_ref, log_ref, sum_ref, gqt_ref, gk_ref, gv_ref, start, size, causal):
    width = q_ref.shape[1]
    part = window(start, size)
    queries = q_ref[...]
    grads = ga_ref[...]
    keys = k_ref[part, :]
    values = v_ref[part, :]
    turned = jnp.transpose(keys.astype(f32)).astype(bf16)
    gk = jnp.zeros((size, width), f32)
    gv = jnp.zeros((size, width), f32)
    for h in range(width // HEAD):
        picked = head_row(width, h)
        scores = dot(keys * picked.astype(bf16), queries, NT)
        weights = jnp.exp2(scores * SCORE_TO_LOG2 - log_ref[h:h + 1, :])
        if causal:
            key_index = lax.broadcasted_iota(jnp.int32, scores.shape, 0) + start
            query_index = lax.broadcasted_iota(jnp.int32, scores.shape, 1)
            weights = jnp.where(key_index <= query_index, weights, 0.0)
        slopes = dot(values * picked.astype(bf16), grads, NT)
        score_grads = (weights * (slopes - sum_ref[h:h + 1, :])).astype(bf16)
        gk = gk + dot(score_grads, queries) * (picked * SCALE)
        gv = gv + dot(weights.astype(bf16), grads) * picked
        some = slice(h * HEAD, (h + 1) * HEAD)
        gqt_ref[some, :] = gqt_ref[some, :] + dot(turned[some, :], score_grads)
    gk_ref[part, :] = gk.astype(bf16)
    gv_ref[part, :] = gv.astype(bf16)


X_FIRST, Z_FIRST = (0, 1, 2), (1, 0, 2)


class Reduce:
    def __init__(self, buf, land, sems, free, order, clips):
        self.buf, self.land, self.sems, self.free = buf, land, sems, free
        bits = bit_count(clips)
        self.halving = min(3, bits)
        index = lax.axis_index("dp")
        start, size, offset = 0, buf.shape[0], 0
        self.steps = []
        for t, b in enumerate([b for b in order if b < self.halving] + list(range(self.halving, bits))):
            bit = lax.rem(index // (1 << b), 2)
            partner = index + (1 - 2 * bit) * (1 << b)
            if t < self.halving:
                size //= 2
                keep, give = start + bit * size, start + (1 - bit) * size
                start = keep
            else:
                keep = give = start
                offset = 0
            self.steps.append((partner, keep, give, offset, size))
            offset += size

    def out(self, t):
        partner, keep, give, offset, size = self.steps[t]
        return remote(
            self.buf.at[window(give, size)], self.land.at[window(offset, size)],
            self.sems.at[0, t], self.sems.at[1, t], "dp", partner,
        )

    def back(self, t, start):
        partner, size = self.steps[t][0], self.steps[t][4]
        part = self.buf.at[window(start, size)]
        return remote(part, part, self.sems.at[2, t], self.sems.at[3, t], "dp", partner)

    def start(self, i):
        if i < self.halving:
            self.out(i).start()
        else:
            t = 2 * self.halving - 1 - i
            pl.semaphore_wait(self.free.at[t], 1)
            self.back(t, self.steps[t][1]).start()

    def release(self, t):
        pl.semaphore_signal(
            self.free.at[t], inc=1, device_id={"dp": self.steps[t][0]}, device_id_type=pl.DeviceIdType.MESH
        )

    def add(self, t):
        partner, keep, give, offset, size = self.steps[t]
        copy = self.out(t)
        copy.wait_recv()
        copy.wait_send()
        if t < self.halving:
            self.release(t)
        chunk = size
        while chunk > 192:
            chunk //= 2

        @pl.loop(0, size // chunk)
        def _(i):
            part = window(keep + i * chunk, chunk)
            brought = self.land[window(offset + i * chunk, chunk), :].astype(f32)
            self.buf[part, :] = (self.buf[part, :].astype(f32) + brought).astype(bf16)

    def finish(self, i):
        if i < self.halving:
            self.add(i)
            if i + 1 == self.halving:
                for t in range(self.halving, len(self.steps)):
                    self.release(t)
                    pl.semaphore_wait(self.free.at[t], 1)
                    self.out(t).start()
                    self.add(t)
        else:
            t = 2 * self.halving - 1 - i
            self.back(t, self.steps[t][2]).wait_recv()
            self.back(t, self.steps[t][1]).wait_send()


def bit_count(clips):
    return clips.bit_length() - 1


def land_rows(rows, clips):
    return rows - (rows >> min(3, bit_count(clips)))


def clip_partners(clips):
    index = lax.axis_index("dp")
    partners = []
    for b in range(bit_count(clips)):
        bit = lax.rem(index // (1 << b), 2)
        partners.append(("dp", index + (1 - 2 * bit) * (1 << b)))
    return partners


def far_partners(clips):
    index = lax.axis_index("dp")
    return [("dp", lax.rem(index, 2) + 2 * (3 - index // 2))] if clips == 8 else []


class Small:
    def __init__(self, buf, land, sems, clips, shared):
        self.buf, self.land, self.sems, self.shared = buf, land, sems, shared
        me, mate, opp, diag = places()
        self.partners = [("mp", mate), ("mp", opp)] + clip_partners(clips)

    def copy(self, t):
        axis, index = self.partners[t]
        rows = pl.ds(0, self.shared if axis == "mp" else self.buf.shape[0])
        return remote(
            self.buf.at[rows], self.land.at[t, rows], self.sems.at[0, t], self.sems.at[1, t], axis, index
        )

    def start(self, t):
        self.copy(t).start()

    def finish(self, t):
        self.copy(t).wait()
        rows = self.shared if self.partners[t][0] == "mp" else self.buf.shape[0]
        self.buf[0:rows, :] = self.buf[0:rows, :] + self.land[t, 0:rows, :]
        if t == 4:
            for later in range(5, len(self.partners)):
                self.start(later)
                self.finish(later)


class Inward:
    def __init__(self, buf, land, sems, free):
        self.buf, self.land, self.sems, self.free = buf, land, sems, free
        index = lax.axis_index("dp")
        side, place = lax.rem(index, 2), index // 2
        half, upper = lax.rem(place, 2), place // 2
        self.inner = half != upper
        self.outer = half == upper
        self.size = buf.shape[0] // 2
        self.pair = index + 1 - 2 * side
        self.near = index + 2 * (1 - 2 * half)
        self.other = index + 2 * (1 - 2 * upper)
        self.keep, self.give = side * self.size, (1 - side) * self.size
        quarter = self.size // 2
        self.mine, self.theirs = self.keep + upper * quarter, self.keep + (1 - upper) * quarter

    def part(self, start, size):
        return self.buf.at[window(start, size)]

    def copy(self, i, receiving=False):
        h, q = self.size, self.size // 2
        if i == 0:
            src, dst, to = self.part(self.give, h), self.land.at[pl.ds(0, h)], self.pair
        elif i == 1:
            src, dst, to = self.part(self.keep, h), self.land.at[pl.ds(0, h)], self.near
        elif i == 2:
            src, dst, to = self.part(self.theirs, q), self.land.at[pl.ds(h, q)], self.other
        elif i == 3:
            src = dst = self.part(self.theirs if receiving else self.mine, q)
            to = self.other
        elif i == 4:
            src = dst = self.part(self.keep, h)
            to = self.near
        else:
            src = dst = self.part(self.give if receiving else self.keep, h)
            to = self.pair
        return remote(src, dst, self.sems.at[0, i], self.sems.at[1, i], "dp", to)

    def signal(self, n, to):
        pl.semaphore_signal(self.free.at[n], inc=1, device_id={"dp": to}, device_id_type=pl.DeviceIdType.MESH)

    def add(self, start, offset, size):
        chunk = size
        while chunk > 192:
            chunk //= 2

        @pl.loop(0, size // chunk)
        def _(i):
            part = window(start + i * chunk, chunk)
            brought = self.land[window(offset + i * chunk, chunk), :].astype(f32)
            self.buf[part, :] = (self.buf[part, :].astype(f32) + brought).astype(bf16)

    def start(self, i):
        if i in (0, 5):
            if i == 5:
                pl.semaphore_wait(self.free.at[0], 1)
            self.copy(i).start()
            return

        @pl.when(self.outer if i == 1 else self.inner)
        def _():
            if i != 2:
                pl.semaphore_wait(self.free.at[{1: 3, 3: 2, 4: 1}[i]], 1)
            self.copy(i).start()

    def finish(self, i):
        h, q = self.size, self.size // 2
        if i == 0:
            self.copy(0).wait_recv()
            self.copy(0).wait_send()
            self.signal(0, self.pair)
            self.add(self.keep, 0, h)

            @pl.when(self.inner)
            def _():
                self.signal(3, self.near)
        elif i == 1:
            @pl.when(self.outer)
            def _():
                self.copy(1).wait_send()
                self.signal(1, self.near)

            @pl.when(self.inner)
            def _():
                self.copy(1).wait_recv()
                self.add(self.keep, 0, h)
        elif i == 2:
            @pl.when(self.inner)
            def _():
                self.copy(2).wait_recv()
                self.copy(2).wait_send()
                self.signal(2, self.other)
                self.add(self.mine, h, q)
        elif i == 3:
            @pl.when(self.inner)
            def _():
                self.copy(3, True).wait_recv()
                self.copy(3).wait_send()
        elif i == 4:
            @pl.when(self.outer)
            def _():
                self.copy(4).wait_recv()

            @pl.when(self.inner)
            def _():
                self.copy(4).wait_send()
        else:
            self.copy(5, True).wait_recv()
            self.copy(5).wait_send()


def clip_sum(buf, land, sems, free, order, clips):
    if clips == 8 and order == X_FIRST:
        return Inward(buf, land, sems, free)
    return Reduce(buf, land, sems, free, order, clips)


def sum_land(rows, order, clips):
    return V(rows * 3 // 4 if clips == 8 and order == X_FIRST else land_rows(rows, clips), 768)


def sum_signals(order, clips):
    if clips == 8 and order == X_FIRST:
        return [dma(2, 6), pltpu.SemaphoreType.REGULAR((4,))]
    return [dma(4, bit_count(clips)), pltpu.SemaphoreType.REGULAR((bit_count(clips),))]


class Refs:
    def __init__(self, names, refs):
        self.__dict__.update(zip(names, refs, strict=True))


def forward_kernel(R, T, names, *refs):
    r = Refs(names, refs)
    S = T
    steps = R // S
    me, mate, opp, diag = places()
    sources = dict(
        w_e=r.qkv.at[0], w_s=r.qkv.at[1], w_c=r.qkv.at[2], w_pe=r.proj.at[0], w_ps=r.proj.at[1], w_pc=r.proj.at[2],
        w_f1=r.fc1.at[0], w_f2=r.fc2.at[0],
    )
    loads = {
        name: pltpu.make_async_copy(src, getattr(r, name), r.load_sem.at[i])
        for i, (name, src) in enumerate(sources.items())
    }
    for load in loads.values():
        load.start()
    saves = []

    def save(*kept):
        for name in kept:
            copy = pltpu.make_async_copy(getattr(r, name), getattr(r, "o_" + name), r.save_sem.at[len(saves)])
            copy.start()
            saves.append(copy)

    gains = r.gain[...].astype(f32)
    shifts = r.shift[...].astype(f32)
    branch_bias = r.out_bias[...].astype(f32)
    head_bias = r.qv_bias[...].astype(f32)
    wide_bias = r.fc1_bias[...].astype(f32)
    own = window(me * T, T)

    meet([("mp", mate), ("mp", opp)])

    gd1 = Gather(r.m1, r.agd1, T, S)
    r.m1[own, :] = layer_norm(r.dec_in[0].astype(f32), gains[2:3], shifts[2:3]).astype(bf16)
    gd1.send(0)
    ge1 = Gather(r.g1, r.ag1, R, S)

    @pl.loop(0, steps)
    def _(j):
        rows = r.enc_in[0, window(j * S, S), :].astype(f32)
        r.g1[window(me * R + j * S, S), :] = layer_norm(rows, gains[0:1], shifts[0:1]).astype(bf16)
        ge1.send(j)

    def project_block(block):
        part = window(block * R, R)
        rows = r.g1[part, :]
        r.q[part, :] = (dot(rows, r.w_e[0], NT) + head_bias[0, 0:1]).astype(bf16)
        r.k[part, :] = dot(rows, r.w_e[1], NT).astype(bf16)
        r.v[part, :] = (dot(rows, r.w_e[2], NT) + head_bias[0, 1:2]).astype(bf16)

    loads["w_e"].wait()

    @pl.loop(0, steps)
    def _(j):
        ge1.mate(j)

    @pl.loop(0, 2)
    def _(i):
        project_block(me + i * (mate - me))

    gd1.mate(0)
    gd1.opp(0)
    gd1.diag(0)
    save("m1")
    loads["w_s"].wait()
    r.sq[...] = (dot(r.m1[...], r.w_s[0], NT) + head_bias[1, 0:1]).astype(bf16)
    r.sk[...] = dot(r.m1[...], r.w_s[1], NT).astype(bf16)
    r.sv[...] = (dot(r.m1[...], r.w_s[2], NT) + head_bias[1, 1:2]).astype(bf16)
    save("sq", "sk", "sv")

    @pl.loop(0, 2)
    def _(i):
        attend_rows(r.sq, r.sk, r.sv, r.sa, r.slc, i * 2 * T, 2 * T, True)

    save("sa")
    r.sl[...] = jnp.transpose(r.slc[...])[0:8]
    save("sl")
    loads["w_ps"].wait()

    @pl.loop(0, steps)
    def _(j):
        ge1.opp(j)

    sd = Scatter(*r.rsd, T, S)
    sd.put_diag(0, dot(r.sa[window(diag * T, T), :], r.w_ps[...]))
    sd.put_opp(0, dot(r.sa[window(opp * T, T), :], r.w_ps[...]))
    sd.put_mate(0, dot(r.sa[window(mate * T, T), :], r.w_ps[...]))
    sd.put_own(0, dot(r.sa[own, :], r.w_ps[...]))

    @pl.loop(0, steps)
    def _(j):
        ge1.diag(j)

    @pl.loop(0, 2)
    def _(i):
        project_block(opp + i * (diag - opp))

    save("g1", "q", "k", "v")
    loads["w_pe"].wait()
    s1 = Scatter(*r.rs1, R, S)

    def attend_chunk(block, j):
        attend_rows(r.q, r.k, r.v, r.a, r.lc, block * R + j * S, S, False)
        return dot(r.a[window(block * R + j * S, S), :], r.w_pe[...])

    def attend_block(block, put):
        attend_rows(r.q, r.k, r.v, r.a, r.lc, block * R, R, False)

        @pl.loop(0, steps)
        def _(j):
            put(j, dot(r.a[window(block * R + j * S, S), :], r.w_pe[...]))

    @pl.loop(0, steps)
    def _(j):
        s1.put_diag(j, attend_chunk(diag, j))
        s1.put_opp(j, attend_chunk(opp, j))

    attend_block(mate, s1.put_mate)
    r.after[...] = r.dec_in[0].astype(f32) + sd.total(0) + branch_bias[2:3]
    gd2 = Gather(r.m2, r.agd2, T, S)
    r.m2[own, :] = layer_norm(r.after[...], gains[3:4], shifts[3:4]).astype(bf16)
    gd2.send(0)
    save("after")
    attend_block(me, s1.put_own)

    ge2 = Gather(r.g2, r.ag2, R, S)

    @pl.loop(0, steps)
    def _(j):
        part = window(j * S, S)
        rows = r.enc_in[0, part, :].astype(f32) + s1.total(j) + branch_bias[0:1]
        r.mid[part, :] = rows
        r.g2[window(me * R + j * S, S), :] = layer_norm(rows, gains[1:2], shifts[1:2]).astype(bf16)
        ge2.send(j)

    r.l[...] = jnp.transpose(r.lc[...])[0:8]
    save("mid", "l", "a")
    loads["w_f1"].wait()
    loads["w_f2"].wait()
    s2 = Scatter(*r.rs2, R, S)

    def feed(block, j):
        part = window(block * R + j * S, S)
        hidden = dot(r.g2[part, :], r.w_f1[...]) + wide_bias[0:1]
        active, slope = gelu_parts(hidden)
        active = active.astype(bf16)
        r.e[part, :] = active
        r.gd[part, :] = slope.astype(bf16)
        return dot(active, r.w_f2[...])

    @pl.loop(0, steps)
    def _(j):
        s2.put_own(j, feed(me, j))

    @pl.loop(0, steps)
    def _(j):
        ge2.mate(j)
        s2.put_mate(j, feed(mate, j))

    @pl.loop(0, steps)
    def _(j):
        ge2.opp(j)
        ge2.diag(j)
        s2.put_diag(j, feed(diag, j))
        s2.put_opp(j, feed(opp, j))

    save("g2", "e", "gd")
    gd2.mate(0)
    gd2.opp(0)
    gd2.diag(0)
    loads["w_c"].wait()
    r.cq[...] = (dot(r.m2[...], r.w_c[0], NT) + head_bias[2, 0:1]).astype(bf16)
    save("m2", "cq")
    ge3 = Gather(r.g3, r.ag3, R, S)

    @pl.loop(0, steps)
    def _(j):
        part = window(j * S, S)
        rows = (r.mid[part, :] + s2.total(j) + branch_bias[1:2]).astype(bf16)
        r.enc[part, :] = rows
        r.g3[window(me * R + j * S, S), :] = rows
        ge3.send(j)

    save("enc")
    position = lax.broadcasted_iota(jnp.int32, (T, 1), 0) + me * T
    valid = jnp.where(position < r.dec_len[...], 1.0, 0.0).astype(f32)
    r.r3[...] = r.dec_cot[0].astype(f32) * valid
    r.z3[own, :] = r.r3[...].astype(bf16)
    gz3 = Gather(r.z3, r.agz3, T, S)
    save("r3")

    def cross_block(block):
        part = window(block * R, R)
        rows = r.g3[part, :]
        r.ck[part, :] = dot(rows, r.w_c[1], NT).astype(bf16)
        r.cv[part, :] = (dot(rows, r.w_c[2], NT) + head_bias[2, 1:2]).astype(bf16)

    @pl.loop(0, steps)
    def _(j):
        ge3.mate(j)

    @pl.loop(0, 2)
    def _(i):
        cross_block(me + i * (mate - me))

    @pl.loop(0, steps)
    def _(j):
        ge3.opp(j)

    gz3.send(0)

    @pl.loop(0, steps)
    def _(j):
        ge3.diag(j)

    @pl.loop(0, 2)
    def _(i):
        cross_block(opp + i * (diag - opp))

    save("g3", "ck", "cv")

    loads["w_pc"].wait()
    sc = Scatter(*r.rsc, T, S)

    def cross_rows(block):
        attend_rows(r.cq, r.ck, r.cv, r.ca, r.clc, block * T, T, False)
        return dot(r.ca[window(block * T, T), :], r.w_pc[...])

    sc.put_diag(0, cross_rows(diag))
    sc.put_opp(0, cross_rows(opp))
    sc.put_mate(0, cross_rows(mate))
    sc.put_own(0, cross_rows(me))
    r.cl[...] = jnp.transpose(r.clc[...])[0:8]
    gz3.mate(0)
    gz3.opp(0)
    gz3.diag(0)
    save("ca", "cl", "z3")
    r.second[...] = r.after[...] + sc.total(0) + branch_bias[3:4]
    save("second")

    @pl.loop(0, steps)
    def _(j):
        for each in (ge1, s1, ge2, s2, ge3):
            each.close(j)

    for each in (gd1, sd, gd2, gz3, sc):
        each.close(0)
    for copy in saves:
        copy.wait()


def call_kernel(kernel, name, collective_id, operands, vmem_names, outs, scratch, vmem_limit, remote_ops=True):
    names = list(operands) + ["o_" + key for key in outs]
    flat, groups = [], []
    for key, spec in scratch.items():
        group = spec if isinstance(spec, list) else [spec]
        groups.append((key, len(group), isinstance(spec, list)))
        flat += group

    def body(*refs):
        head, tail = list(refs[:len(names)]), list(refs[len(names):])
        all_names, all_refs = list(names), head
        for key, count, is_list in groups:
            part, tail = tail[:count], tail[count:]
            all_names.append(key)
            all_refs.append(part if is_list else part[0])
        kernel(all_names, *all_refs)

    results = pl.pallas_call(
        body,
        out_shape=list(outs.values()),
        in_specs=[VMEM if key in vmem_names else ANY for key in operands],
        out_specs=[ANY] * len(outs),
        scratch_shapes=flat,
        compiler_params=pltpu.CompilerParams(
            collective_id=collective_id, has_side_effects=True, vmem_limit_bytes=vmem_limit
        ),
        name=name,
    )(*operands.values())
    return dict(zip(outs, results))


def V(*shape):
    return pltpu.VMEM(shape, bf16)


def V32(*shape):
    return pltpu.VMEM(shape, f32)


def B(*shape):
    return jax.ShapeDtypeStruct(shape, bf16)


def B32(*shape):
    return jax.ShapeDtypeStruct(shape, f32)


def dma(*shape):
    return pltpu.SemaphoreType.DMA(shape)


def forward_call(operands, R, T, D, W, F):
    steps = R // T
    N, M = 4 * R, 4 * T
    outs = dict(
        enc=B(R, D), g1=B(N, D), q=B(N, W), k=B(N, W), v=B(N, W), a=B(N, W), l=B32(8, N), mid=B32(R, D),
        g2=B(N, D), e=B(N, F), gd=B(N, F), g3=B(N, D), ck=B(N, W), cv=B(N, W),
        m1=B(M, D), sq=B(M, W), sk=B(M, W), sv=B(M, W), sa=B(M, W), sl=B32(8, M), after=B32(T, D),
        m2=B(M, D), cq=B(M, W), ca=B(M, W), cl=B32(8, M), z3=B(M, D), r3=B32(T, D), second=B32(T, D),
    )
    scratch = {key: pltpu.VMEM(shape.shape, shape.dtype) for key, shape in outs.items()}
    scratch |= dict(
        w_e=V(3, W, D), w_s=V(3, W, D), w_c=V(3, W, D), w_pe=V(W, D), w_ps=V(W, D), w_pc=V(W, D),
        w_f1=V(D, F), w_f2=V(F, D), lc=V32(N, 128), slc=V32(M, 128), clc=V32(M, 128),
        rs1=scatter_shapes(R, D, steps), rs2=scatter_shapes(R, D, steps), rsd=scatter_shapes(T, D, 1),
        rsc=scatter_shapes(T, D, 1), ag1=dma(6, steps), ag2=dma(6, steps), ag3=dma(6, steps),
        agd1=dma(6, 1), agd2=dma(6, 1), agz3=dma(6, 1), load_sem=dma(8), save_sem=dma(len(outs)),
    )
    kept_in_hbm = ("qkv", "proj", "fc1", "fc2")
    return call_kernel(
        functools.partial(forward_kernel, R, T), "forward", 0, operands,
        [key for key in operands if key not in kept_in_hbm], outs, scratch, 60 << 20,
    )


SCHEDULE = (
    0, 1, 2, 3, 4, 6, 5, 10, "b+0", "a+0", 7, 8, 9, "b-0", "a-0", "a+1", 11, "b+1", 12, 13, 14, "b-1", "c+0", "b+2",
    17, 16, "a-1", "a+2", 18, 19, 20, 22, "b-2", 15, "b+3", 25, 26, 28, "s+0", "c-0", 23, "c+1", "a-2", "a+3", 21,
    24, 29, "b-3", "a-3", "a+4", 32, "b+4", 30, 33, "s-0", "s+1", "c-1", 31, "c+2", "e+0", "b-4", "a-4", "a+5",
    "b+5", 27, "c-2", "c+3", 35, 36, 37, "s-1", "s+2", 38, "c-3", "c+4", 39, "e-0", 40, "e+1", 41, "f+0", 42, 43,
    46, "g+0", 44, 47, "h+0", "s-2", "s+3", "e-1", "c-4", "s-3", "c+5", 48, "e+2", 45, 49, "s+4", 34, "g-0", 50,
    "e-2", "e+3", "f-0", "h-0", 51, "f+1", "g+1", "m+0", "s-4", "m-0", "e-3", "h+1", "m+1", "a-5", "c-5", "s+5",
    "e+4", "g-1", "g+2", "g-2", "g+3", "m-1", "f-1", "f+2", "m+2", "h-1", "h+2", "g-3", "f-2", "e-4", "e+5", "g+4",
    "f+3", "s-5", "m-2", "h-2", "m+3", "h+3", "g-4", "b-5", "m-3", "f-3", 52, "f+4", "h-3", "g+5", "h+4", "m+4",
    "f-4", "f+5", "h-4", "h+5", "m-4", "g-5", "h-5", "e-5", "f-5",
)


GAIN, SHIFT, OUT_BIAS, FC1_BIAS, QV_BIAS, SMALL = 0, 5, 10, 16, 18, 24
ORDERS = {key: Z_FIRST if key in "bf" else X_FIRST for key in "abcsefgh"}


def backward_kernel(R, T, clips, names, *refs):
    r = Refs(names, refs)
    S = T
    steps = R // S
    me, mate, opp, diag = places()
    own = window(me * T, T)
    sources = dict(
        second=r.i_second, d_f1=r.fc1.at[1], d_f2=r.fc2.at[1], z3=r.i_z3, r3=r.i_r3, w_pc=r.proj.at[2], ca=r.i_ca,
        cl=r.i_cl, cq=r.i_cq, ck=r.i_ck, cv=r.i_cv, w_c=r.qkv.at[2], g3=r.i_g3, after=r.i_after,
        cot=r.enc_cot.at[0], gd=r.i_gd, w_s=r.qkv.at[1], w_ps=r.proj.at[1],
        sq=r.i_sq, sk=r.i_sk, sv=r.i_sv, sa=r.i_sa, sl=r.i_sl, e=r.i_e, g2=r.i_g2, mid=r.i_mid,
        w_pe=r.proj.at[0], q=r.i_q, a=r.i_a, l=r.i_l, w_e=r.qkv.at[0],
    )
    late = dict(m2=(r.i_m2, r.gu), m1=(r.i_m1, r.dg), g1=(r.i_g1, r.g3), k=(r.i_k, r.ck), v=(r.i_v, r.cv))
    late |= dict(w_f1=(r.fc1.at[0], r.d_f1), w_f2=(r.fc2.at[0], r.d_f2))
    late["frames"] = (r.enc_in.at[0], r.cot)
    loads = {
        name: pltpu.make_async_copy(src, getattr(r, name), r.load_sem.at[i])
        for i, (name, src) in enumerate(sources.items())
    }
    for load in loads.values():
        load.start()
    for i, (name, (src, dst)) in enumerate(late.items()):
        loads[name] = pltpu.make_async_copy(src, dst, r.late_sem.at[i])

    def fetch(*wanted):
        for name in wanted:
            loads[name].start()

    def need(*wanted):
        for name in wanted:
            loads[name].wait()

    saves = []

    def save(src, dst):
        copy = pltpu.make_async_copy(src, dst, r.save_sem.at[len(saves)])
        copy.start()
        saves.append(copy)

    gains = r.gain[...].astype(f32)
    shifts = r.shift[...].astype(f32)
    branch_bias = r.out_bias[...].astype(f32)
    wide_bias = r.fc1_bias[...].astype(f32)
    small = r.sums
    small[...] = jnp.zeros_like(small)
    r.cgqt[...] = jnp.zeros_like(r.cgqt)
    r.sgqt[...] = jnp.zeros_like(r.sgqt)
    r.gqt[...] = jnp.zeros_like(r.gqt)
    position = lax.broadcasted_iota(jnp.int32, (T, 1), 0) + me * T
    valid = jnp.where(position < r.dec_len[...], 1.0, 0.0).astype(f32)

    def clip_bucket(key, buf, land):
        return clip_sum(buf, land, *getattr(r, "red_" + key), ORDERS[key], clips)

    buckets = dict(
        a=clip_bucket("a", r.d1a, r.land_a), b=clip_bucket("b", r.d1b, r.land_b),
        c=clip_bucket("c", r.cross, r.land_c), s=clip_bucket("s", r.self, r.land_s),
        e=clip_bucket("e", r.e1a, r.land_e), f=clip_bucket("f", r.e1b, r.land_b),
        g=clip_bucket("g", r.e2a, r.land_g), h=clip_bucket("h", r.e2b, r.land_h),
        m=Small(r.sums, r.small_land, r.small_sem, clips, 16),
    )
    gm3, gz2 = Gather(r.m3, r.agm3, T, S), Gather(r.dz2, r.agz2, T, S)
    gzs, gz1, gze = Gather(r.zs, r.ags, T, S), Gather(r.z1, r.agz1, R, S), Gather(r.z2, r.agze, R, S)
    sb, sf = Scatter(*r.near_a, r.sem_b, T, S), Scatter(*r.near_b, r.sem_f, T, S)
    sq, sd = Scatter(*r.near_c, r.sem_q, T, S), Scatter(*r.near_a, r.sem_d, T, S)
    sm, s1, s2 = [Scatter(*r.wide, sem, R, S) for sem in (r.sem_m, r.sem_1, r.sem_2)]

    def norm_sums(i, gain_sum, shift_sum):
        add_rows(small, GAIN + i, gain_sum)
        add_rows(small, SHIFT + i, shift_sum)

    pieces = []

    def each_step(work):
        for j in range(steps):
            pieces.append(functools.partial(work, j))

    def begin():
        meet(buckets["m"].partners + far_partners(clips))
        need("second")
        r.m3[own, :] = layer_norm(r.second[...], gains[4:5], shifts[4:5]).astype(bf16)
        gm3.send(0)
        need("d_f1", "d_f2", "z3")

    pieces.append(begin)

    def feed_decoder(block, put_back):
        part = window(block * T, T)
        hidden = dot(r.m3[part, :], r.d_f1[...]) + wide_bias[1:2]
        active, slope = gelu_parts(hidden)
        active = active.astype(bf16)
        r.dg[part, :] = active
        back = (dot(r.z3[part, :], r.d_f2[...], NT) * slope).astype(bf16)
        r.gu[part, :] = back
        put_back(0, dot(back, r.d_f1[...], NT))

    def feed_own():
        feed_decoder(me, sb.put_own)

    def feed_mate():
        gm3.mate(0)
        feed_decoder(mate, sb.put_mate)

    def feed_diag():
        gm3.opp(0)
        gm3.diag(0)
        feed_decoder(diag, sb.put_diag)

    def feed_opp():
        feed_decoder(opp, sb.put_opp)

    def decoder_fc1():
        r.d1a[...] = dot(r.m3[...], r.gu[...], TN).astype(bf16)

    def decoder_fc2():
        r.d1b[...] = dot(r.dg[...], r.z3[...], TN).astype(bf16)

    pieces += [feed_own, feed_mate, feed_diag, feed_opp, decoder_fc1, decoder_fc2]

    def cross_residual():
        fetch("w_f1")
        need("r3")
        rows, gain_sum, shift_sum = norm_back(r.second[...], gains[4:5], sb.total(0))
        norm_sums(4, gain_sum, shift_sum)
        r.r3[...] = r.r3[...] + rows
        r.dz2[own, :] = r.r3[...].astype(bf16)
        gz2.send(0)
        add_rows(small, OUT_BIAS + 4, column_sums(r.z3[own, :].astype(f32)))
        add_rows(small, OUT_BIAS + 3, column_sums(r.dz2[own, :].astype(f32)))
        add_rows(small, FC1_BIAS + 1, matrix_sums(r.gu))
        need("w_pc", "ca", "cl", "cq", "ck", "cv", "w_c")

    def cross_mixed():
        gz2.mate(0)
        gz2.opp(0)
        gz2.diag(0)
        r.cga[...] = dot(r.dz2[...], r.w_pc[...], NT).astype(bf16)
        r.cs[...] = head_sums(r.ca, r.cga)

    def cross_keys(start, size):
        attend_back_rows(r.cq, r.ck, r.cv, r.cga, r.cl, r.cs, r.cgqt, r.gk, r.gv, start, size, False)

    def memory_rows(block, j):
        part = window(block * R + j * S, S)
        return dot(r.gk[part, :], r.w_c[1]) + dot(r.gv[part, :], r.w_c[2])

    def cross_far():
        @pl.loop(0, steps)
        def _(j):
            cross_keys(diag * R + j * S, S)
            sm.put_diag(j, memory_rows(diag, j))
            cross_keys(opp * R + j * S, S)
            sm.put_opp(j, memory_rows(opp, j))

    def forward_rows():
        for block, put in ((diag, sf.put_diag), (opp, sf.put_opp), (mate, sf.put_mate), (me, sf.put_own)):
            put(0, dot(r.dg[window(block * T, T), :], r.d_f2[...]))
        fetch("w_f2")

    def cross_near(block, put):
        cross_keys(block * R, R)

        @pl.loop(0, steps)
        def _(j):
            put(j, memory_rows(block, j))

    def cross_queries():
        r.cgq[...] = (jnp.transpose(r.cgqt[...]) * SCALE).astype(bf16)
        for block, put in ((diag, sq.put_diag), (opp, sq.put_opp), (mate, sq.put_mate), (me, sq.put_own)):
            put(0, dot(r.cgq[window(block * T, T), :], r.w_c[0]))
        fetch("m2")
        need("g3", "cot")

    def cross_weights():
        need("m2")
        r.cross[0:192, :] = dot(r.cgq[...], r.gu[...], TN).astype(bf16)
        r.cross[192:384, :] = dot(r.gk[...], r.g3[...], TN).astype(bf16)
        r.cross[384:576, :] = dot(r.gv[...], r.g3[...], TN).astype(bf16)
        r.cross[576:768, :] = dot(r.ca[...], r.dz2[...], TN).astype(bf16)
        small[QV_BIAS + 4:QV_BIAS + 5, 0:192] = matrix_sums(r.cgq)
        small[QV_BIAS + 5:QV_BIAS + 6, 0:192] = matrix_sums(r.gv)

    def decoder_out():
        r.dec[...] = ((r.second[...] + sf.total(0) + branch_bias[4:5]) * valid).astype(bf16)
        save(r.dec, r.o_dec)

    def self_residual():
        need("after")
        rows, gain_sum, shift_sum = norm_back(r.after[...], gains[3:4], sq.total(0))
        norm_sums(3, gain_sum, shift_sum)
        r.r3[...] = r.r3[...] + rows
        r.zs[own, :] = r.r3[...].astype(bf16)
        gzs.send(0)
        add_rows(small, OUT_BIAS + 2, column_sums(r.zs[own, :].astype(f32)))
        sb.close(0)

    pieces += [
        cross_residual, cross_mixed, cross_far, forward_rows, lambda: cross_near(mate, sm.put_mate),
        lambda: cross_near(me, sm.put_own), cross_queries, cross_weights, decoder_out, self_residual,
    ]

    def encoder_residual(j):
        part = window(j * S, S)
        rows = r.cot[part, :].astype(f32) + sm.total(j)
        sm.close(j)
        r.renc[part, :] = rows
        r.z1[window(me * R + j * S, S), :] = rows.astype(bf16)
        gz1.send(j)

    each_step(encoder_residual)

    def feed(block, j):
        part = window(block * R + j * S, S)
        back = (dot(r.z1[part, :], r.d_f2[...], NT) * r.gd[part, :].astype(f32)).astype(bf16)
        r.gd[part, :] = back
        return dot(back, r.d_f1[...], NT)

    def encoder_feed_own():
        need("w_f1", "w_f2", "gd", "e", "g2", "mid")
        fetch("k", "v", "frames")

        @pl.loop(0, steps)
        def _(j):
            s1.put_own(j, feed(me, j))

    def encoder_feed_mate():
        @pl.loop(0, steps)
        def _(j):
            gz1.mate(j)
            s1.put_mate(j, feed(mate, j))

    def encoder_feed_far(j):
        gz1.opp(j)
        gz1.diag(j)
        s1.put_diag(j, feed(diag, j))
        s1.put_opp(j, feed(opp, j))

    pieces += [encoder_feed_own, encoder_feed_mate]
    each_step(encoder_feed_far)

    def self_mixed():
        gzs.mate(0)
        gzs.opp(0)
        gzs.diag(0)
        fetch("m1")
        need("w_s", "w_ps", "sq", "sk", "sv", "sa", "sl")
        r.sga[...] = dot(r.zs[...], r.w_ps[...], NT).astype(bf16)
        r.cs[...] = head_sums(r.sa, r.sga)

    def self_back():
        @pl.loop(0, 2)
        def _(i):
            attend_back_rows(
                r.sq, r.sk, r.sv, r.sga, r.sl, r.cs, r.sgqt, r.sgk, r.sgv, i * 2 * T, 2 * T, True
            )

        r.sgq[...] = (jnp.transpose(r.sgqt[...]) * SCALE).astype(bf16)

    def self_rows():
        for block, put in ((diag, sd.put_diag), (opp, sd.put_opp), (mate, sd.put_mate), (me, sd.put_own)):
            part = window(block * T, T)
            put(0, dot(r.sgq[part, :], r.w_s[0]) + dot(r.sgk[part, :], r.w_s[1]) + dot(r.sgv[part, :], r.w_s[2]))

    def self_weights():
        need("m1")
        r.self[0:192, :] = dot(r.sgq[...], r.dg[...], TN).astype(bf16)
        r.self[192:384, :] = dot(r.sgk[...], r.dg[...], TN).astype(bf16)
        r.self[384:576, :] = dot(r.sgv[...], r.dg[...], TN).astype(bf16)
        r.self[576:768, :] = dot(r.sa[...], r.zs[...], TN).astype(bf16)

    pieces += [self_mixed, self_back, self_rows, self_weights]

    def middle_residual(j):
        part = window(j * S, S)
        rows, gain_sum, shift_sum = norm_back(r.mid[part, :], gains[1:2], s1.total(j))
        norm_sums(1, gain_sum, shift_sum)
        s1.close(j)
        rows = r.renc[part, :] + rows
        r.mid[part, :] = rows
        r.z2[window(me * R + j * S, S), :] = rows.astype(bf16)
        gze.send(j)

    each_step(middle_residual)

    def encoder_fc1():
        r.e1a[...] = dot(r.g2[...], r.gd[...], TN).astype(bf16)

    def encoder_fc2():
        r.e1b[...] = dot(r.e[...], r.z1[...], TN).astype(bf16)

    def decoder_rows():
        add_rows(small, FC1_BIAS, matrix_sums(r.gd))
        add_rows(small, OUT_BIAS + 1, column_sums(r.z1[window(me * R, R), :].astype(f32)))
        small[QV_BIAS + 2:QV_BIAS + 3, 0:192] = matrix_sums(r.sgq)
        small[QV_BIAS + 3:QV_BIAS + 4, 0:192] = matrix_sums(r.sgv)
        rows, gain_sum, shift_sum = norm_back(r.dec_in[0].astype(f32), gains[2:3], sd.total(0))
        norm_sums(2, gain_sum, shift_sum)
        r.r3[...] = r.r3[...] + rows
        save(r.r3, r.o_decg)

    def mixed_block(block):
        part = window(block * R, R)
        r.ga[part, :] = dot(r.z2[part, :], r.w_pe[...], NT).astype(bf16)

    def mixed_near():
        fetch("g1")
        need("w_pe", "q", "k", "v", "a", "l", "w_e")
        mixed_block(me)

        @pl.loop(0, steps)
        def _(j):
            gze.mate(j)

        mixed_block(mate)

    def mixed_far():
        @pl.loop(0, steps)
        def _(j):
            gze.opp(j)

        @pl.loop(0, steps)
        def _(j):
            gze.diag(j)

        @pl.loop(0, 2)
        def _(i):
            mixed_block(opp + i * (diag - opp))

        r.es[...] = head_sums(r.a, r.ga)

    def attend_piece(i):
        attend_back_rows(r.q, r.ck, r.cv, r.ga, r.l, r.es, r.gqt, r.gk, r.gv, i * 2 * T, 2 * T, False)

    def encoder_queries():
        r.gq[...] = (jnp.transpose(r.gqt[...]) * SCALE).astype(bf16)
        need("g1")

    def attend_rows_back(block, j):
        part = window(block * R + j * S, S)
        return dot(r.gq[part, :], r.w_e[0]) + dot(r.gk[part, :], r.w_e[1]) + dot(r.gv[part, :], r.w_e[2])

    def rows_far():
        @pl.loop(0, steps)
        def _(j):
            s2.put_diag(j, attend_rows_back(diag, j))
            s2.put_opp(j, attend_rows_back(opp, j))

    def rows_near():
        @pl.loop(0, steps)
        def _(j):
            s2.put_mate(j, attend_rows_back(mate, j))
            s2.put_own(j, attend_rows_back(me, j))

    def encoder_weights_a():
        r.e2a[0:192, :] = dot(r.gq[...], r.g3[...], TN).astype(bf16)
        r.e2a[192:384, :] = dot(r.gk[...], r.g3[...], TN).astype(bf16)

    def encoder_weights_b():
        r.e2b[0:192, :] = dot(r.gv[...], r.g3[...], TN).astype(bf16)
        r.e2b[192:384, :] = dot(r.a[...], r.z2[...], TN).astype(bf16)

    def encoder_sums():
        small[QV_BIAS:QV_BIAS + 1, 0:192] = matrix_sums(r.gq)
        small[QV_BIAS + 1:QV_BIAS + 2, 0:192] = matrix_sums(r.gv)
        add_rows(small, OUT_BIAS, column_sums(r.z2[window(me * R, R), :].astype(f32)))

    def frames_residual(j):
        part = window(j * S, S)
        if j == 0:
            need("frames")
        rows, gain_sum, shift_sum = norm_back(r.cot[part, :].astype(f32), gains[0:1], s2.total(j))
        norm_sums(0, gain_sum, shift_sum)
        r.mid[part, :] = r.mid[part, :] + rows

    pieces += [encoder_fc1, encoder_fc2, decoder_rows, mixed_near, mixed_far]
    for i in range(2 * R // T):
        pieces.append(functools.partial(attend_piece, i))
    pieces += [encoder_queries, rows_far, rows_near, encoder_weights_a, encoder_weights_b, encoder_sums]
    each_step(frames_residual)
    pieces.append(lambda: save(r.mid, r.o_encg))

    last = {
        ("a", 5): [(r.d1a, r.o_fc1.at[1])],
        ("b", 5): [(r.d1b, r.o_fc2.at[1])],
        ("c", 5): [(r.cross.at[0:576], r.o_qkv.at[2]), (r.cross.at[576:768], r.o_proj.at[2])],
        ("s", 5): [(r.self.at[0:576], r.o_qkv.at[1]), (r.self.at[576:768], r.o_proj.at[1])],
        ("e", 5): [(r.e1a, r.o_fc1.at[0])],
        ("f", 5): [(r.e1b, r.o_fc2.at[0])],
        ("g", 5): [(r.e2a, r.o_qkv.at[0, 0:384])],
        ("h", 5): [(r.e2b.at[0:192], r.o_qkv.at[0, 384:576]), (r.e2b.at[192:384], r.o_proj.at[0])],
        ("m", 4): [(r.sums, r.o_small)],
    }
    for item in SCHEDULE:
        if isinstance(item, int):
            pieces[item]()
            continue
        name, sign, i = item[0], item[1], int(item[2])
        if sign == "+":
            buckets[name].start(i)
        else:
            buckets[name].finish(i)
            for pair in last.get((name, i), ()):
                save(*pair)

    @pl.loop(0, steps)
    def _(j):
        for each in (gz1, gze, s2):
            each.close(j)

    for each in (gm3, gz2, gzs, sf, sq, sd):
        each.close(0)
    for copy in saves:
        copy.wait()


def backward_call(operands, clips, R, T, D, W, F):
    steps = R // T
    N, M = 4 * R, 4 * T
    partners = 2 + bit_count(clips)
    outs = dict(
        dec=B(T, D), encg=B32(R, D), decg=B32(T, D), qkv=B(3, 3 * W, D), proj=B(3, W, D), fc1=B(2, D, F),
        fc2=B(2, F, D), small=B32(SMALL, D),
    )
    land = lambda key, rows: sum_land(rows, ORDERS[key], clips)
    near = lambda: scatter_shapes(T, D, 1)[:-1]
    scratch = dict(
        second=V32(T, D), d_f1=V(D, F), d_f2=V(F, D), z3=V(M, D), r3=V32(T, D), w_pc=V(W, D), ca=V(M, W), cl=V32(8, M),
        cq=V(M, W), ck=V(N, W), cv=V(N, W), w_c=V(3, W, D), g3=V(N, D), after=V32(T, D), cot=V(R, D),
        gd=V(N, F), w_s=V(3, W, D), w_ps=V(W, D), sq=V(M, W), sk=V(M, W),
        sv=V(M, W), sa=V(M, W), sl=V32(8, M), e=V(N, F), g2=V(N, D), mid=V32(R, D), w_pe=V(W, D), q=V(N, W),
        a=V(N, W), l=V32(8, N), w_e=V(3, W, D),
        m3=V(M, D), dg=V(M, F), gu=V(M, F), dz2=V(M, D), cga=V(M, W), cs=V32(8, M), cgqt=V32(W, M),
        cgq=V(M, W), gk=V(N, W), gv=V(N, W), dec=V(T, D), zs=V(M, D), renc=V32(R, D), z1=V(N, D),
        sga=V(M, W), sgqt=V32(W, M), sgq=V(M, W), sgk=V(M, W), sgv=V(M, W), z2=V(N, D), ga=V(N, W),
        es=V32(8, N), gqt=V32(W, N), gq=V(N, W), sums=V32(SMALL, D),
        d1a=V(D, F), d1b=V(F, D), cross=V(4 * W, D), self=V(4 * W, D), e1a=V(D, F), e1b=V(F, D), e2a=V(2 * W, D),
        e2b=V(2 * W, D), land_a=land("a", D), land_b=land("b", F), land_c=land("c", 4 * W), land_s=land("s", 4 * W),
        land_e=land("e", D), land_g=land("g", 2 * W), land_h=land("h", 2 * W), small_land=V32(partners, SMALL, D), small_sem=dma(2, partners),
        near_a=near(), near_b=near(), near_c=near(), wide=scatter_shapes(R, D, steps)[:-1],
        sem_b=dma(6, 1), sem_f=dma(6, 1), sem_q=dma(6, 1), sem_d=dma(6, 1),
        sem_m=dma(6, steps), sem_1=dma(6, steps), sem_2=dma(6, steps),
        agm3=dma(6, 1), agz2=dma(6, 1), ags=dma(6, 1), agz1=dma(6, steps), agze=dma(6, steps),
        load_sem=dma(31), late_sem=dma(8), save_sem=dma(16),
    )
    scratch |= {"red_" + key: sum_signals(order, clips) for key, order in ORDERS.items()}
    in_vmem = ("gain", "shift", "out_bias", "fc1_bias", "dec_len", "dec_in")
    return call_kernel(
        functools.partial(backward_kernel, R, T, clips), "backward", 1, operands, in_vmem, outs, scratch, 63 << 20
    )


def finish_kernel(
    i_enc, i_dec, i_encg, i_decg, small, i_qkv, i_proj, i_fc1, i_fc2,
    o_enc, o_dec, o_encg, o_decg, o_gain, o_shift, o_qkv, o_qvb, o_proj, o_bias, o_fc1, o_fc1b, o_fc2,
    narrow, wide, r_enc, r_dec, r_encg, r_decg, row_sem, in_sem, out_sem,
):
    chunk = narrow.shape[1]
    parts = []
    for src, dst in ((i_qkv, o_qkv), (i_proj, o_proj), (i_fc1, o_fc1), (i_fc2, o_fc2)):
        for i in range(src.shape[0]):
            for start in range(0, src.shape[1], chunk):
                parts.append((src.at[i, pl.ds(start, chunk)], dst.at[i, pl.ds(start, chunk)]))
    loads = [pltpu.make_async_copy(src, narrow.at[n], in_sem.at[n]) for n, (src, _) in enumerate(parts)]
    stores = [pltpu.make_async_copy(wide.at[n], dst, out_sem.at[n]) for n, (_, dst) in enumerate(parts)]
    pairs = ((i_enc, r_enc, o_enc), (i_dec, r_dec, o_dec), (i_encg, r_encg, o_encg), (i_decg, r_decg, o_decg))
    moves = [pltpu.make_async_copy(src, held, row_sem.at[0, n]) for n, (src, held, _) in enumerate(pairs)]
    passes = [pltpu.make_async_copy(held, dst.at[0], row_sem.at[1, n]) for n, (_, held, dst) in enumerate(pairs)]
    for copy in loads + moves:
        copy.start()
    o_gain[...] = small[GAIN:GAIN + 5, :]
    o_shift[...] = small[SHIFT:SHIFT + 5, :]
    o_bias[...] = small[OUT_BIAS:OUT_BIAS + 5, :]
    o_fc1b[...] = small[FC1_BIAS:FC1_BIAS + 2, :]
    for i in range(3):
        o_qvb[i] = small[QV_BIAS + 2 * i:QV_BIAS + 2 * i + 2, 0:o_qvb.shape[2]]
    for n, (load, store) in enumerate(zip(loads, stores)):
        load.wait()
        wide[n] = narrow[n].astype(f32)
        store.start()
    for move, copy in zip(moves, passes):
        move.wait()
        copy.start()
    for copy in passes + stores:
        copy.wait()


def finish_call(enc_out, last, W):
    R, D = last["encg"].shape
    T = last["decg"].shape[0]
    F = last["fc1"].shape[2]
    chunk = W
    count = sum(last[name].shape[0] * last[name].shape[1] // chunk for name in ("qkv", "proj", "fc1", "fc2"))
    B32 = lambda *shape: jax.ShapeDtypeStruct(shape, f32)
    shapes = [
        jax.ShapeDtypeStruct((1, R, D), bf16), jax.ShapeDtypeStruct((1, T, D), bf16), B32(1, R, D), B32(1, T, D),
        B32(5, D), B32(5, D), B32(3, 3 * W, D), B32(3, 2, W), B32(3, W, D), B32(5, D), B32(2, D, F), B32(2, F), B32(2, F, D),
    ]
    whole = [ANY, ANY, ANY, ANY, VMEM, VMEM, ANY, VMEM, ANY, VMEM, ANY, VMEM, ANY]
    return pl.pallas_call(
        finish_kernel,
        out_shape=shapes,
        in_specs=[ANY] * 4 + [VMEM] + [ANY] * 4,
        out_specs=whole,
        scratch_shapes=[
            pltpu.VMEM((count, chunk, D), bf16), pltpu.VMEM((count, chunk, D), f32),
            pltpu.VMEM((R, D), bf16), pltpu.VMEM((T, D), bf16), pltpu.VMEM((R, D), f32), pltpu.VMEM((T, D), f32),
            pltpu.SemaphoreType.DMA((2, 4)), pltpu.SemaphoreType.DMA((count,)), pltpu.SemaphoreType.DMA((count,)),
        ],
        compiler_params=pltpu.CompilerParams(vmem_limit_bytes=60 << 20),
        name="finish",
    )(
        enc_out, last["dec"], last["encg"], last["decg"], last["small"],
        last["qkv"], last["proj"], last["fc1"], last["fc2"],
    )


def on_device(
    clips,
    enc_in, dec_in, dec_len, norm_gain, norm_shift, qkv, qv_bias, proj, out_bias, fc1, fc1_bias, fc2, enc_cot, dec_cot,
):
    turned = jnp.swapaxes(qkv, 2, 3)
    W, D = turned.shape[2:]
    R, T, F = enc_in.shape[1], dec_in.shape[1], fc1.shape[2]
    shared = dict(
        enc_in=enc_in, dec_in=dec_in, gain=norm_gain, shift=norm_shift, out_bias=out_bias, fc1_bias=fc1_bias,
        dec_len=dec_len.reshape(1, 1), qkv=turned, proj=proj, fc1=fc1, fc2=fc2,
    )
    kept = forward_call(shared | dict(qv_bias=qv_bias, dec_cot=dec_cot), R, T, D, W, F)
    carried = {"i_" + key: value for key, value in kept.items() if key != "enc"}
    last = backward_call(shared | dict(enc_cot=enc_cot) | carried, clips, R, T, D, W, F)
    outs = list(finish_call(kept["enc"], last, W))
    outs[6] = jnp.swapaxes(outs[6].reshape(3, 3, W, D), 2, 3)
    return tuple(outs)


def solution(mesh):
    rows = P("dp", "mp", None)
    columns = P(None, None, None, "mp")
    return jax.shard_map(
        functools.partial(on_device, mesh.shape["dp"]),
        mesh=mesh,
        in_specs=(
            rows, rows, P("dp"), P(), P(), columns, P(None, None, "mp"), P(None, "mp", None), P(),
            P(None, None, "mp"), P(None, "mp"), P(None, "mp", None), rows, rows,
        ),
        out_specs=(
            rows, rows, rows, rows, P(), P(), columns, P(None, None, "mp"), P(None, "mp", None), P(),
            P(None, None, "mp"), P(None, "mp"), P(None, "mp", None),
        ),
        check_vma=False,
    )
```
